128 devices in a mesh: pool: 16 (over z, y), grp: 8 (over x, core).
Axes of the slice: x: 4, y: 4, z: 4, core: 2. Of those that a mesh axis runs over, the one named last changes fastest.
Arguments:
- embeddings: bfloat16 [131072, 1024], P(('pool', 'grp')), may hold values from -6 to 6
- members: int32 [256, 512], replicated, may hold values from 0 to 131071, as said below
- valid: int32 [256], replicated, may hold values from 128 to 512, as said below
- block_cluster: int32 [256], replicated, may hold values from 0 to 255, as said below
Outputs:
- duplicate_score: float32 [131072], P(('pool', 'grp'))
The draws below stay inside these ranges and needn't reach their ends.
Inputs may be any that keep to these rules, and one draw needn't show every extreme that they name: `members`: every pool row is held by at most one live slot. Device d (pool-major index) owns blocks d * 2 to d * 2 + 1; of the rows held by one device's live slots, at most 8 lie in any one row shard (rows s * 1024 to s * 1024 + 1023, the rows of device s), the counts from two shards differ by at most one, and in every draw the live rows of some device come exactly 8 from every shard. Dead slots hold arbitrary row numbers. `valid`: in every draw all 2 blocks of some device are full. `block_cluster`: Nondecreasing; equal values form runs of blocks inside one cluster group of 16 blocks, each value is the index of its run's first block, the first block of each group starts a new cluster, and the last block forms a cluster of its own.
All inputs are finite; a program needn't handle non-finite values.
Results may differ from the reference program's by a relative error of at most 0.0014.
Values may be sent and summed in bfloat16 or wider, within the bound.
No kernel may reach another device: no remote copies, remote signals or barrier semaphores. Data moves between devices by JAX's collectives and lax.ppermute only.
A program may use at most 64 MiB of HBM per device.

```python
import jax
import jax.numpy as jnp
from jax import lax

E = 1024
BLK = 512
BPD = 2
SLOTS_DEV = 1024
ROWS_DEV = 1024
GBLK = 16
BLOCKS = 256
POOL = 131072


def block_counts(key):
    first_key, second_key = jax.random.split(jax.random.fold_in(key, 11))
    counts = jax.random.randint(first_key, (BLOCKS,), BLK // 4, BLK + 1)
    device_count = BLOCKS // BPD
    full_device = jax.random.randint(second_key, (), 0, device_count)
    owner = jnp.arange(BLOCKS, dtype=jnp.int32) // BPD
    return jnp.where(owner == full_device, BLK, counts).astype(jnp.int32)


def draw_valid(key, part):
    return block_counts(key)


def draw_members(key, part):
    counts_all = block_counts(key)
    key = jax.random.fold_in(key, 5)
    device_count = BLOCKS // BPD
    perm_key, rows_key, order_key, filler_key = jax.random.split(key, 4)
    live_count = counts_all.reshape(device_count, BPD).sum(axis=1)
    source_order = jax.vmap(lambda sub: jax.random.permutation(sub, device_count))(jax.random.split(perm_key, device_count)).astype(jnp.int32)
    position = jnp.arange(SLOTS_DEV, dtype=jnp.int32)
    item_source = source_order[:, position % device_count]
    item_rank = position // device_count
    item_live = position[None, :] < live_count[:, None]
    inverse = jnp.argsort(source_order, axis=1, stable=True).astype(jnp.int32)
    pair_counts = live_count[:, None] // device_count + (inverse < (live_count % device_count)[:, None]).astype(jnp.int32)
    offsets = jnp.cumsum(pair_counts, axis=0) - pair_counts
    local_row = jnp.take_along_axis(offsets, item_source, axis=1) + item_rank[None, :]
    local_row = jnp.clip(local_row, 0, ROWS_DEV - 1)
    row_order = jax.vmap(lambda sub: jax.random.permutation(sub, ROWS_DEV))(jax.random.split(rows_key, device_count)).astype(jnp.int32)
    row_ids = item_source * ROWS_DEV + row_order[item_source, local_row]
    shuffle = jax.vmap(lambda sub: jax.random.permutation(sub, SLOTS_DEV))(jax.random.split(order_key, device_count)).astype(jnp.int32)
    score = jnp.where(item_live, shuffle, SLOTS_DEV + position[None, :])
    order = jnp.argsort(score, axis=1, stable=True).astype(jnp.int32)
    ordered = jnp.take_along_axis(row_ids, order, axis=1)
    counts_dev = counts_all.reshape(device_count, BPD)
    starts = jnp.cumsum(counts_dev, axis=1) - counts_dev
    column = jnp.arange(BLK, dtype=jnp.int32)
    live_index = jnp.clip(starts[:, :, None] + column[None, None, :], 0, SLOTS_DEV - 1).reshape(device_count, SLOTS_DEV)
    placed = jnp.take_along_axis(ordered, live_index, axis=1).reshape(device_count, BPD, BLK)
    slot_live = column[None, None, :] < counts_dev[:, :, None]
    filler = jax.random.randint(filler_key, (device_count, BPD, BLK), 0, POOL)
    return jnp.where(slot_live, placed, filler).reshape(BLOCKS, BLK).astype(jnp.int32)


def draw_block_cluster(key, part):
    key = jax.random.fold_in(key, 7)
    rate_key, start_key = jax.random.split(key)
    group_count = BLOCKS // GBLK
    rate = jax.random.randint(rate_key, (group_count, 1), 2, GBLK + 1)
    throws = jax.random.randint(start_key, (group_count, GBLK), 0, 1048576)
    starts = (throws % rate == 0) | (jnp.arange(GBLK, dtype=jnp.int32)[None, :] == 0)
    flat = starts.reshape(-1)
    index = jnp.arange(BLOCKS, dtype=jnp.int32)
    flat = flat | (index == BLOCKS - 1)
    marks = jnp.where(flat, index, 0).astype(jnp.int32)
    return lax.cummax(marks, axis=0).astype(jnp.int32)


def shard_levels(rng, shape, shards, least, largest):
    loudness, own = 1.0, jax.random.fold_in(rng, 6)
    for dim, parts in shards:
        steps = jnp.exp(jax.random.uniform(jax.random.fold_in(own, dim), (parts,), jnp.float32, least / len(shards), largest / len(shards)))
        loudness = loudness * jnp.repeat(steps, shape[dim] // parts).reshape([-1 if axis == dim else 1 for axis in range(len(shape))])
    return loudness


def noise(rng, shape, deviation, reach, pieces=(), kind=jnp.bfloat16):
    values = deviation * jax.random.normal(rng, shape, jnp.float32)
    if pieces:
        values = values * shard_levels(rng, shape, pieces, -0.22, 0.18)
    return jnp.clip(values, -reach, reach).astype(kind)


def setup_inputs(seed: int = 0) -> dict:
    streams_of = jax.random.split(jax.random.key(seed), 5)
    return {
        "embeddings": noise(streams_of[0], (POOL, E), 1.0, 6.0, ((0, 128),)),
        "members": draw_members(jax.random.fold_in(streams_of[4], 71), 0),
        "valid": draw_valid(jax.random.fold_in(streams_of[4], 71), 0),
        "block_cluster": draw_block_cluster(jax.random.fold_in(streams_of[4], 71), 0),
    }


EPS = 1e-06

def reference(embeddings, members, valid, block_cluster):
    wide = embeddings.astype(jnp.float32)
    unit = (wide * lax.rsqrt(lax.optimization_barrier(jnp.sum(wide * wide, axis=1, keepdims=True)) + EPS)).astype(jnp.bfloat16)
    blocks = jnp.take(unit, members.reshape(-1), axis=0).reshape(BLOCKS, BLK, E)
    column = jnp.arange(BLK, dtype=jnp.int32)

    def per_query(query):
        query_rows = blocks[query]
        group_start = query // GBLK * GBLK

        def inner(offset, running):
            key_block = group_start + offset

            def tile(current):
                sims = jnp.dot(query_rows, blocks[key_block].T, preferred_element_type=jnp.float32)
                keep = (column[None, :] < valid[key_block]) & ((key_block < query) | (column[None, :] < column[:, None]))
                return jnp.maximum(current, lax.optimization_barrier(jnp.max(jnp.where(keep, sims, 0.0), axis=1)))
            usable = (block_cluster[key_block] == block_cluster[query]) & (key_block <= query)
            return lax.cond(usable, tile, lambda current: current, running)
        return lax.fori_loop(0, GBLK, inner, jnp.zeros((BLK,), jnp.float32))
    best = lax.map(per_query, jnp.arange(BLOCKS, dtype=jnp.int32))
    live = column[None, :] < valid[:, None]
    target = jnp.where(live, members, POOL).reshape(-1).astype(jnp.int32)
    scores = jnp.zeros((POOL + 1,), jnp.float32).at[target].set(best.reshape(-1))
    return scores[:POOL]
```

```python
import jax
import jax.numpy as jnp
from jax import lax
from jax.experimental import pallas as pl
from jax.experimental.pallas import tpu as pltpu
from jax.sharding import PartitionSpec as P

EPS = 1e-06
F32 = jnp.float32
BF16 = jnp.bfloat16
I32 = jnp.int32
CHUNKS = 2
NT = (((1,), (1,)), ((), ()))
PARAMS = pltpu.CompilerParams(vmem_limit_bytes=50 * 1024 * 1024)


def iota(shape, dim):
    return lax.broadcasted_iota(I32, shape, dim)


def normal_rows(rows):
    return (rows * lax.rsqrt(jnp.sum(rows * rows, axis=1, keepdims=True) + EPS)).astype(BF16)


def picked_rows(table, emb_ref, first, count, pools):
    width = emb_ref.shape[0]
    wanted = []
    for k in range(first, first + count):
        hit = table[:, k : k + 1] == iota((table.shape[0], width), 1)
        wanted.append(jnp.where(hit, 1.0, 0.0).reshape(pools, -1, width))
    choice = jnp.concatenate(wanted, axis=1).reshape(-1, width).astype(BF16)
    return normal_rows(jnp.dot(choice, emb_ref[...], preferred_element_type=F32))


def table_kernel(
    pools, group, places, members_ref, valid_ref, emb_ref, table_ref, out_ref, found_ref
):
    rows_dev = emb_ref.shape[0]
    device = lax.axis_index("pool") * group + lax.axis_index("grp")
    blocks, block_len = members_ref.shape
    devices = blocks // 2
    before = jnp.where(
        iota((block_len, block_len), 0) < iota((block_len, block_len), 1), 1.0, 0.0
    ).astype(BF16)
    at = iota((blocks, blocks), 1) == iota((blocks, blocks), 0)
    live = jnp.sum(jnp.where(at, valid_ref[...], 0), axis=1, keepdims=True)
    local = members_ref[...] - device * rows_dev
    mine = (local >= 0) & (local < rows_dev) & (iota((blocks, block_len), 1) < live)
    ones = jnp.where(mine, 1.0, 0.0)
    counts = jnp.broadcast_to(jnp.sum(ones, axis=1, keepdims=True), (blocks, 128))
    counts = jnp.where(iota((blocks, 128), 0) % 2 == 1, pltpu.roll(counts, 1, 0), 0.0)
    rank = jnp.dot(ones.astype(BF16), before, preferred_element_type=F32) + counts[:, :1]
    rank = jnp.where(mine, rank, -1.0)
    value = (local + 1).astype(F32)
    lane = iota((blocks, 128), 1)
    found = jnp.zeros((blocks, 128), F32)
    for k in range(places):
        entry = jnp.sum(jnp.where(rank == k, value, 0.0), axis=1, keepdims=True)
        found = jnp.where(lane == k, entry, found)
    found_ref[...] = found
    pair = found_ref[pl.ds(0, devices, stride=2), :] + found_ref[pl.ds(1, devices, stride=2), :]
    table = pair.astype(I32) - 1
    table_ref[...] = table
    out_ref[...] = picked_rows(table, emb_ref, 0, places // CHUNKS, pools)


def rows_kernel(pools, first, count, table_ref, emb_ref, out_ref):
    out_ref[...] = picked_rows(table_ref[...], emb_ref, first, count, pools)


def meta_kernel(group, places, members_ref, valid_ref, cluster_ref, out_ref):
    blocks, block_len = members_ref.shape
    sources = blocks // 2
    slots = 2 * block_len
    pool = lax.axis_index("pool")
    width = group * places
    before = jnp.where(iota((slots, slots), 0) < iota((slots, slots), 1), 1.0, 0.0).astype(BF16)
    slot = iota((1, slots), 1)
    kind = iota((2 * width, slots), 0)
    kind_place = kind % width // group
    kind_owner = kind % group
    kind_value = jnp.where(kind < width, slot // 32, slot % 32 + 1)
    found = jnp.zeros((sources, 2 * width), F32)
    block_lane = iota((1, blocks), 1)
    lane = iota((1, width), 1)
    first_cluster = jnp.zeros((1, width), I32)
    second_cluster = jnp.zeros((1, width), I32)
    for owner in range(group):
        block = (pool * group + owner) * 2
        halves, lives = [], []
        for half in range(2):
            halves.append(members_ref[pl.ds(block + half, 1), :])
            at = block_lane == block + half
            lives.append(jnp.sum(jnp.where(at, valid_ref[...], 0), axis=1, keepdims=True))
            cluster = jnp.sum(jnp.where(at, cluster_ref[...], 0), axis=1, keepdims=True)
            if half == 0:
                first_cluster = jnp.where(lane % group == owner, cluster, first_cluster)
            else:
                second_cluster = jnp.where(lane % group == owner, cluster, second_cluster)
        rows = jnp.concatenate(halves, axis=1)
        end = jnp.where(slot < block_len, lives[0], block_len + lives[1])
        origin = jnp.where(slot < end, rows // slots, -1)
        match = iota((sources, slots), 0) == origin
        ones = jnp.where(match, 1.0, 0.0).astype(BF16)
        ranks = jnp.dot(ones, before, preferred_element_type=F32)
        rank = jnp.sum(jnp.where(match, ranks, 0.0), axis=0, keepdims=True).astype(I32)
        weight = jnp.where((kind_owner == owner) & (kind_place == rank), kind_value, 0)
        found = found + lax.dot_general(
            ones, weight.astype(F32).astype(BF16), NT, preferred_element_type=F32
        )
    found = found.astype(I32)
    place = found[:, :width] * 32 + found[:, width:] - 1
    filled = found[:, width:] > 0
    position = jnp.where(filled, place + lane % group * slots, -1)
    cluster = jnp.where(place < block_len, first_cluster, second_cluster)
    out_ref[:, :width] = position
    out_ref[:, width:] = jnp.where(filled, cluster, -1)


def columns(row):
    return jnp.transpose(jnp.broadcast_to(row, (128, row.shape[1])))


def block_pair(left, right, sims_ref, left_meta, right_meta, row_ref, row_at, col_ref, col_at):
    left_pos, left_cluster = left_meta
    right_pos, right_cluster = right_meta
    sims_ref[...] = lax.dot_general(left, right, NT, preferred_element_type=F32)
    count, across = sims_ref.shape
    step = 128
    col = [jnp.zeros((8, 128), F32) for _ in range(across // 128)]
    for top in range(0, count, step):
        pos = left_pos[row_at + top : row_at + top + step, :]
        cluster = left_cluster[row_at + top : row_at + top + step, :]
        best = row_ref[row_at + top : row_at + top + step, :]
        for part in range(across // 128):
            lanes = slice(part * 128, part * 128 + 128)
            sims = sims_ref[top : top + step, lanes]
            sims = jnp.where(cluster == right_cluster[:, lanes], sims, 0.0)
            earlier = right_pos[:, lanes] < pos
            best = jnp.maximum(best, jnp.where(earlier, sims, 0.0))
            if col_ref is not None:
                later = jnp.where(earlier, 0.0, sims)
                col[part] = jnp.maximum(col[part], jnp.max(later.reshape(-1, 8, 128), axis=0))
        row_ref[row_at + top : row_at + top + step, :] = best
    if col_ref is not None:
        for part in range(across // 128):
            lanes = pl.ds(col_at + part * 128, 128)
            col_ref[:, lanes] = jnp.maximum(col_ref[:, lanes], col[part])


def place_meta(meta_ref, index, dead, pos_ref, cluster_ref):
    pos_ref[...] = columns(meta_ref[0, pl.ds(index, 1), :])
    cluster = meta_ref[1, pl.ds(index, 1), :]
    cluster_ref[...] = columns(jnp.where(cluster < 0, dead, cluster))


def row_result(row_ref):
    return jnp.max(jnp.transpose(row_ref[...]), axis=0, keepdims=True)


def col_result(col_ref):
    return jnp.max(col_ref[...], axis=0, keepdims=True)


def near_kernel(
    own0, own1, sib0, sib1, meta_ref, out_ref, sims, own_pos, own_cluster, own_row, own_col, sib_col
):
    index = lax.axis_index("grp")
    core = index % 2
    half = own0.shape[0]
    own, sib = (own0, own1), (sib0, sib1)
    place_meta(meta_ref, index, -2, own_pos, own_cluster)
    for ref in (own_row, own_col, sib_col):
        ref[...] = jnp.zeros(ref.shape, F32)
    left = (own_pos, own_cluster)
    for a, b in ((0, 0), (0, 1), (1, 1)):
        lanes = pl.ds(b * half, half)
        right = (meta_ref[0, pl.ds(index, 1), lanes], meta_ref[1, pl.ds(index, 1), lanes])
        block_pair(
            own[a][...], own[b][...], sims.at[(a + b) % 2], left, right, own_row, a * half,
            None if a == b else own_col, b * half,
        )
    other = index + 1 - 2 * core

    def with_sibling(flip):
        for a in range(2):
            b = a ^ flip
            lanes = pl.ds(b * half, half)
            right = (meta_ref[0, pl.ds(other, 1), lanes], meta_ref[1, pl.ds(other, 1), lanes])
            block_pair(
                own[a][...], sib[b][...], sims.at[a], left, right, own_row, a * half, sib_col, b * half
            )

    pl.when(core == 0)(lambda: with_sibling(0))
    pl.when(core == 1)(lambda: with_sibling(1))
    out_ref[0:1, :] = jnp.maximum(row_result(own_row), col_result(own_col))
    out_ref[1:2, :] = col_result(sib_col)


def far_kernel(
    pools, group, own0, own1, sib0, sib1, low0, low1, lows0, lows1, high0, high1, meta_ref, near_ref,
    out_ref, held, sems, sims, pos, clusters, rows, high_col, every,
):
    index = lax.axis_index("grp")
    chip = index // 2
    core = index % 2
    sources = [high0, own0, own1, sib0, sib1, high1, low0, low1, lows0, lows1]
    copies = []
    for n, source in enumerate(sources):
        copy = pltpu.make_async_copy(source, held.at[n], sems.at[n])
        copy.start()
        copies.append(copy)
    half = own0.shape[0]
    below = (index + group - 2) % group
    above = (index + 2) % group
    other = index + 1 - 2 * core
    below_other = below + 1 - 2 * core
    for n, cls in enumerate((index, other, below, below_other)):
        place_meta(meta_ref, cls, -2, pos.at[n], clusters.at[n])
    rows[...] = jnp.zeros(rows.shape, F32)
    high_col[...] = jnp.zeros(high_col.shape, F32)

    def pair(n, a, b, flight):
        lanes = pl.ds(b * half, half)
        right = (meta_ref[0, pl.ds(above, 1), lanes], meta_ref[1, pl.ds(above, 1), lanes])
        left = (pos.at[n], clusters.at[n])
        place = (1, 3, 6, 8)[n] + a
        block_pair(
            held[place], held[0 if b == 0 else 5], sims.at[flight % 2], left, right, rows.at[n],
            a * half, high_col, b * half,
        )

    copies[0].wait()
    for n in range(4):
        copies[1 + n].wait()
        pair(n // 2, n % 2, 0, n)
    copies[5].wait()
    for n in range(4):
        pair(n // 2, n % 2, 1, n)
    for n in range(6, 10):
        copies[n].wait()

    def distant(flip):
        for n in range(4):
            pair(2 + n // 2, n % 2, n % 2 ^ flip, n)

    first = (chip == 1) | (chip == 2)
    pl.when(first)(lambda: distant(0))
    pl.when(jnp.logical_not(first))(lambda: distant(1))
    every[...] = jnp.zeros(every.shape, F32)
    every[pl.ds(index, 1), :] = jnp.maximum(near_ref[0:1, :], row_result(rows.at[0]))
    every[pl.ds(other, 1), :] = jnp.maximum(near_ref[1:2, :], row_result(rows.at[1]))
    every[pl.ds(below, 1), :] = row_result(rows.at[2])
    every[pl.ds(below_other, 1), :] = row_result(rows.at[3])
    every[pl.ds(above, 1), :] = col_result(high_col)
    width = half // pools
    for p in range(pools):
        for h in range(CHUNKS):
            out_ref[p * group : (p + 1) * group, h * width : (h + 1) * width] = every[
                :, h * half + p * width : h * half + (p + 1) * width
            ]


def score_kernel(pools, group, places, table_ref, returned_ref, out_ref):
    rows_dev = out_ref.shape[1]
    arrived = jnp.transpose(
        jnp.concatenate([returned_ref[...], jnp.zeros_like(returned_ref)], axis=1)
    )
    table = table_ref[...]
    row = iota((8, rows_dev), 1)
    total = jnp.zeros((8, rows_dev), F32)
    for p in range(pools):
        for k in range(places):
            value = jnp.max(
                arrived[k * group : (k + 1) * group, p * group : (p + 1) * group],
                axis=1,
                keepdims=True,
            )
            entry = table[p * group : (p + 1) * group, k : k + 1]
            total = jnp.where(entry == row, value, total)
    out_ref[...] = jnp.sum(total, axis=0, keepdims=True)


def body(embeddings, members, valid, block_cluster):
    rows_dev, feature = embeddings.shape
    pools = lax.axis_size("pool")
    group = lax.axis_size("grp")
    devices = pools * group
    places = rows_dev // devices
    half = rows_dev // CHUNKS
    sds = jax.ShapeDtypeStruct
    valid_row = valid.reshape(1, -1)
    cluster_row = block_cluster.reshape(1, -1)

    table, out0 = pl.pallas_call(
        lambda *refs: table_kernel(pools, group, places, *refs),
        out_shape=(sds((devices, 128), I32), sds((half, feature), BF16)),
        scratch_shapes=[pltpu.VMEM((2 * devices, 128), F32)],
        compiler_params=PARAMS,
        name="table",
    )(members, valid_row, embeddings)
    out1 = pl.pallas_call(
        lambda *refs: rows_kernel(pools, places // CHUNKS, places // CHUNKS, *refs),
        out_shape=sds((half, feature), BF16),
        compiler_params=PARAMS,
        name="rows",
    )(table, embeddings)
    meta = pl.pallas_call(
        lambda *refs: meta_kernel(group, places, *refs),
        out_shape=sds((devices, 2 * group * places), I32),
        compiler_params=PARAMS,
        name="meta",
    )(members, valid_row, cluster_row)
    meta = (
        meta.reshape(pools, group, 2, CHUNKS, half // pools)
        .transpose(2, 1, 3, 0, 4)
        .reshape(2, group, rows_dev)
    )

    def shift(rows, by):
        return lax.ppermute(rows, "grp", [(g, (g + by) % group) for g in range(group)])

    def swap(rows):
        return lax.ppermute(rows, "grp", [(g, g ^ 1) for g in range(group)])

    own, sib, low, lows, high = [], [], [], [], []
    for out in (out0, out1):
        rows = lax.all_to_all(out, "pool", split_axis=0, concat_axis=0, tiled=True)
        own.append(rows)
        low.append(shift(rows, 2))
        high.append(shift(rows, -2))
        sib.append(swap(rows))
        lows.append(swap(low[-1]))

    near = pl.pallas_call(
        near_kernel,
        out_shape=sds((2, rows_dev), F32),
        scratch_shapes=[
            pltpu.VMEM((2, half, half), F32),
            pltpu.VMEM((rows_dev, 128), I32),
            pltpu.VMEM((rows_dev, 128), I32),
            pltpu.VMEM((rows_dev, 128), F32),
            pltpu.VMEM((8, rows_dev), F32),
            pltpu.VMEM((8, rows_dev), F32),
        ],
        compiler_params=PARAMS,
        cost_estimate=pl.CostEstimate(
            flops=5 * 2 * half * half * feature, bytes_accessed=4 * half * feature * 2, transcendentals=0
        ),
        name="near",
    )(*own, *sib, meta)
    hbm = pl.BlockSpec(memory_space=pl.ANY)
    vmem = pl.BlockSpec(memory_space=pltpu.VMEM)
    best = pl.pallas_call(
        lambda *refs: far_kernel(pools, group, *refs),
        out_shape=sds((devices, group * places), F32),
        in_specs=[hbm] * 10 + [vmem] * 2,
        scratch_shapes=[
            pltpu.VMEM((10, half, feature), BF16),
            pltpu.SemaphoreType.DMA((10,)),
            pltpu.VMEM((2, half, half), F32),
            pltpu.VMEM((4, rows_dev, 128), I32),
            pltpu.VMEM((4, rows_dev, 128), I32),
            pltpu.VMEM((4, rows_dev, 128), F32),
            pltpu.VMEM((8, rows_dev), F32),
            pltpu.VMEM((group, rows_dev), F32),
        ],
        compiler_params=PARAMS,
        cost_estimate=pl.CostEstimate(
            flops=12 * 2 * half * half * feature, bytes_accessed=10 * half * feature * 2, transcendentals=0
        ),
        name="far",
    )(*own, *sib, *low, *lows, *high, meta, near)
    returned = lax.all_to_all(best, ("pool", "grp"), split_axis=0, concat_axis=0, tiled=True)
    scores = pl.pallas_call(
        lambda *refs: score_kernel(pools, group, places, *refs),
        out_shape=sds((1, rows_dev), F32),
        compiler_params=PARAMS,
        name="score",
    )(table, returned)
    return scores.reshape(rows_dev)


def solution(mesh):
    in_specs = (P(("pool", "grp"), None), P(), P(), P())
    out_specs = P(("pool", "grp"))
    return jax.shard_map(body, mesh=mesh, in_specs=in_specs, out_specs=out_specs, check_vma=False)
```

```python
import jax
import jax.numpy as jnp
from jax import lax
from jax.experimental import pallas as pl
from jax.experimental.pallas import tpu as pltpu
from jax.sharding import PartitionSpec as P

EPS = 1e-06
F32 = jnp.float32
BF16 = jnp.bfloat16
I32 = jnp.int32
QUARTER = 256
CODE = 8192
NT = (((1,), (1,)), ((), ()))
PARAMS = pltpu.CompilerParams(vmem_limit_bytes=24 * 1024 * 1024)


def iota(shape, dim):
    return lax.broadcasted_iota(I32, shape, dim)


def normal_rows(rows):
    return (rows * lax.rsqrt(jnp.sum(rows * rows, axis=1, keepdims=True) + EPS)).astype(BF16)


def picked_rows(table, emb, first, count, pools):
    width = emb.shape[0]
    wanted = []
    for k in range(first, first + count):
        hit = table[:, k : k + 1] == iota((table.shape[0], width), 1)
        wanted.append(jnp.where(hit, 1.0, 0.0).reshape(pools, -1, width))
    choice = jnp.concatenate(wanted, axis=1).reshape(-1, width).astype(BF16)
    return normal_rows(jnp.dot(choice, emb, preferred_element_type=F32))


def table_kernel(
    pools, group, places, last, members_hbm, valid_hbm, emb_hbm, table_ref, main_ref, last_ref,
    members_ref, valid_ref, emb_ref, found_ref, sems,
):
    copies = []
    for n, (source, target) in enumerate(
        ((members_hbm, members_ref), (valid_hbm, valid_ref), (emb_hbm, emb_ref))
    ):
        copies.append(pltpu.make_async_copy(source, target, sems.at[n]))
        copies[-1].start()
    rows_dev = emb_ref.shape[0]
    device = lax.axis_index("pool") * group + lax.axis_index("grp")
    blocks, block_len = members_ref.shape
    devices = blocks // 2
    before = jnp.where(
        iota((block_len, block_len), 0) < iota((block_len, block_len), 1), 1.0, 0.0
    ).astype(BF16)
    at = iota((blocks, blocks), 1) == iota((blocks, blocks), 0)
    copies[0].wait()
    copies[1].wait()
    live = jnp.sum(jnp.where(at, valid_ref[...], 0), axis=1, keepdims=True)
    local = members_ref[...] - device * rows_dev
    mine = (local >= 0) & (local < rows_dev) & (iota((blocks, block_len), 1) < live)
    ones = jnp.where(mine, 1.0, 0.0)
    counts = jnp.broadcast_to(jnp.sum(ones, axis=1, keepdims=True), (blocks, 128))
    counts = jnp.where(iota((blocks, 128), 0) % 2 == 1, pltpu.roll(counts, 1, 0), 0.0)
    rank = jnp.dot(ones.astype(BF16), before, preferred_element_type=F32) + counts[:, :1]
    rank = jnp.where(mine, rank, -1.0)
    value = (local + 1).astype(F32)
    lane = iota((blocks, 128), 1)
    found = jnp.zeros((blocks, 128), F32)
    for k in range(places):
        entry = jnp.sum(jnp.where(rank == k, value, 0.0), axis=1, keepdims=True)
        found = jnp.where(lane == k, entry, found)
    found_ref[...] = found
    pair = found_ref[pl.ds(0, devices, stride=2), :] + found_ref[pl.ds(1, devices, stride=2), :]
    table = pair.astype(I32) - 1
    table_ref[...] = table
    copies[2].wait()
    last_ref[...] = picked_rows(table, emb_ref[...], places - last, last, pools)
    main_ref[...] = picked_rows(table, emb_ref[...], 0, places - last, pools)


def columns(row):
    return jnp.transpose(jnp.broadcast_to(row, (128, row.shape[1])))


def relatives():
    group = lax.axis_size("grp")
    index = lax.axis_index("grp")
    flip = 1 - 2 * (index % 2)
    below = (index + group - 2) % group
    return index, index + flip, below, below + flip, (index + 2) % group


def meta_kernel(
    group, places, last, members_hbm, valid_hbm, cluster_hbm, out_ref, codes_ref,
    members_ref, valid_ref, cluster_ref, sems,
):
    blocks = valid_ref.shape[1]
    block_len = members_ref.shape[1]
    pool = lax.axis_index("pool")
    first_block = pl.multiple_of(pool * 2 * group, 2 * group)
    copies = []
    for n, (source, target) in enumerate(
        (
            (members_hbm.at[pl.ds(first_block, 2 * group), :], members_ref),
            (valid_hbm, valid_ref),
            (cluster_hbm, cluster_ref),
        )
    ):
        copies.append(pltpu.make_async_copy(source, target, sems.at[n]))
        copies[-1].start()
    sources = blocks // 2
    slots = 2 * block_len
    width = group * places
    before = jnp.where(iota((slots, slots), 0) < iota((slots, slots), 1), 1.0, 0.0).astype(BF16)
    slot = iota((1, slots), 1)
    kind = iota((2 * width, slots), 0)
    kind_place = kind % width // group
    kind_owner = kind % group
    kind_value = jnp.where(kind < width, slot // 32, slot % 32 + 1)
    found = jnp.zeros((sources, 2 * width), F32)
    block_lane = iota((1, blocks), 1)
    lane = iota((1, width), 1)
    first_cluster = jnp.zeros((1, width), I32)
    second_cluster = jnp.zeros((1, width), I32)
    for copy in copies:
        copy.wait()
    for owner in range(group):
        halves, lives = [], []
        for half in range(2):
            halves.append(members_ref[2 * owner + half : 2 * owner + half + 1, :])
            at = block_lane == first_block + 2 * owner + half
            lives.append(jnp.sum(jnp.where(at, valid_ref[...], 0), axis=1, keepdims=True))
            cluster = jnp.sum(jnp.where(at, cluster_ref[...], 0), axis=1, keepdims=True)
            if half == 0:
                first_cluster = jnp.where(lane % group == owner, cluster, first_cluster)
            else:
                second_cluster = jnp.where(lane % group == owner, cluster, second_cluster)
        rows = jnp.concatenate(halves, axis=1)
        end = jnp.where(slot < block_len, lives[0], block_len + lives[1])
        origin = jnp.where(slot < end, rows // slots, -1)
        match = iota((sources, slots), 0) == origin
        ones = jnp.where(match, 1.0, 0.0).astype(BF16)
        ranks = jnp.dot(ones, before, preferred_element_type=F32)
        rank = jnp.sum(jnp.where(match, ranks, 0.0), axis=0, keepdims=True).astype(I32)
        weight = jnp.where((kind_owner == owner) & (kind_place == rank), kind_value, 0)
        found = found + lax.dot_general(
            ones, weight.astype(F32).astype(BF16), NT, preferred_element_type=F32
        )
    found = found.astype(I32)
    place = found[:, :width] * 32 + found[:, width:] - 1
    filled = found[:, width:] > 0
    position = jnp.where(filled, place + lane % group * slots, -1)
    cluster = jnp.where(filled, jnp.where(place < block_len, first_cluster, second_cluster), -1)
    main = (places - last) * group
    rest = last * group
    pools = sources // group
    for n, values in enumerate((position, cluster)):
        for p in range(pools):
            own = values[p * group : (p + 1) * group, :]
            out_ref[n, :, p * main : (p + 1) * main] = own[:, :main]
            at = pools * main + p * rest
            out_ref[n, :, at : at + rest] = own[:, main:]
    for n, cls in enumerate(relatives()[:4]):
        pos = out_ref[0, pl.ds(cls, 1), :]
        cluster = out_ref[1, pl.ds(cls, 1), :]
        codes_ref[n, :, :] = columns(jnp.where(cluster < 0, -2 * CODE, cluster * CODE + pos))


def run(pieces, sims_ref):
    for n in range(len(pieces) + 1):
        if n < len(pieces):
            piece = pieces[n]
            sims_ref[n % 2, : piece["count"], :] = lax.dot_general(
                piece["left"](), piece["right"](), NT, preferred_element_type=F32
            )
        if n > 0:
            take_maxima(sims_ref.at[(n - 1) % 2], **pieces[n - 1])


def take_maxima(sims_ref, left, right, count, codes, rows, start, pos_row, cluster_row, col, col_start, same):
    step = 128
    right_pos, right_cluster = pos_row(), cluster_row()
    parts = QUARTER // 128
    best_col = [jnp.zeros((8, 128), F32) for _ in range(parts)]
    for top in range(0, count, step):
        code = codes[start + top : start + top + step, :]
        pos = code & (CODE - 1)
        cluster = code >> 13
        best = rows[start + top : start + top + step, :]
        for part in range(parts):
            lanes = slice(part * 128, part * 128 + 128)
            sims = sims_ref[top : top + step, lanes]
            sims = jnp.where(cluster == right_cluster[:, lanes], sims, 0.0)
            earlier = right_pos[:, lanes] < pos
            best = jnp.maximum(best, jnp.where(earlier, sims, 0.0))
            if top < same:
                later = jnp.where(earlier, 0.0, sims)
                best_col[part] = jnp.maximum(
                    best_col[part], jnp.max(later.reshape(-1, 8, 128), axis=0)
                )
        rows[start + top : start + top + step, :] = best
    if same > 0:
        for part in range(parts):
            lanes = slice(col_start + part * 128, col_start + part * 128 + 128)
            col[:, lanes] = jnp.maximum(col[:, lanes], best_col[part])


def row_result(row_ref):
    return jnp.max(jnp.transpose(row_ref[...]), axis=0, keepdims=True)


def col_result(col_ref):
    return jnp.max(col_ref[...], axis=0, keepdims=True)


OWN, SIB, LOW, LOWS, HIGH = range(5)


class Tiles:
    def __init__(self, meta, codes, rows, cols, parts):
        self.meta, self.codes, self.rows, self.cols, self.parts = meta, codes, rows, cols, parts
        self.relatives = relatives()
        for ref in (rows, cols):
            ref[...] = jnp.zeros(ref.shape, F32)

    def load(self, cls, quarter, count=1):
        ref, at = self.parts[cls, quarter]
        if len(ref.shape) == 3:
            return ref[:, at : at + QUARTER // ref.shape[0], :].reshape(-1, ref.shape[2])
        return ref[at : at + count * QUARTER, :]

    def piece(self, left, quarter, count, right, right_quarter, same=None):
        lanes = slice(right_quarter * QUARTER, (right_quarter + 1) * QUARTER)
        cls = self.relatives[right]
        return dict(
            left=lambda: self.load(left, quarter, count),
            right=lambda: self.load(right, right_quarter),
            count=count * QUARTER,
            codes=self.codes.at[left],
            rows=self.rows.at[left],
            start=quarter * QUARTER,
            pos_row=lambda: self.meta[0, pl.ds(cls, 1), lanes],
            cluster_row=lambda: self.meta[1, pl.ds(cls, 1), lanes],
            col=self.cols.at[right],
            col_start=right_quarter * QUARTER,
            same=count * QUARTER if same is None else same,
        )

    def matched(self, flip, left, right, pairs):
        return [
            self.piece(left, a, 1, right, b) for a, b in pairs if (a + b) % 2 == flip
        ]

    def finish(self, before, out):
        for cls in range(5):
            best = col_result(self.cols.at[cls])
            if cls < HIGH:
                best = jnp.maximum(best, row_result(self.rows.at[cls]))
            if before is not None:
                best = jnp.maximum(best, before[cls : cls + 1, :])
            out[cls : cls + 1, :] = best


def either(flag, work):
    pl.when(flag)(lambda: work(1))
    pl.when(jnp.logical_not(flag))(lambda: work(0))


def second_core():
    return lax.axis_index("grp") % 2 == 1


def outer_chip():
    chip = lax.axis_index("grp") // 2
    return (chip == 0) | (chip == 3)


def quarters(*groups):
    parts = {}
    for cls, refs in groups:
        for quarter, ref, at in refs:
            parts[cls, quarter] = (ref, at)
    return parts


def whole(ref):
    return [(q, ref, q * QUARTER) for q in range(3)]


def near_kernel(own0, sib0, meta, codes, out, sims, rows, cols):
    tiles = Tiles(meta, codes, rows, cols, quarters((OWN, whole(own0)), (SIB, whole(sib0))))
    run([tiles.piece(OWN, 0, b + 1, OWN, b, same=b * QUARTER) for b in range(3)], sims)
    pairs = [(a, b) for b in range(3) for a in range(3)]
    either(second_core(), lambda flip: run(tiles.matched(flip, OWN, SIB, pairs), sims))
    tiles.finish(None, out)


def middle_kernel(
    own0, sib0, arrived, sib3, lows3, low0, low1, lows0, lows1, high0, high1, meta, codes, before,
    out, sims, rows, cols,
):
    tiles = Tiles(
        meta, codes, rows, cols,
        quarters(
            (OWN, whole(own0) + [(3, arrived, 0)]),
            (SIB, whole(sib0) + [(3, sib3, 0)]),
            (LOW, [(0, low0, 0), (1, low1, 0), (3, arrived, 16)]),
            (LOWS, [(0, lows0, 0), (1, lows1, 0), (3, lows3, 0)]),
            (HIGH, [(0, high0, 0), (1, high1, 0), (3, arrived, 32)]),
        ),
    )
    pieces = [tiles.piece(OWN, 0, 3, OWN, 3), tiles.piece(OWN, 3, 1, OWN, 3, same=0)]
    for b in (0, 1, 3):
        for cls in (OWN, SIB):
            pieces.append(tiles.piece(cls, 0, 3, HIGH, b))
            pieces.append(tiles.piece(cls, 3, 1, HIGH, b))
    run(pieces, sims)
    pairs = [(a, b) for b in range(4) for a in range(4) if 3 in (a, b)]
    either(second_core(), lambda flip: run(tiles.matched(flip, OWN, SIB, pairs), sims))
    pairs = [(a, b) for b in (0, 1, 3) for a in (0, 1, 3)]
    either(
        outer_chip(),
        lambda flip: run(
            tiles.matched(flip, LOW, HIGH, pairs) + tiles.matched(flip, LOWS, HIGH, pairs), sims
        ),
    )
    tiles.finish(before, out)


def late_kernel(
    own0, sib0, arrived, sib3, lows3, low0, low1, low2, lows0, lows1, high0, high1, high2, meta,
    codes, before, out, sims, rows, cols,
):
    tiles = Tiles(
        meta, codes, rows, cols,
        quarters(
            (OWN, whole(own0) + [(3, arrived, 0)]),
            (SIB, whole(sib0) + [(3, sib3, 0)]),
            (LOW, [(0, low0, 0), (1, low1, 0), (2, low2, 0), (3, arrived, 16)]),
            (LOWS, [(0, lows0, 0), (1, lows1, 0), (3, lows3, 0)]),
            (HIGH, [(0, high0, 0), (1, high1, 0), (2, high2, 0), (3, arrived, 32)]),
        ),
    )
    pieces = []
    for cls in (OWN, SIB):
        pieces.append(tiles.piece(cls, 0, 3, HIGH, 2))
        pieces.append(tiles.piece(cls, 3, 1, HIGH, 2))
    run(pieces, sims)
    pairs = [(a, b) for b in range(4) for a in range(4) if 2 in (a, b)]
    others = [(a, 2) for a in (0, 1, 3)]
    either(
        outer_chip(),
        lambda flip: run(
            tiles.matched(flip, LOW, HIGH, pairs) + tiles.matched(flip, LOWS, HIGH, others), sims
        ),
    )
    tiles.finish(before, out)


def last_kernel(
    pools, group, main, rest, arrived, lows2, high0, high1, high2, meta, codes, before,
    out, sims, rows, cols, best, every,
):
    tiles = Tiles(
        meta, codes, rows, cols,
        quarters(
            (LOWS, [(2, lows2, 0)]),
            (HIGH, [(0, high0, 0), (1, high1, 0), (2, high2, 0), (3, arrived, 32)]),
        ),
    )
    pairs = [(2, b) for b in range(4)]
    either(outer_chip(), lambda flip: run(tiles.matched(flip, LOWS, HIGH, pairs), sims))
    best[...] = before[...]
    span = slice(2 * QUARTER, 3 * QUARTER)
    found = jnp.max(jnp.transpose(rows[LOWS, span, :]), axis=0, keepdims=True)
    best[LOWS : LOWS + 1, span] = jnp.maximum(best[LOWS : LOWS + 1, span], found)
    best[HIGH : HIGH + 1, :] = jnp.maximum(best[HIGH : HIGH + 1, :], col_result(cols.at[HIGH]))
    every[...] = jnp.zeros(every.shape, F32)
    for cls, place in enumerate(tiles.relatives):
        every[pl.ds(place, 1), :] = best[cls : cls + 1, :]
    for p in range(pools):
        rows_out = slice(p * group, (p + 1) * group)
        out[rows_out, :main] = every[:, p * main : (p + 1) * main]
        at = pools * main + p * rest
        out[rows_out, main:] = every[:, at : at + rest]


def score_kernel(pools, group, places, table_ref, returned_ref, out_ref):
    rows_dev = out_ref.shape[1]
    arrived = jnp.transpose(
        jnp.concatenate([returned_ref[...], jnp.zeros_like(returned_ref)], axis=1)
    )
    table = table_ref[...]
    row = iota((8, rows_dev), 1)
    total = jnp.zeros((8, rows_dev), F32)
    for p in range(pools):
        for k in range(places):
            value = jnp.max(
                arrived[k * group : (k + 1) * group, p * group : (p + 1) * group],
                axis=1,
                keepdims=True,
            )
            entry = table[p * group : (p + 1) * group, k : k + 1]
            total = jnp.where(entry == row, value, total)
    out_ref[...] = jnp.sum(total, axis=0, keepdims=True)


def body(embeddings, members, valid, block_cluster):
    rows_dev, feature = embeddings.shape
    pools = lax.axis_size("pool")
    group = lax.axis_size("grp")
    devices = pools * group
    places = rows_dev // devices
    last = places // 4
    sds = jax.ShapeDtypeStruct
    hbm = pl.BlockSpec(memory_space=pltpu.HBM)
    valid_row = valid.reshape(1, -1)
    cluster_row = block_cluster.reshape(1, -1)
    blocks, block_len = members.shape

    table, main, rest = pl.pallas_call(
        lambda *refs: table_kernel(pools, group, places, last, *refs),
        out_shape=(
            sds((devices, 128), I32),
            sds((3 * QUARTER, feature), BF16),
            sds((QUARTER, feature), BF16),
        ),
        in_specs=[hbm] * 3,
        scratch_shapes=[
            pltpu.VMEM((blocks, block_len), I32),
            pltpu.VMEM((1, blocks), I32),
            pltpu.VMEM((rows_dev, feature), BF16),
            pltpu.VMEM((blocks, 128), F32),
            pltpu.SemaphoreType.DMA((3,)),
        ],
        compiler_params=PARAMS,
        cost_estimate=cost(rows_dev * rows_dev * feature),
        name="table",
    )(members, valid_row, embeddings)
    meta, codes = pl.pallas_call(
        lambda *refs: meta_kernel(group, places, last, *refs),
        out_shape=(sds((2, group, rows_dev), I32), sds((4, rows_dev, 128), I32)),
        in_specs=[hbm] * 3,
        scratch_shapes=[
            pltpu.VMEM((2 * group, block_len), I32),
            pltpu.VMEM((1, blocks), I32),
            pltpu.VMEM((1, blocks), I32),
            pltpu.SemaphoreType.DMA((3,)),
        ],
        compiler_params=PARAMS,
        cost_estimate=cost(2 * rows_dev**3),
        name="meta",
    )(members, valid_row, cluster_row)

    def shift(rows, by):
        return lax.ppermute(rows, "grp", [(g, (g + by) % group) for g in range(group)])

    def swap(rows):
        return lax.ppermute(rows, "grp", [(g, g ^ 1) for g in range(group)])

    def to_pools(rows):
        return lax.all_to_all(rows, "pool", split_axis=0, concat_axis=0, tiled=True)

    low_rest, high_rest = shift(rest, 2), shift(rest, -2)
    own0 = to_pools(main.reshape(pools, -1, feature)).reshape(-1, feature)
    sent = [part.reshape(pools, -1, feature) for part in (rest, low_rest, high_rest)]
    arrived = to_pools(jnp.concatenate(sent, axis=1))
    low, lows, high = [], [], []
    for q in range(3):
        part = own0[q * QUARTER : (q + 1) * QUARTER]
        low.append(shift(part, 2))
        high.append(shift(part, -2))
        lows.append(swap(low[-1]))
    sib0 = swap(own0)
    width = QUARTER // pools
    sib3 = swap(arrived[:, :width].reshape(-1, feature))
    lows3 = swap(arrived[:, width : 2 * width].reshape(-1, feature))

    def tiles(kernel, name, squares, operands, out_shape=(8, rows_dev), more=()):
        return pl.pallas_call(
            kernel,
            out_shape=sds(out_shape, F32),
            scratch_shapes=[
                pltpu.VMEM((2, 3 * QUARTER, QUARTER), F32),
                pltpu.VMEM((4, rows_dev, 128), F32),
                pltpu.VMEM((5, 8, rows_dev), F32),
                *more,
            ],
            compiler_params=PARAMS,
            cost_estimate=cost(squares * QUARTER * QUARTER * feature),
            name=name,
        )(*operands)

    near = tiles(near_kernel, "near", 11, (own0, sib0, meta, codes))
    middle = tiles(
        middle_kernel, "middle", 42,
        (own0, sib0, arrived, sib3, lows3, *low[:2], *lows[:2], *high[:2], meta, codes, near),
    )
    late = tiles(
        late_kernel, "late", 14,
        (own0, sib0, arrived, sib3, lows3, *low, *lows[:2], *high, meta, codes, middle),
    )
    best = tiles(
        lambda *refs: last_kernel(pools, group, group * (places - last), group * last, *refs),
        "last", 2, (arrived, lows[2], *high, meta, codes, late),
        out_shape=(devices, group * places),
        more=(pltpu.VMEM((8, rows_dev), F32), pltpu.VMEM((group, rows_dev), F32)),
    )
    returned = lax.all_to_all(best, ("pool", "grp"), split_axis=0, concat_axis=0, tiled=True)
    scores = pl.pallas_call(
        lambda *refs: score_kernel(pools, group, places, *refs),
        out_shape=sds((1, rows_dev), F32),
        compiler_params=PARAMS,
        name="score",
    )(table, returned)
    return scores.reshape(rows_dev)


def cost(products):
    return pl.CostEstimate(flops=2 * products, bytes_accessed=0, transcendentals=0)


def solution(mesh):
    in_specs = (P(("pool", "grp"), None), P(), P(), P())
    out_specs = P(("pool", "grp"))
    return jax.shard_map(body, mesh=mesh, in_specs=in_specs, out_specs=out_specs, check_vma=False)
```

```python
import jax
import jax.numpy as jnp
from jax import lax
from jax.experimental import pallas as pl
from jax.experimental.pallas import tpu as pltpu
from jax.sharding import PartitionSpec as P

EPS = 1e-06
F32 = jnp.float32
BF16 = jnp.bfloat16
I32 = jnp.int32
QUARTER = 256
CODE = 8192
NT = (((1,), (1,)), ((), ()))
PARAMS = pltpu.CompilerParams(vmem_limit_bytes=20 * 1024 * 1024)
TABLE_PARAMS = pltpu.CompilerParams(vmem_limit_bytes=62 * 1024 * 1024)


def iota(shape, dim):
    return lax.broadcasted_iota(I32, shape, dim)


def normal_rows(rows):
    return (rows * lax.rsqrt(jnp.sum(rows * rows, axis=1, keepdims=True) + EPS)).astype(BF16)


def picked_rows(table, emb, first, count, pools):
    width = emb.shape[0]
    wanted = []
    for k in range(first, first + count):
        hit = table[:, k : k + 1] == iota((table.shape[0], width), 1)
        wanted.append(jnp.where(hit, 1.0, 0.0).reshape(pools, -1, width))
    choice = jnp.concatenate(wanted, axis=1).reshape(-1, width).astype(BF16)
    return normal_rows(jnp.dot(choice, emb, preferred_element_type=F32))


def table_kernel(
    pools, group, places, last, members_hbm, valid_hbm, emb_hbm, table_ref, main_ref,
    members_ref, valid_ref, emb_ref, found_ref, sems,
):
    copies = []
    for n, (source, target) in enumerate(
        ((members_hbm, members_ref), (valid_hbm, valid_ref), (emb_hbm, emb_ref))
    ):
        copies.append(pltpu.make_async_copy(source, target, sems.at[n]))
        copies[-1].start()
    rows_dev = emb_ref.shape[0]
    device = lax.axis_index("pool") * group + lax.axis_index("grp")
    blocks, block_len = members_ref.shape
    devices = blocks // 2
    before = jnp.where(
        iota((block_len, block_len), 0) < iota((block_len, block_len), 1), 1.0, 0.0
    ).astype(BF16)
    at = iota((blocks, blocks), 1) == iota((blocks, blocks), 0)
    copies[0].wait()
    copies[1].wait()
    live = jnp.sum(jnp.where(at, valid_ref[...], 0), axis=1, keepdims=True)
    local = members_ref[...] - device * rows_dev
    mine = (local >= 0) & (local < rows_dev) & (iota((blocks, block_len), 1) < live)
    ones = jnp.where(mine, 1.0, 0.0)
    counts = jnp.broadcast_to(jnp.sum(ones, axis=1, keepdims=True), (blocks, 128))
    counts = jnp.where(iota((blocks, 128), 0) % 2 == 1, pltpu.roll(counts, 1, 0), 0.0)
    rank = jnp.dot(ones.astype(BF16), before, preferred_element_type=F32) + counts[:, :1]
    rank = jnp.where(mine, rank, -1.0)
    value = (local + 1).astype(F32)
    lane = iota((blocks, 128), 1)
    found = jnp.zeros((blocks, 128), F32)
    for k in range(places):
        entry = jnp.sum(jnp.where(rank == k, value, 0.0), axis=1, keepdims=True)
        found = jnp.where(lane == k, entry, found)
    found_ref[...] = found
    pair = found_ref[pl.ds(0, devices, stride=2), :] + found_ref[pl.ds(1, devices, stride=2), :]
    table = pair.astype(I32) - 1
    table_ref[...] = table
    copies[2].wait()
    main_ref[...] = picked_rows(table, emb_ref[...], 0, places - last, pools)


def rest_kernel(pools, places, last, table_ref, emb_ref, after, out):
    del after
    out[...] = picked_rows(table_ref[...], emb_ref[...], places - last, last, pools)


def relatives():
    group = lax.axis_size("grp")
    index = lax.axis_index("grp")
    flip = 1 - 2 * (index % 2)
    below = (index + group - 2) % group
    return index, index + flip, below, below + flip, (index + 2) % group


def meta_kernel(
    group, places, last, members_hbm, valid_hbm, cluster_hbm, out_ref, codes_ref,
    members_ref, valid_ref, cluster_ref, packed_ref, sems,
):
    blocks = valid_ref.shape[1]
    block_len = members_ref.shape[1]
    pool = lax.axis_index("pool")
    first_block = pl.multiple_of(pool * 2 * group, 2 * group)
    copies = []
    for n, (source, target) in enumerate(
        (
            (members_hbm.at[pl.ds(first_block, 2 * group), :], members_ref),
            (valid_hbm, valid_ref),
            (cluster_hbm, cluster_ref),
        )
    ):
        copies.append(pltpu.make_async_copy(source, target, sems.at[n]))
        copies[-1].start()
    sources = blocks // 2
    slots = 2 * block_len
    width = group * places
    before = jnp.where(iota((slots, slots), 0) < iota((slots, slots), 1), 1.0, 0.0).astype(BF16)
    slot = iota((1, slots), 1)
    kind = iota((2 * width, slots), 0)
    kind_place = kind % width // group
    kind_owner = kind % group
    kind_value = jnp.where(kind < width, slot // 32, slot % 32 + 1)
    found = jnp.zeros((sources, 2 * width), F32)
    block_lane = iota((1, blocks), 1)
    lane = iota((1, width), 1)
    first_cluster = jnp.zeros((1, width), I32)
    second_cluster = jnp.zeros((1, width), I32)
    for copy in copies:
        copy.wait()
    for owner in range(group):
        halves, lives = [], []
        for half in range(2):
            halves.append(members_ref[2 * owner + half : 2 * owner + half + 1, :])
            at = block_lane == first_block + 2 * owner + half
            lives.append(jnp.sum(jnp.where(at, valid_ref[...], 0), axis=1, keepdims=True))
            cluster = jnp.sum(jnp.where(at, cluster_ref[...], 0), axis=1, keepdims=True)
            if half == 0:
                first_cluster = jnp.where(lane % group == owner, cluster, first_cluster)
            else:
                second_cluster = jnp.where(lane % group == owner, cluster, second_cluster)
        rows = jnp.concatenate(halves, axis=1)
        end = jnp.where(slot < block_len, lives[0], block_len + lives[1])
        origin = jnp.where(slot < end, rows // slots, -1)
        match = iota((sources, slots), 0) == origin
        ones = jnp.where(match, 1.0, 0.0).astype(BF16)
        ranks = jnp.dot(ones, before, preferred_element_type=F32)
        rank = jnp.sum(jnp.where(match, ranks, 0.0), axis=0, keepdims=True).astype(I32)
        weight = jnp.where((kind_owner == owner) & (kind_place == rank), kind_value, 0)
        found = found + lax.dot_general(
            ones, weight.astype(F32).astype(BF16), NT, preferred_element_type=F32
        )
    found = found.astype(I32)
    place = found[:, :width] * 32 + found[:, width:] - 1
    filled = found[:, width:] > 0
    position = jnp.where(filled, place + lane % group * slots, -1)
    cluster = jnp.where(filled, jnp.where(place < block_len, first_cluster, second_cluster), -1)
    main = (places - last) * group
    rest = last * group
    pools = sources // group
    for n, values in enumerate((position, cluster)):
        for p in range(pools):
            own = values[p * group : (p + 1) * group, :]
            out_ref[n, :, p * main : (p + 1) * main] = own[:, :main]
            at = pools * main + p * rest
            out_ref[n, :, at : at + rest] = own[:, main:]
    packed_ref[...] = jnp.zeros(packed_ref.shape, I32)
    for n, cls in enumerate(relatives()[:4]):
        pos = out_ref[0, pl.ds(cls, 1), :]
        cluster = out_ref[1, pl.ds(cls, 1), :]
        packed_ref[n : n + 1, :] = jnp.where(cluster < 0, -2 * CODE, cluster * CODE + pos)
    codes_ref[...] = jnp.transpose(packed_ref[...])


def run(pieces, sims_ref):
    for n in range(len(pieces) + 1):
        if n < len(pieces):
            piece = pieces[n]
            sims_ref[n % 2, : piece["count"], :] = lax.dot_general(
                piece["left"](), piece["right"](), NT, preferred_element_type=F32
            )
        if n > 0:
            take_maxima(sims_ref.at[(n - 1) % 2], **pieces[n - 1])


def take_maxima(sims_ref, left, right, count, codes, cls, rows, start, pos_row, cluster_row, col, col_start, same):
    step = 128
    right_pos, right_cluster = pos_row(), cluster_row()
    parts = QUARTER // 128
    best_col = [jnp.zeros((8, 128), F32) for _ in range(parts)]
    for top in range(0, count, step):
        code = codes[start + top : start + top + step, cls : cls + 1]
        code = jnp.broadcast_to(code, (step, 128))
        pos = code & (CODE - 1)
        cluster = code >> 13
        best = rows[start + top : start + top + step, :]
        for part in range(parts):
            lanes = slice(part * 128, part * 128 + 128)
            sims = sims_ref[top : top + step, lanes]
            sims = jnp.where(cluster == right_cluster[:, lanes], sims, 0.0)
            earlier = right_pos[:, lanes] < pos
            best = jnp.maximum(best, jnp.where(earlier, sims, 0.0))
            if top < same:
                later = jnp.where(earlier, 0.0, sims)
                best_col[part] = jnp.maximum(
                    best_col[part], jnp.max(later.reshape(-1, 8, 128), axis=0)
                )
        rows[start + top : start + top + step, :] = best
    if same > 0:
        for part in range(parts):
            lanes = slice(col_start + part * 128, col_start + part * 128 + 128)
            col[:, lanes] = jnp.maximum(col[:, lanes], best_col[part])


def row_result(row_ref):
    return jnp.max(jnp.transpose(row_ref[...]), axis=0, keepdims=True)


def col_result(col_ref):
    return jnp.max(col_ref[...], axis=0, keepdims=True)


OWN, SIB, LOW, LOWS, HIGH = range(5)


class Fetch:
    def __init__(self, sources, held, sems):
        self.held, self.copies = dict(), dict()
        for n, source in enumerate(sources):
            copy = pltpu.make_async_copy(source, held[n], sems.at[n])
            copy.start()
            self.held[n], self.copies[n] = held[n], copy

    def get(self, n):
        copy = self.copies.pop(n, None)
        if copy is not None:
            copy.wait()
        return self.held[n]

    def all(self):
        for n in list(self.copies):
            self.get(n)


class Tiles:
    def __init__(self, fetch, meta, codes, rows, cols, parts):
        self.fetch, self.parts = fetch, parts
        self.meta, self.codes, self.rows, self.cols = meta, codes, rows, cols
        self.relatives = relatives()
        for ref in (rows, cols):
            ref[...] = jnp.zeros(ref.shape, F32)

    def load(self, cls, quarter, count=1):
        number, at = self.parts[cls, quarter]
        ref = self.fetch.get(number)
        if len(ref.shape) == 3:
            return ref[:, at : at + QUARTER // ref.shape[0], :].reshape(-1, ref.shape[2])
        return ref[at : at + count * QUARTER, :]

    def piece(self, left, quarter, count, right, right_quarter, same=None):
        lanes = slice(right_quarter * QUARTER, (right_quarter + 1) * QUARTER)
        place = self.relatives[right]
        return dict(
            left=lambda: self.load(left, quarter, count),
            right=lambda: self.load(right, right_quarter),
            count=count * QUARTER,
            codes=self.codes,
            cls=left,
            rows=self.rows.at[left],
            start=quarter * QUARTER,
            pos_row=lambda: self.meta[0, pl.ds(place, 1), lanes],
            cluster_row=lambda: self.meta[1, pl.ds(place, 1), lanes],
            col=self.cols.at[right],
            col_start=right_quarter * QUARTER,
            same=count * QUARTER if same is None else same,
        )

    def matched(self, flip, left, right, pairs):
        return [
            self.piece(left, a, 1, right, b) for a, b in pairs if (a + b) % 2 == flip
        ]

    def finish(self, before, out):
        for cls in range(5):
            best = col_result(self.cols.at[cls])
            if cls < HIGH:
                best = jnp.maximum(best, row_result(self.rows.at[cls]))
            if before is not None:
                best = jnp.maximum(best, before[cls : cls + 1, :])
            out[cls : cls + 1, :] = best


def either(flag, work):
    pl.when(flag)(lambda: work(1))
    pl.when(jnp.logical_not(flag))(lambda: work(0))


def second_core():
    return lax.axis_index("grp") % 2 == 1


def outer_chip():
    chip = lax.axis_index("grp") // 2
    return (chip == 0) | (chip == 3)


def parts_of(**groups):
    names = dict(own=OWN, sib=SIB, low=LOW, lows=LOWS, high=HIGH)
    return {(names[name], q): part for name, parts in groups.items() for q, part in parts.items()}


def whole(n):
    return {q: (n, q * QUARTER) for q in range(3)}


def halves(n):
    return {q: (n, q * QUARTER) for q in range(2)}


def join_kernel(pools, rest, low_rest, high_rest, out):
    width = QUARTER // pools
    for n, part in enumerate((rest, low_rest, high_rest)):
        out[:, n * width : (n + 1) * width, :] = part[...].reshape(pools, width, -1)


def cut_kernel(arrived, after, out):
    del after
    out[...] = arrived[:, : out.shape[1], :]


def follow_kernel(rows, after, out):
    del after
    out[...] = rows[...]


def near_kernel(own0, sib0, meta, codes, out, sims, rows, cols, sems, *held):
    fetch = Fetch((own0, sib0), held, sems)
    tiles = Tiles(fetch, meta, codes, rows, cols, parts_of(own=whole(0), sib=whole(1)))
    run([tiles.piece(OWN, 0, b + 1, OWN, b, same=b * QUARTER) for b in range(3)], sims)
    fetch.all()
    pairs = [(a, b) for b in range(3) for a in range(3)]
    either(second_core(), lambda flip: run(tiles.matched(flip, OWN, SIB, pairs), sims))
    tiles.finish(None, out)


def middle_kernel(
    own0, arrived, high01, sib0, swapped, low01, lows01, meta, codes, before, out,
    sims, rows, cols, sems, *held,
):
    fetch = Fetch((own0, arrived, high01, sib0, swapped, low01, lows01), held, sems)
    width = arrived.shape[1] // 3
    tiles = Tiles(
        fetch, meta, codes, rows, cols,
        parts_of(
            own={**whole(0), 3: (1, 0)},
            sib={**whole(3), 3: (4, 0)},
            low={**halves(5), 3: (1, width)},
            lows={**halves(6), 3: (4, width)},
            high={**halves(2), 3: (1, 2 * width)},
        ),
    )
    pieces = [tiles.piece(OWN, 0, 3, OWN, 3), tiles.piece(OWN, 3, 1, OWN, 3, same=0)]
    for cls in (OWN, SIB):
        for b in (3, 0, 1):
            pieces.append(tiles.piece(cls, 0, 3, HIGH, b))
            pieces.append(tiles.piece(cls, 3, 1, HIGH, b))
    run(pieces, sims)
    fetch.all()
    pairs = [(a, b) for b in range(4) for a in range(4) if 3 in (a, b)]
    either(second_core(), lambda flip: run(tiles.matched(flip, OWN, SIB, pairs), sims))
    pairs = [(a, b) for b in (0, 1, 3) for a in (0, 1, 3)]
    either(
        outer_chip(),
        lambda flip: run(
            tiles.matched(flip, LOW, HIGH, pairs) + tiles.matched(flip, LOWS, HIGH, pairs), sims
        ),
    )
    tiles.finish(before, out)


def late_kernel(
    own0, high2, sib0, arrived, swapped, low2, low01, lows01, high01, meta, codes, before, out,
    sims, rows, cols, sems, *held,
):
    fetch = Fetch((own0, high2, sib0, arrived, swapped, low2, low01, lows01, high01), held, sems)
    width = arrived.shape[1] // 3
    tiles = Tiles(
        fetch, meta, codes, rows, cols,
        parts_of(
            own={**whole(0), 3: (3, 0)},
            sib={**whole(2), 3: (4, 0)},
            low={**halves(6), 2: (5, 0), 3: (3, width)},
            lows={**halves(7), 3: (4, width)},
            high={**halves(8), 2: (1, 0), 3: (3, 2 * width)},
        ),
    )
    pieces = []
    for cls in (OWN, SIB):
        pieces.append(tiles.piece(cls, 0, 3, HIGH, 2))
    for cls in (OWN, SIB):
        pieces.append(tiles.piece(cls, 3, 1, HIGH, 2))
    run(pieces, sims)
    fetch.all()
    pairs = [(a, b) for b in range(4) for a in range(4) if 2 in (a, b)]
    others = [(a, 2) for a in (0, 1, 3)]
    either(
        outer_chip(),
        lambda flip: run(
            tiles.matched(flip, LOW, HIGH, pairs) + tiles.matched(flip, LOWS, HIGH, others), sims
        ),
    )
    tiles.finish(before, out)


def last_kernel(
    pools, group, main, rest, lows2, high01, high2, arrived, meta, codes, before, out,
    sims, rows, cols, best, every, sems, *held,
):
    fetch = Fetch((lows2, high01, high2, arrived), held, sems)
    width = arrived.shape[1] // 3
    tiles = Tiles(
        fetch, meta, codes, rows, cols,
        parts_of(lows={2: (0, 0)}, high={**halves(1), 2: (2, 0), 3: (3, 2 * width)}),
    )
    fetch.all()
    pairs = [(2, b) for b in range(4)]
    either(outer_chip(), lambda flip: run(tiles.matched(flip, LOWS, HIGH, pairs), sims))
    best[...] = before[...]
    span = slice(2 * QUARTER, 3 * QUARTER)
    found = jnp.max(jnp.transpose(rows[LOWS, span, :]), axis=0, keepdims=True)
    best[LOWS : LOWS + 1, span] = jnp.maximum(best[LOWS : LOWS + 1, span], found)
    best[HIGH : HIGH + 1, :] = jnp.maximum(best[HIGH : HIGH + 1, :], col_result(cols.at[HIGH]))
    every[...] = jnp.zeros(every.shape, F32)
    for cls, place in enumerate(tiles.relatives):
        every[pl.ds(place, 1), :] = best[cls : cls + 1, :]
    for p in range(pools):
        rows_out = slice(p * group, (p + 1) * group)
        out[rows_out, :main] = every[:, p * main : (p + 1) * main]
        at = pools * main + p * rest
        out[rows_out, main:] = every[:, at : at + rest]


def score_kernel(pools, group, places, table_ref, returned_ref, out_ref):
    rows_dev = out_ref.shape[1]
    arrived = jnp.transpose(
        jnp.concatenate([returned_ref[...], jnp.zeros_like(returned_ref)], axis=1)
    )
    table = table_ref[...]
    row = iota((8, rows_dev), 1)
    total = jnp.zeros((8, rows_dev), F32)
    for p in range(pools):
        for k in range(places):
            value = jnp.max(
                arrived[k * group : (k + 1) * group, p * group : (p + 1) * group],
                axis=1,
                keepdims=True,
            )
            entry = table[p * group : (p + 1) * group, k : k + 1]
            total = jnp.where(entry == row, value, total)
    out_ref[...] = jnp.sum(total, axis=0, keepdims=True)


def body(embeddings, members, valid, block_cluster):
    rows_dev, feature = embeddings.shape
    pools = lax.axis_size("pool")
    group = lax.axis_size("grp")
    devices = pools * group
    places = rows_dev // devices
    last = places // 4
    sds = jax.ShapeDtypeStruct
    hbm = pl.BlockSpec(memory_space=pltpu.HBM)
    valid_row = valid.reshape(1, -1)
    cluster_row = block_cluster.reshape(1, -1)
    blocks, block_len = members.shape

    table, main = pl.pallas_call(
        lambda *refs: table_kernel(pools, group, places, last, *refs),
        out_shape=(
            sds((devices, 128), I32),
            sds((3 * QUARTER, feature), BF16),
        ),
        in_specs=[hbm] * 3,
        scratch_shapes=[
            pltpu.VMEM((blocks, block_len), I32),
            pltpu.VMEM((1, blocks), I32),
            pltpu.VMEM((rows_dev, feature), BF16),
            pltpu.VMEM((blocks, 128), F32),
            pltpu.SemaphoreType.DMA((3,)),
        ],
        compiler_params=TABLE_PARAMS,
        cost_estimate=cost(rows_dev * rows_dev * feature),
        name="table",
    )(members, valid_row, embeddings)
    meta, codes = pl.pallas_call(
        lambda *refs: meta_kernel(group, places, last, *refs),
        out_shape=(sds((2, group, rows_dev), I32), sds((rows_dev, 128), I32)),
        in_specs=[hbm] * 3,
        scratch_shapes=[
            pltpu.VMEM((2 * group, block_len), I32),
            pltpu.VMEM((1, blocks), I32),
            pltpu.VMEM((1, blocks), I32),
            pltpu.VMEM((128, rows_dev), I32),
            pltpu.SemaphoreType.DMA((3,)),
        ],
        compiler_params=PARAMS,
        cost_estimate=cost(2 * rows_dev**3),
        name="meta",
    )(members, valid_row, cluster_row)

    def shift(rows, by):
        return lax.ppermute(rows, "grp", [(g, (g + by) % group) for g in range(group)])

    def swap(rows):
        return lax.ppermute(rows, "grp", [(g, g ^ 1) for g in range(group)])

    def to_pools(rows):
        return lax.all_to_all(rows, "pool", split_axis=0, concat_axis=0, tiled=True)

    vmem = pl.BlockSpec(memory_space=pltpu.VMEM)
    rest = pl.pallas_call(
        lambda *refs: rest_kernel(pools, places, last, *refs),
        out_shape=sds((QUARTER, feature), BF16),
        in_specs=[vmem, vmem, hbm],
        compiler_params=PARAMS,
        name="rest",
    )(table, embeddings, meta)
    low_rest, high_rest = shift(rest, 2), shift(rest, -2)
    own0 = to_pools(main.reshape(pools, -1, feature)).reshape(-1, feature)
    sent = pl.pallas_call(
        lambda *refs: join_kernel(pools, *refs),
        out_shape=sds((pools, 3 * QUARTER // pools, feature), BF16),
        compiler_params=PARAMS,
        name="join",
    )(rest, low_rest, high_rest)
    arrived = to_pools(sent)
    early = own0[: 2 * QUARTER]
    low01, high01 = shift(early, 2), shift(early, -2)
    sib0 = swap(own0)

    def tiles(kernel, name, squares, operands, small, out_shape=sds((8, rows_dev), F32), more=()):
        return pl.pallas_call(
            kernel,
            out_shape=out_shape,
            in_specs=[hbm] * len(operands) + [vmem] * len(small),
            scratch_shapes=[
                pltpu.VMEM((2, 3 * QUARTER, QUARTER), F32),
                pltpu.VMEM((4, rows_dev, 128), F32),
                pltpu.VMEM((5, 8, rows_dev), F32),
                *more,
                pltpu.SemaphoreType.DMA((len(operands),)),
                *[pltpu.VMEM(operand.shape, BF16) for operand in operands],
            ],
            compiler_params=PARAMS,
            cost_estimate=cost(squares * QUARTER * QUARTER * feature),
            name=name,
        )(*operands, *small)

    near = tiles(near_kernel, "near", 11, (own0, sib0), (meta, codes))
    tail = own0[2 * QUARTER :]
    low2, high2 = shift(tail, 2), shift(tail, -2)
    crossing = pl.pallas_call(
        cut_kernel,
        out_shape=sds((pools, 2 * QUARTER // pools, feature), BF16),
        in_specs=[vmem, hbm],
        compiler_params=PARAMS,
        name="cut",
    )(arrived, near)
    swapped = swap(crossing)
    low01 = pl.pallas_call(
        follow_kernel,
        out_shape=sds(low01.shape, BF16),
        in_specs=[vmem, hbm],
        compiler_params=PARAMS,
        name="follow",
    )(low01, near)
    lows01 = swap(low01)
    middle = tiles(
        middle_kernel, "middle", 42,
        (own0, arrived, high01, sib0, swapped, low01, lows01), (meta, codes, near),
    )
    late = tiles(
        late_kernel, "late", 14,
        (own0, high2, sib0, arrived, swapped, low2, low01, lows01, high01), (meta, codes, middle),
    )
    best = tiles(
        lambda *refs: last_kernel(pools, group, group * (places - last), group * last, *refs),
        "last", 2, (swap(low2), high01, high2, arrived), (meta, codes, late),
        out_shape=sds((devices, group * places), F32),
        more=(pltpu.VMEM((8, rows_dev), F32), pltpu.VMEM((group, rows_dev), F32)),
    )
    returned = lax.all_to_all(best, ("pool", "grp"), split_axis=0, concat_axis=0, tiled=True)
    scores = pl.pallas_call(
        lambda *refs: score_kernel(pools, group, places, *refs),
        out_shape=sds((1, rows_dev), F32),
        compiler_params=PARAMS,
        name="score",
    )(table, returned)
    return scores.reshape(rows_dev)


def cost(products):
    return pl.CostEstimate(flops=2 * products, bytes_accessed=0, transcendentals=0)


def solution(mesh):
    in_specs = (P(("pool", "grp"), None), P(), P(), P())
    out_specs = P(("pool", "grp"))
    return jax.shard_map(body, mesh=mesh, in_specs=in_specs, out_specs=out_specs, check_vma=False)
```

```python
import jax
import jax.numpy as jnp
from jax import lax
from jax.experimental import pallas as pl
from jax.experimental.pallas import tpu as pltpu
from jax.sharding import PartitionSpec as P

EPS = 1e-06
F32 = jnp.float32
BF16 = jnp.bfloat16
I32 = jnp.int32
QUARTER = 256
CODE = 8192
NT = (((1,), (1,)), ((), ()))
PARAMS = pltpu.CompilerParams(vmem_limit_bytes=20 * 1024 * 1024)
TABLE_PARAMS = pltpu.CompilerParams(vmem_limit_bytes=62 * 1024 * 1024)


def iota(shape, dim):
    return lax.broadcasted_iota(I32, shape, dim)


def normal_rows(rows):
    return (rows * lax.rsqrt(jnp.sum(rows * rows, axis=1, keepdims=True) + EPS)).astype(BF16)


def picked_rows(table, emb, first, count, pools):
    width = emb.shape[0]
    wanted = []
    for k in range(first, first + count):
        hit = table[:, k : k + 1] == iota((table.shape[0], width), 1)
        wanted.append(jnp.where(hit, 1.0, 0.0).reshape(pools, -1, width))
    choice = jnp.concatenate(wanted, axis=1).reshape(-1, width).astype(BF16)
    return normal_rows(jnp.dot(choice, emb, preferred_element_type=F32))


def table_kernel(
    pools, group, places, last, members_hbm, valid_hbm, emb_hbm, table_ref, main_ref,
    members_ref, valid_ref, emb_ref, found_ref, sems,
):
    copies = []
    for n, (source, target) in enumerate(
        ((members_hbm, members_ref), (valid_hbm, valid_ref), (emb_hbm, emb_ref))
    ):
        copies.append(pltpu.make_async_copy(source, target, sems.at[n]))
        copies[-1].start()
    rows_dev = emb_ref.shape[0]
    device = lax.axis_index("pool") * group + lax.axis_index("grp")
    blocks, block_len = members_ref.shape
    devices = blocks // 2
    before = jnp.where(
        iota((block_len, block_len), 0) < iota((block_len, block_len), 1), 1.0, 0.0
    ).astype(BF16)
    at = iota((blocks, blocks), 1) == iota((blocks, blocks), 0)
    copies[0].wait()
    copies[1].wait()
    live = jnp.sum(jnp.where(at, valid_ref[...], 0), axis=1, keepdims=True)
    local = members_ref[...] - device * rows_dev
    mine = (local >= 0) & (local < rows_dev) & (iota((blocks, block_len), 1) < live)
    ones = jnp.where(mine, 1.0, 0.0)
    counts = jnp.broadcast_to(jnp.sum(ones, axis=1, keepdims=True), (blocks, 128))
    counts = jnp.where(iota((blocks, 128), 0) % 2 == 1, pltpu.roll(counts, 1, 0), 0.0)
    rank = jnp.dot(ones.astype(BF16), before, preferred_element_type=F32) + counts[:, :1]
    rank = jnp.where(mine, rank, -1.0)
    value = (local + 1).astype(F32)
    lane = iota((blocks, 128), 1)
    found = jnp.zeros((blocks, 128), F32)
    for k in range(places):
        entry = jnp.sum(jnp.where(rank == k, value, 0.0), axis=1, keepdims=True)
        found = jnp.where(lane == k, entry, found)
    found_ref[...] = found
    pair = found_ref[pl.ds(0, devices, stride=2), :] + found_ref[pl.ds(1, devices, stride=2), :]
    table = pair.astype(I32) - 1
    table_ref[...] = table
    copies[2].wait()
    main_ref[...] = picked_rows(table, emb_ref[...], 0, places - last, pools)


def rest_kernel(pools, places, last, table_ref, emb_ref, after, out):
    del after
    out[...] = picked_rows(table_ref[...], emb_ref[...], places - last, last, pools)


def relatives():
    group = lax.axis_size("grp")
    index = lax.axis_index("grp")
    flip = 1 - 2 * (index % 2)
    below = (index + group - 2) % group
    return index, index + flip, below, below + flip, (index + 2) % group


def meta_kernel(
    group, places, last, members_hbm, valid_hbm, cluster_hbm, out_ref, codes_ref,
    members_ref, valid_ref, cluster_ref, packed_ref, sems,
):
    blocks = valid_ref.shape[1]
    block_len = members_ref.shape[1]
    pool = lax.axis_index("pool")
    first_block = pl.multiple_of(pool * 2 * group, 2 * group)
    copies = []
    for n, (source, target) in enumerate(
        (
            (members_hbm.at[pl.ds(first_block, 2 * group), :], members_ref),
            (valid_hbm, valid_ref),
            (cluster_hbm, cluster_ref),
        )
    ):
        copies.append(pltpu.make_async_copy(source, target, sems.at[n]))
        copies[-1].start()
    sources = blocks // 2
    slots = 2 * block_len
    width = group * places
    before = jnp.where(iota((slots, slots), 0) < iota((slots, slots), 1), 1.0, 0.0).astype(BF16)
    slot = iota((1, slots), 1)
    kind = iota((2 * width, slots), 0)
    kind_place = kind % width // group
    kind_owner = kind % group
    kind_value = jnp.where(kind < width, slot // 32, slot % 32 + 1)
    found = jnp.zeros((sources, 2 * width), F32)
    block_lane = iota((1, blocks), 1)
    lane = iota((1, width), 1)
    first_cluster = jnp.zeros((1, width), I32)
    second_cluster = jnp.zeros((1, width), I32)
    for copy in copies:
        copy.wait()
    for owner in range(group):
        halves, lives = [], []
        for half in range(2):
            halves.append(members_ref[2 * owner + half : 2 * owner + half + 1, :])
            at = block_lane == first_block + 2 * owner + half
            lives.append(jnp.sum(jnp.where(at, valid_ref[...], 0), axis=1, keepdims=True))
            cluster = jnp.sum(jnp.where(at, cluster_ref[...], 0), axis=1, keepdims=True)
            if half == 0:
                first_cluster = jnp.where(lane % group == owner, cluster, first_cluster)
            else:
                second_cluster = jnp.where(lane % group == owner, cluster, second_cluster)
        rows = jnp.concatenate(halves, axis=1)
        end = jnp.where(slot < block_len, lives[0], block_len + lives[1])
        origin = jnp.where(slot < end, rows // slots, -1)
        match = iota((sources, slots), 0) == origin
        ones = jnp.where(match, 1.0, 0.0).astype(BF16)
        ranks = jnp.dot(ones, before, preferred_element_type=F32)
        rank = jnp.sum(jnp.where(match, ranks, 0.0), axis=0, keepdims=True).astype(I32)
        weight = jnp.where((kind_owner == owner) & (kind_place == rank), kind_value, 0)
        found = found + lax.dot_general(
            ones, weight.astype(F32).astype(BF16), NT, preferred_element_type=F32
        )
    found = found.astype(I32)
    place = found[:, :width] * 32 + found[:, width:] - 1
    filled = found[:, width:] > 0
    position = jnp.where(filled, place + lane % group * slots, -1)
    cluster = jnp.where(filled, jnp.where(place < block_len, first_cluster, second_cluster), -1)
    main = (places - last) * group
    rest = last * group
    pools = sources // group
    for n, values in enumerate((position, cluster)):
        for p in range(pools):
            own = values[p * group : (p + 1) * group, :]
            out_ref[n, :, p * main : (p + 1) * main] = own[:, :main]
            at = pools * main + p * rest
            out_ref[n, :, at : at + rest] = own[:, main:]
    packed_ref[...] = jnp.zeros(packed_ref.shape, I32)
    for n, cls in enumerate(relatives()[:4]):
        pos = out_ref[0, pl.ds(cls, 1), :]
        cluster = out_ref[1, pl.ds(cls, 1), :]
        packed_ref[n : n + 1, :] = jnp.where(cluster < 0, -2 * CODE, cluster * CODE + pos)
    codes_ref[...] = jnp.transpose(packed_ref[...])


def run(pieces, sims_ref):
    for n in range(len(pieces) + 1):
        if n < len(pieces):
            piece = pieces[n]
            sims_ref[n % 2, : piece["count"], :] = lax.dot_general(
                piece["left"](), piece["right"](), NT, preferred_element_type=F32
            )
        if n > 0:
            take_maxima(sims_ref.at[(n - 1) % 2], **pieces[n - 1])


def take_maxima(sims_ref, left, right, count, codes, cls, rows, start, pos_row, cluster_row, col, col_start, same):
    step = 128
    right_pos, right_cluster = pos_row(), cluster_row()
    parts = QUARTER // 128
    best_col = [jnp.zeros((8, 128), F32) for _ in range(parts)]
    for top in range(0, count, step):
        code = codes[start + top : start + top + step, cls : cls + 1]
        code = jnp.broadcast_to(code, (step, 128))
        pos = code & (CODE - 1)
        cluster = code >> 13
        best = rows[start + top : start + top + step, :]
        for part in range(parts):
            lanes = slice(part * 128, part * 128 + 128)
            sims = sims_ref[top : top + step, lanes]
            sims = jnp.where(cluster == right_cluster[:, lanes], sims, 0.0)
            earlier = right_pos[:, lanes] < pos
            best = jnp.maximum(best, jnp.where(earlier, sims, 0.0))
            if top < same:
                later = jnp.where(earlier, 0.0, sims)
                best_col[part] = jnp.maximum(
                    best_col[part], jnp.max(later.reshape(-1, 8, 128), axis=0)
                )
        rows[start + top : start + top + step, :] = best
    if same > 0:
        for part in range(parts):
            lanes = slice(col_start + part * 128, col_start + part * 128 + 128)
            col[:, lanes] = jnp.maximum(col[:, lanes], best_col[part])


def row_result(row_ref):
    return jnp.max(jnp.transpose(row_ref[...]), axis=0, keepdims=True)


def col_result(col_ref):
    return jnp.max(col_ref[...], axis=0, keepdims=True)


OWN, SIB, LOW, LOWS, HIGH = range(5)


class Fetch:
    def __init__(self, sources, held, sems):
        self.held, self.copies = dict(), dict()
        for n, source in enumerate(sources):
            copy = pltpu.make_async_copy(source, held[n], sems.at[n])
            copy.start()
            self.held[n], self.copies[n] = held[n], copy

    def get(self, n):
        copy = self.copies.pop(n, None)
        if copy is not None:
            copy.wait()
        return self.held[n]

    def all(self):
        for n in list(self.copies):
            self.get(n)


class Tiles:
    def __init__(self, fetch, meta, codes, rows, cols, parts):
        self.fetch, self.parts = fetch, parts
        self.meta, self.codes, self.rows, self.cols = meta, codes, rows, cols
        self.relatives = relatives()
        for ref in (rows, cols):
            ref[...] = jnp.zeros(ref.shape, F32)

    def load(self, cls, quarter, count=1):
        number, at = self.parts[cls, quarter]
        ref = self.fetch.get(number)
        if len(ref.shape) == 3:
            return ref[:, at : at + QUARTER // ref.shape[0], :].reshape(-1, ref.shape[2])
        return ref[at : at + count * QUARTER, :]

    def piece(self, left, quarter, count, right, right_quarter, same=None):
        lanes = slice(right_quarter * QUARTER, (right_quarter + 1) * QUARTER)
        place = self.relatives[right]
        return dict(
            left=lambda: self.load(left, quarter, count),
            right=lambda: self.load(right, right_quarter),
            count=count * QUARTER,
            codes=self.codes,
            cls=left,
            rows=self.rows.at[left],
            start=quarter * QUARTER,
            pos_row=lambda: self.meta[0, pl.ds(place, 1), lanes],
            cluster_row=lambda: self.meta[1, pl.ds(place, 1), lanes],
            col=self.cols.at[right],
            col_start=right_quarter * QUARTER,
            same=count * QUARTER if same is None else same,
        )

    def matched(self, flip, left, right, pairs):
        return [
            self.piece(left, a, 1, right, b) for a, b in pairs if (a + b) % 2 == flip
        ]

    def finish(self, before, out):
        for cls in range(5):
            best = col_result(self.cols.at[cls])
            if cls < HIGH:
                best = jnp.maximum(best, row_result(self.rows.at[cls]))
            if before is not None:
                best = jnp.maximum(best, before[cls : cls + 1, :])
            out[cls : cls + 1, :] = best


def either(flag, work):
    pl.when(flag)(lambda: work(1))
    pl.when(jnp.logical_not(flag))(lambda: work(0))


def second_core():
    return lax.axis_index("grp") % 2 == 1


def outer_chip():
    chip = lax.axis_index("grp") // 2
    return (chip == 0) | (chip == 3)


def parts_of(**groups):
    names = dict(own=OWN, sib=SIB, low=LOW, lows=LOWS, high=HIGH)
    return {(names[name], q): part for name, parts in groups.items() for q, part in parts.items()}


def whole(n):
    return {q: (n, q * QUARTER) for q in range(3)}


def join_kernel(pools, rest, low_rest, high_rest, out):
    width = QUARTER // pools
    for n, part in enumerate((rest, low_rest, high_rest)):
        out[:, n * width : (n + 1) * width, :] = part[...].reshape(pools, width, -1)


def cut_kernel(arrived, after, out):
    del after
    out[...] = arrived[:, : out.shape[1], :]


def follow_kernel(rows, after, also_after, out):
    del after, also_after
    out[...] = rows[...]


def near_kernel(own0, sib0, meta, codes, out, sims, rows, cols, sems, *held):
    fetch = Fetch((own0, sib0), held, sems)
    tiles = Tiles(fetch, meta, codes, rows, cols, parts_of(own=whole(0), sib=whole(1)))
    run([tiles.piece(OWN, 0, b + 1, OWN, b, same=b * QUARTER) for b in range(3)], sims)
    fetch.all()
    pairs = [(a, b) for b in range(3) for a in range(3)]
    either(second_core(), lambda flip: run(tiles.matched(flip, OWN, SIB, pairs), sims))
    tiles.finish(None, out)


def early_kernel(
    own0, arrived, sib0, swapped, meta, codes, before, out, sims, rows, cols, sems, *held
):
    fetch = Fetch((own0, arrived, sib0, swapped), held, sems)
    width = arrived.shape[1] // 3
    tiles = Tiles(
        fetch, meta, codes, rows, cols,
        parts_of(
            own={**whole(0), 3: (1, 0)},
            sib={**whole(2), 3: (3, 0)},
            low={3: (1, width)},
            lows={3: (3, width)},
            high={3: (1, 2 * width)},
        ),
    )
    pieces = [tiles.piece(OWN, 0, 3, OWN, 3), tiles.piece(OWN, 3, 1, OWN, 3, same=0)]
    for cls in (OWN, SIB):
        pieces.append(tiles.piece(cls, 0, 3, HIGH, 3))
        pieces.append(tiles.piece(cls, 3, 1, HIGH, 3))
    run(pieces, sims)
    fetch.all()
    pairs = [(a, b) for b in range(4) for a in range(4) if 3 in (a, b)]
    either(second_core(), lambda flip: run(tiles.matched(flip, OWN, SIB, pairs), sims))
    both = [tiles.piece(cls, 3, 1, HIGH, 3) for cls in (LOW, LOWS)]
    pl.when(jnp.logical_not(outer_chip()))(lambda: run(both, sims))
    tiles.finish(before, out)


def late_kernel(
    own0, high0, sib0, arrived, swapped, low0, meta, codes, before, out,
    sims, rows, cols, sems, *held,
):
    fetch = Fetch((own0, high0, sib0, arrived, swapped, low0), held, sems)
    width = arrived.shape[1] // 3
    tiles = Tiles(
        fetch, meta, codes, rows, cols,
        parts_of(
            own={**whole(0), 3: (3, 0)},
            sib={**whole(2), 3: (4, 0)},
            low={**whole(5), 3: (3, width)},
            lows={3: (4, width)},
            high={**whole(1), 3: (3, 2 * width)},
        ),
    )
    pieces = [tiles.piece(cls, 0, 3, HIGH, b) for cls in (OWN, SIB) for b in range(3)]
    pieces += [tiles.piece(cls, 3, 1, HIGH, b) for cls in (OWN, SIB) for b in range(3)]
    run(pieces, sims)
    fetch.all()
    pairs = [(a, b) for b in range(4) for a in range(4) if (a, b) != (3, 3)]
    others = [(3, b) for b in range(3)]
    either(
        outer_chip(),
        lambda flip: run(
            tiles.matched(flip, LOW, HIGH, pairs) + tiles.matched(flip, LOWS, HIGH, others), sims
        ),
    )
    tiles.finish(before, out)


def last_kernel(
    pools, group, main, rest, lows0, high0, arrived, meta, codes, before, out,
    sims, rows, cols, best, every, sems, *held,
):
    fetch = Fetch((lows0, high0, arrived), held, sems)
    width = arrived.shape[1] // 3
    tiles = Tiles(
        fetch, meta, codes, rows, cols,
        parts_of(lows=whole(0), high={**whole(1), 3: (2, 2 * width)}),
    )
    fetch.all()
    pairs = [(a, b) for b in range(4) for a in range(3)]
    either(outer_chip(), lambda flip: run(tiles.matched(flip, LOWS, HIGH, pairs), sims))
    best[...] = before[...]
    best[LOWS : LOWS + 1, :] = jnp.maximum(best[LOWS : LOWS + 1, :], row_result(rows.at[LOWS]))
    best[HIGH : HIGH + 1, :] = jnp.maximum(best[HIGH : HIGH + 1, :], col_result(cols.at[HIGH]))
    every[...] = jnp.zeros(every.shape, F32)
    for cls, place in enumerate(tiles.relatives):
        every[pl.ds(place, 1), :] = best[cls : cls + 1, :]
    for p in range(pools):
        rows_out = slice(p * group, (p + 1) * group)
        out[rows_out, :main] = every[:, p * main : (p + 1) * main]
        at = pools * main + p * rest
        out[rows_out, main:] = every[:, at : at + rest]


def score_kernel(pools, group, places, table_ref, returned_ref, out_ref):
    rows_dev = out_ref.shape[1]
    arrived = jnp.transpose(
        jnp.concatenate([returned_ref[...], jnp.zeros_like(returned_ref)], axis=1)
    )
    table = table_ref[...]
    row = iota((8, rows_dev), 1)
    total = jnp.zeros((8, rows_dev), F32)
    for p in range(pools):
        for k in range(places):
            value = jnp.max(
                arrived[k * group : (k + 1) * group, p * group : (p + 1) * group],
                axis=1,
                keepdims=True,
            )
            entry = table[p * group : (p + 1) * group, k : k + 1]
            total = jnp.where(entry == row, value, total)
    out_ref[...] = jnp.sum(total, axis=0, keepdims=True)


def body(embeddings, members, valid, block_cluster):
    rows_dev, feature = embeddings.shape
    pools = lax.axis_size("pool")
    group = lax.axis_size("grp")
    devices = pools * group
    places = rows_dev // devices
    last = places // 4
    sds = jax.ShapeDtypeStruct
    hbm = pl.BlockSpec(memory_space=pltpu.HBM)
    valid_row = valid.reshape(1, -1)
    cluster_row = block_cluster.reshape(1, -1)
    blocks, block_len = members.shape

    table, main = pl.pallas_call(
        lambda *refs: table_kernel(pools, group, places, last, *refs),
        out_shape=(
            sds((devices, 128), I32),
            sds((3 * QUARTER, feature), BF16),
        ),
        in_specs=[hbm] * 3,
        scratch_shapes=[
            pltpu.VMEM((blocks, block_len), I32),
            pltpu.VMEM((1, blocks), I32),
            pltpu.VMEM((rows_dev, feature), BF16),
            pltpu.VMEM((blocks, 128), F32),
            pltpu.SemaphoreType.DMA((3,)),
        ],
        compiler_params=TABLE_PARAMS,
        cost_estimate=cost(rows_dev * rows_dev * feature),
        name="table",
    )(members, valid_row, embeddings)
    meta, codes = pl.pallas_call(
        lambda *refs: meta_kernel(group, places, last, *refs),
        out_shape=(sds((2, group, rows_dev), I32), sds((rows_dev, 128), I32)),
        in_specs=[hbm] * 3,
        scratch_shapes=[
            pltpu.VMEM((2 * group, block_len), I32),
            pltpu.VMEM((1, blocks), I32),
            pltpu.VMEM((1, blocks), I32),
            pltpu.VMEM((128, rows_dev), I32),
            pltpu.SemaphoreType.DMA((3,)),
        ],
        compiler_params=PARAMS,
        cost_estimate=cost(2 * rows_dev**3),
        name="meta",
    )(members, valid_row, cluster_row)

    def shift(rows, by):
        return lax.ppermute(rows, "grp", [(g, (g + by) % group) for g in range(group)])

    def swap(rows):
        return lax.ppermute(rows, "grp", [(g, g ^ 1) for g in range(group)])

    def to_pools(rows):
        return lax.all_to_all(rows, "pool", split_axis=0, concat_axis=0, tiled=True)

    vmem = pl.BlockSpec(memory_space=pltpu.VMEM)
    rest = pl.pallas_call(
        lambda *refs: rest_kernel(pools, places, last, *refs),
        out_shape=sds((QUARTER, feature), BF16),
        in_specs=[vmem, vmem, hbm],
        compiler_params=PARAMS,
        name="rest",
    )(table, embeddings, meta)
    low_rest, high_rest = shift(rest, 2), shift(rest, -2)
    own0 = to_pools(main.reshape(pools, -1, feature)).reshape(-1, feature)
    sent = pl.pallas_call(
        lambda *refs: join_kernel(pools, *refs),
        out_shape=sds((pools, 3 * QUARTER // pools, feature), BF16),
        compiler_params=PARAMS,
        name="join",
    )(rest, low_rest, high_rest)
    arrived = to_pools(sent)
    low0, high0 = shift(own0, 2), shift(own0, -2)
    sib0 = swap(own0)

    def tiles(kernel, name, squares, operands, small, out_shape=sds((8, rows_dev), F32), more=()):
        return pl.pallas_call(
            kernel,
            out_shape=out_shape,
            in_specs=[hbm] * len(operands) + [vmem] * len(small),
            scratch_shapes=[
                pltpu.VMEM((2, 3 * QUARTER, QUARTER), F32),
                pltpu.VMEM((4, rows_dev, 128), F32),
                pltpu.VMEM((5, 8, rows_dev), F32),
                *more,
                pltpu.SemaphoreType.DMA((len(operands),)),
                *[pltpu.VMEM(operand.shape, BF16) for operand in operands],
            ],
            compiler_params=PARAMS,
            cost_estimate=cost(squares * QUARTER * QUARTER * feature),
            name=name,
        )(*operands, *small)

    near = tiles(near_kernel, "near", 11, (own0, sib0), (meta, codes))
    crossing = pl.pallas_call(
        cut_kernel,
        out_shape=sds((pools, 2 * QUARTER // pools, feature), BF16),
        in_specs=[vmem, hbm],
        compiler_params=PARAMS,
        name="cut",
    )(arrived, near)
    swapped = swap(crossing)
    early = tiles(
        early_kernel, "early", 16, (own0, arrived, sib0, swapped), (meta, codes, near)
    )
    lows0 = swap(
        pl.pallas_call(
            follow_kernel,
            out_shape=sds(low0.shape, BF16),
            in_specs=[vmem, hbm, hbm],
            compiler_params=PARAMS,
            name="follow",
        )(low0, high0, early)
    )
    late = tiles(
        late_kernel, "late", 32, (own0, high0, sib0, arrived, swapped, low0), (meta, codes, early)
    )
    best = tiles(
        lambda *refs: last_kernel(pools, group, group * (places - last), group * last, *refs),
        "last", 6, (lows0, high0, arrived), (meta, codes, late),
        out_shape=sds((devices, group * places), F32),
        more=(pltpu.VMEM((8, rows_dev), F32), pltpu.VMEM((group, rows_dev), F32)),
    )
    returned = lax.all_to_all(best, ("pool", "grp"), split_axis=0, concat_axis=0, tiled=True)
    scores = pl.pallas_call(
        lambda *refs: score_kernel(pools, group, places, *refs),
        out_shape=sds((1, rows_dev), F32),
        compiler_params=PARAMS,
        name="score",
    )(table, returned)
    return scores.reshape(rows_dev)


def cost(products):
    return pl.CostEstimate(flops=2 * products, bytes_accessed=0, transcendentals=0)


def solution(mesh):
    in_specs = (P(("pool", "grp"), None), P(), P(), P())
    out_specs = P(("pool", "grp"))
    return jax.shard_map(body, mesh=mesh, in_specs=in_specs, out_specs=out_specs, check_vma=False)
```

```python
import jax
import jax.numpy as jnp
from jax import lax
from jax.experimental import pallas as pl
from jax.experimental.pallas import tpu as pltpu
from jax.sharding import PartitionSpec as P

EPS = 1e-06
F32 = jnp.float32
BF16 = jnp.bfloat16
I32 = jnp.int32
QUARTER = 256
CODE = 8192
NT = (((1,), (1,)), ((), ()))
PARAMS = pltpu.CompilerParams(vmem_limit_bytes=20 * 1024 * 1024)
TABLE_PARAMS = pltpu.CompilerParams(vmem_limit_bytes=62 * 1024 * 1024)


def iota(shape, dim):
    return lax.broadcasted_iota(I32, shape, dim)


def normal_rows(rows):
    return (rows * lax.rsqrt(jnp.sum(rows * rows, axis=1, keepdims=True) + EPS)).astype(BF16)


def picked_rows(table, emb, first, count, pools):
    width = emb.shape[0]
    wanted = []
    for k in range(first, first + count):
        hit = table[:, k : k + 1] == iota((table.shape[0], width), 1)
        wanted.append(jnp.where(hit, 1.0, 0.0).reshape(pools, -1, width))
    choice = jnp.concatenate(wanted, axis=1).reshape(-1, width).astype(BF16)
    return normal_rows(jnp.dot(choice, emb, preferred_element_type=F32))


def table_kernel(
    pools, group, places, last, members_hbm, valid_hbm, emb_hbm, table_ref, main_ref,
    members_ref, valid_ref, emb_ref, found_ref, sems,
):
    copies = []
    for n, (source, target) in enumerate(
        ((members_hbm, members_ref), (valid_hbm, valid_ref), (emb_hbm, emb_ref))
    ):
        copies.append(pltpu.make_async_copy(source, target, sems.at[n]))
        copies[-1].start()
    rows_dev = emb_ref.shape[0]
    device = lax.axis_index("pool") * group + lax.axis_index("grp")
    blocks, block_len = members_ref.shape
    devices = blocks // 2
    before = jnp.where(
        iota((block_len, block_len), 0) < iota((block_len, block_len), 1), 1.0, 0.0
    ).astype(BF16)
    at = iota((blocks, blocks), 1) == iota((blocks, blocks), 0)
    copies[0].wait()
    copies[1].wait()
    live = jnp.sum(jnp.where(at, valid_ref[...], 0), axis=1, keepdims=True)
    local = members_ref[...] - device * rows_dev
    mine = (local >= 0) & (local < rows_dev) & (iota((blocks, block_len), 1) < live)
    ones = jnp.where(mine, 1.0, 0.0)
    counts = jnp.broadcast_to(jnp.sum(ones, axis=1, keepdims=True), (blocks, 128))
    counts = jnp.where(iota((blocks, 128), 0) % 2 == 1, pltpu.roll(counts, 1, 0), 0.0)
    rank = jnp.dot(ones.astype(BF16), before, preferred_element_type=F32) + counts[:, :1]
    rank = jnp.where(mine, rank, -1.0)
    value = (local + 1).astype(F32)
    lane = iota((blocks, 128), 1)
    found = jnp.zeros((blocks, 128), F32)
    for k in range(places):
        entry = jnp.sum(jnp.where(rank == k, value, 0.0), axis=1, keepdims=True)
        found = jnp.where(lane == k, entry, found)
    found_ref[...] = found
    pair = found_ref[pl.ds(0, devices, stride=2), :] + found_ref[pl.ds(1, devices, stride=2), :]
    table = pair.astype(I32) - 1
    table_ref[...] = table
    copies[2].wait()
    main_ref[...] = picked_rows(table, emb_ref[...], 0, places - last, pools)


def rest_kernel(pools, places, last, table_ref, emb_ref, after, out):
    del after
    out[...] = picked_rows(table_ref[...], emb_ref[...], places - last, last, pools)


def relatives():
    group = lax.axis_size("grp")
    index = lax.axis_index("grp")
    flip = 1 - 2 * (index % 2)
    below = (index + group - 2) % group
    return index, index + flip, below, below + flip, (index + 2) % group


def meta_kernel(
    group, places, last, members_hbm, valid_hbm, cluster_hbm, out_ref, codes_ref,
    members_ref, valid_ref, cluster_ref, packed_ref, sems,
):
    blocks = valid_ref.shape[1]
    block_len = members_ref.shape[1]
    pool = lax.axis_index("pool")
    first_block = pl.multiple_of(pool * 2 * group, 2 * group)
    copies = []
    for n, (source, target) in enumerate(
        (
            (members_hbm.at[pl.ds(first_block, 2 * group), :], members_ref),
            (valid_hbm, valid_ref),
            (cluster_hbm, cluster_ref),
        )
    ):
        copies.append(pltpu.make_async_copy(source, target, sems.at[n]))
        copies[-1].start()
    sources = blocks // 2
    slots = 2 * block_len
    width = group * places
    before = jnp.where(iota((slots, slots), 0) < iota((slots, slots), 1), 1.0, 0.0).astype(BF16)
    slot = iota((1, slots), 1)
    kind = iota((2 * width, slots), 0)
    kind_place = kind % width // group
    kind_owner = kind % group
    kind_value = jnp.where(kind < width, slot // 32, slot % 32 + 1)
    found = jnp.zeros((sources, 2 * width), F32)
    block_lane = iota((1, blocks), 1)
    lane = iota((1, width), 1)
    first_cluster = jnp.zeros((1, width), I32)
    second_cluster = jnp.zeros((1, width), I32)
    for copy in copies:
        copy.wait()
    for owner in range(group):
        halves, lives = [], []
        for half in range(2):
            halves.append(members_ref[2 * owner + half : 2 * owner + half + 1, :])
            at = block_lane == first_block + 2 * owner + half
            lives.append(jnp.sum(jnp.where(at, valid_ref[...], 0), axis=1, keepdims=True))
            cluster = jnp.sum(jnp.where(at, cluster_ref[...], 0), axis=1, keepdims=True)
            if half == 0:
                first_cluster = jnp.where(lane % group == owner, cluster, first_cluster)
            else:
                second_cluster = jnp.where(lane % group == owner, cluster, second_cluster)
        rows = jnp.concatenate(halves, axis=1)
        end = jnp.where(slot < block_len, lives[0], block_len + lives[1])
        origin = jnp.where(slot < end, rows // slots, -1)
        match = iota((sources, slots), 0) == origin
        ones = jnp.where(match, 1.0, 0.0).astype(BF16)
        ranks = jnp.dot(ones, before, preferred_element_type=F32)
        rank = jnp.sum(jnp.where(match, ranks, 0.0), axis=0, keepdims=True).astype(I32)
        weight = jnp.where((kind_owner == owner) & (kind_place == rank), kind_value, 0)
        found = found + lax.dot_general(
            ones, weight.astype(F32).astype(BF16), NT, preferred_element_type=F32
        )
    found = found.astype(I32)
    place = found[:, :width] * 32 + found[:, width:] - 1
    filled = found[:, width:] > 0
    position = jnp.where(filled, place + lane % group * slots, -1)
    cluster = jnp.where(filled, jnp.where(place < block_len, first_cluster, second_cluster), -1)
    main = (places - last) * group
    rest = last * group
    pools = sources // group
    for n, values in enumerate((position, cluster)):
        for p in range(pools):
            own = values[p * group : (p + 1) * group, :]
            out_ref[n, :, p * main : (p + 1) * main] = own[:, :main]
            at = pools * main + p * rest
            out_ref[n, :, at : at + rest] = own[:, main:]
    packed_ref[...] = jnp.zeros(packed_ref.shape, I32)
    for n, cls in enumerate(relatives()[:4]):
        pos = out_ref[0, pl.ds(cls, 1), :]
        cluster = out_ref[1, pl.ds(cls, 1), :]
        packed_ref[n : n + 1, :] = jnp.where(cluster < 0, -2 * CODE, cluster * CODE + pos)
    codes_ref[...] = jnp.transpose(packed_ref[...])


def run(pieces, sims_ref, fetch=None):
    for n in range(len(pieces) + 1):
        if n == 1 and fetch is not None:
            fetch.rest()
        if n < len(pieces):
            piece = pieces[n]
            sims_ref[n % 2, : piece["count"], :] = lax.dot_general(
                piece["left"](), piece["right"](), NT, preferred_element_type=F32
            )
        if n > 0:
            take_maxima(sims_ref.at[(n - 1) % 2], **pieces[n - 1])


def take_maxima(sims_ref, left, right, count, codes, cls, rows, start, pos_row, cluster_row, col, col_start, same):
    step = 128
    right_pos, right_cluster = pos_row(), cluster_row()
    parts = QUARTER // 128
    best_col = [jnp.zeros((8, 128), F32) for _ in range(parts)]
    for top in range(0, count, step):
        code = codes[start + top : start + top + step, cls : cls + 1]
        code = jnp.broadcast_to(code, (step, 128))
        pos = code & (CODE - 1)
        cluster = code >> 13
        best = rows[start + top : start + top + step, :]
        for part in range(parts):
            lanes = slice(part * 128, part * 128 + 128)
            sims = sims_ref[top : top + step, lanes]
            sims = jnp.where(cluster == right_cluster[:, lanes], sims, 0.0)
            earlier = right_pos[:, lanes] < pos
            best = jnp.maximum(best, jnp.where(earlier, sims, 0.0))
            if top < same:
                later = jnp.where(earlier, 0.0, sims)
                best_col[part] = jnp.maximum(
                    best_col[part], jnp.max(later.reshape(-1, 8, 128), axis=0)
                )
        rows[start + top : start + top + step, :] = best
    if same > 0:
        for part in range(parts):
            lanes = slice(col_start + part * 128, col_start + part * 128 + 128)
            col[:, lanes] = jnp.maximum(col[:, lanes], best_col[part])


def row_result(row_ref):
    return jnp.max(jnp.transpose(row_ref[...]), axis=0, keepdims=True)


def col_result(col_ref):
    return jnp.max(col_ref[...], axis=0, keepdims=True)


OWN, SIB, LOW, LOWS, HIGH = range(5)


class Fetch:
    def __init__(self, sources, held, sems, first):
        self.copies, self.held, self.waited = [], held, set()
        for n, source in enumerate(sources):
            self.copies.append(pltpu.make_async_copy(source, held[n], sems.at[n]))
        for copy in self.copies[:first]:
            copy.start()
        self.late = self.copies[first:]

    def get(self, n):
        if n not in self.waited:
            self.copies[n].wait()
            self.waited.add(n)
        return self.held[n]

    def rest(self):
        for copy in self.late:
            copy.start()
        self.late = []

    def all(self):
        for n in range(len(self.copies)):
            self.get(n)


class Tiles:
    def __init__(self, fetch, meta, codes, rows, cols, parts):
        self.fetch, self.parts = fetch, parts
        self.meta, self.codes, self.rows, self.cols = meta, codes, rows, cols
        self.relatives = relatives()
        for ref in (rows, cols):
            ref[...] = jnp.zeros(ref.shape, F32)

    def load(self, cls, quarter, count=1):
        number, at = self.parts[cls, quarter]
        ref = self.fetch.get(number)
        if len(ref.shape) == 3:
            return ref[:, at : at + QUARTER // ref.shape[0], :].reshape(-1, ref.shape[2])
        return ref[at : at + count * QUARTER, :]

    def piece(self, left, quarter, count, right, right_quarter, same=None):
        lanes = slice(right_quarter * QUARTER, (right_quarter + 1) * QUARTER)
        place = self.relatives[right]
        return dict(
            left=lambda: self.load(left, quarter, count),
            right=lambda: self.load(right, right_quarter),
            count=count * QUARTER,
            codes=self.codes,
            cls=left,
            rows=self.rows.at[left],
            start=quarter * QUARTER,
            pos_row=lambda: self.meta[0, pl.ds(place, 1), lanes],
            cluster_row=lambda: self.meta[1, pl.ds(place, 1), lanes],
            col=self.cols.at[right],
            col_start=right_quarter * QUARTER,
            same=count * QUARTER if same is None else same,
        )

    def matched(self, flip, left, right, pairs):
        return [
            self.piece(left, a, 1, right, b) for a, b in pairs if (a + b) % 2 == flip
        ]

    def finish(self, before, out):
        for cls in range(5):
            best = col_result(self.cols.at[cls])
            if cls < HIGH:
                best = jnp.maximum(best, row_result(self.rows.at[cls]))
            if before is not None:
                best = jnp.maximum(best, before[cls : cls + 1, :])
            out[cls : cls + 1, :] = best


def either(flag, work):
    pl.when(flag)(lambda: work(1))
    pl.when(jnp.logical_not(flag))(lambda: work(0))


def second_core():
    return lax.axis_index("grp") % 2 == 1


def outer_chip():
    chip = lax.axis_index("grp") // 2
    return (chip == 0) | (chip == 3)


def parts_of(**groups):
    names = dict(own=OWN, sib=SIB, low=LOW, lows=LOWS, high=HIGH)
    return {(names[name], q): part for name, parts in groups.items() for q, part in parts.items()}


def whole(n):
    return {q: (n, q * QUARTER) for q in range(3)}


def join_kernel(pools, rest, low_rest, high_rest, out):
    width = QUARTER // pools
    for n, part in enumerate((rest, low_rest, high_rest)):
        out[:, n * width : (n + 1) * width, :] = part[...].reshape(pools, width, -1)


def follow_kernel(rows, after, also_after, out):
    del rows, after, also_after, out


def early_kernel(own0, sib0, arrived, swapped, meta, codes, out, sims, rows, cols, sems, *held):
    fetch = Fetch((own0, sib0, arrived, swapped), held, sems, 1)
    width = arrived.shape[1] // 3
    tiles = Tiles(
        fetch, meta, codes, rows, cols,
        parts_of(
            own={**whole(0), 3: (2, 0)},
            sib={**whole(1), 3: (3, 0)},
            low={3: (2, width)},
            lows={3: (3, width)},
            high={3: (2, 2 * width)},
        ),
    )
    pieces = [tiles.piece(OWN, 0, b + 1, OWN, b, same=b * QUARTER) for b in range(3)]
    pieces += [tiles.piece(OWN, 0, 3, OWN, 3), tiles.piece(OWN, 3, 1, OWN, 3, same=0)]
    for cls in (OWN, SIB):
        pieces.append(tiles.piece(cls, 0, 3, HIGH, 3))
        pieces.append(tiles.piece(cls, 3, 1, HIGH, 3))
    run(pieces, sims, fetch)
    fetch.all()
    pairs = [(a, b) for b in range(4) for a in range(4)]
    either(second_core(), lambda flip: run(tiles.matched(flip, OWN, SIB, pairs), sims))
    both = [tiles.piece(cls, 3, 1, HIGH, 3) for cls in (LOW, LOWS)]
    pl.when(jnp.logical_not(outer_chip()))(lambda: run(both, sims))
    tiles.finish(None, out)


def late_kernel(
    own0, high0, sib0, arrived, swapped, low0, meta, codes, before, out,
    sims, rows, cols, sems, *held,
):
    fetch = Fetch((own0, high0, sib0, arrived, swapped, low0), held, sems, 2)
    width = arrived.shape[1] // 3
    tiles = Tiles(
        fetch, meta, codes, rows, cols,
        parts_of(
            own={**whole(0), 3: (3, 0)},
            sib={**whole(2), 3: (4, 0)},
            low={**whole(5), 3: (3, width)},
            lows={3: (4, width)},
            high={**whole(1), 3: (3, 2 * width)},
        ),
    )
    pieces = [tiles.piece(cls, 0, 3, HIGH, b) for cls in (OWN, SIB) for b in range(3)]
    pieces += [tiles.piece(cls, 3, 1, HIGH, b) for cls in (OWN, SIB) for b in range(3)]
    run(pieces, sims, fetch)
    fetch.all()
    pairs = [(a, b) for b in range(4) for a in range(4) if (a, b) != (3, 3)]
    others = [(3, b) for b in range(3)]
    either(
        outer_chip(),
        lambda flip: run(
            tiles.matched(flip, LOW, HIGH, pairs) + tiles.matched(flip, LOWS, HIGH, others), sims
        ),
    )
    tiles.finish(before, out)


def last_kernel(
    pools, group, main, rest, lows0, high0, arrived, meta, codes, before, out,
    sims, rows, cols, best, every, sems, *held,
):
    fetch = Fetch((lows0, high0, arrived), held, sems, 3)
    width = arrived.shape[1] // 3
    tiles = Tiles(
        fetch, meta, codes, rows, cols,
        parts_of(lows=whole(0), high={**whole(1), 3: (2, 2 * width)}),
    )
    fetch.all()
    pairs = [(a, b) for b in range(4) for a in range(3)]
    either(outer_chip(), lambda flip: run(tiles.matched(flip, LOWS, HIGH, pairs), sims))
    best[...] = before[...]
    best[LOWS : LOWS + 1, :] = jnp.maximum(best[LOWS : LOWS + 1, :], row_result(rows.at[LOWS]))
    best[HIGH : HIGH + 1, :] = jnp.maximum(best[HIGH : HIGH + 1, :], col_result(cols.at[HIGH]))
    every[...] = jnp.zeros(every.shape, F32)
    for cls, place in enumerate(tiles.relatives):
        every[pl.ds(place, 1), :] = best[cls : cls + 1, :]
    for p in range(pools):
        rows_out = slice(p * group, (p + 1) * group)
        out[rows_out, :main] = every[:, p * main : (p + 1) * main]
        at = pools * main + p * rest
        out[rows_out, main:] = every[:, at : at + rest]


def score_kernel(pools, group, places, table_ref, returned_ref, out_ref):
    rows_dev = out_ref.shape[1]
    arrived = jnp.transpose(
        jnp.concatenate([returned_ref[...], jnp.zeros_like(returned_ref)], axis=1)
    )
    table = table_ref[...]
    row = iota((8, rows_dev), 1)
    total = jnp.zeros((8, rows_dev), F32)
    for p in range(pools):
        for k in range(places):
            value = jnp.max(
                arrived[k * group : (k + 1) * group, p * group : (p + 1) * group],
                axis=1,
                keepdims=True,
            )
            entry = table[p * group : (p + 1) * group, k : k + 1]
            total = jnp.where(entry == row, value, total)
    out_ref[...] = jnp.sum(total, axis=0, keepdims=True)


def body(embeddings, members, valid, block_cluster):
    rows_dev, feature = embeddings.shape
    pools = lax.axis_size("pool")
    group = lax.axis_size("grp")
    devices = pools * group
    places = rows_dev // devices
    last = places // 4
    sds = jax.ShapeDtypeStruct
    hbm = pl.BlockSpec(memory_space=pltpu.HBM)
    valid_row = valid.reshape(1, -1)
    cluster_row = block_cluster.reshape(1, -1)
    blocks, block_len = members.shape

    table, main = pl.pallas_call(
        lambda *refs: table_kernel(pools, group, places, last, *refs),
        out_shape=(
            sds((devices, 128), I32),
            sds((3 * QUARTER, feature), BF16),
        ),
        in_specs=[hbm] * 3,
        scratch_shapes=[
            pltpu.VMEM((blocks, block_len), I32),
            pltpu.VMEM((1, blocks), I32),
            pltpu.VMEM((rows_dev, feature), BF16),
            pltpu.VMEM((blocks, 128), F32),
            pltpu.SemaphoreType.DMA((3,)),
        ],
        compiler_params=TABLE_PARAMS,
        cost_estimate=cost(rows_dev * rows_dev * feature),
        name="table",
    )(members, valid_row, embeddings)
    meta, codes = pl.pallas_call(
        lambda *refs: meta_kernel(group, places, last, *refs),
        out_shape=(sds((2, group, rows_dev), I32), sds((rows_dev, 128), I32)),
        in_specs=[hbm] * 3,
        scratch_shapes=[
            pltpu.VMEM((2 * group, block_len), I32),
            pltpu.VMEM((1, blocks), I32),
            pltpu.VMEM((1, blocks), I32),
            pltpu.VMEM((128, rows_dev), I32),
            pltpu.SemaphoreType.DMA((3,)),
        ],
        compiler_params=PARAMS,
        cost_estimate=cost(2 * rows_dev**3),
        name="meta",
    )(members, valid_row, cluster_row)

    def shift(rows, by):
        return lax.ppermute(rows, "grp", [(g, (g + by) % group) for g in range(group)])

    def swap(rows):
        return lax.ppermute(rows, "grp", [(g, g ^ 1) for g in range(group)])

    def to_pools(rows):
        return lax.all_to_all(rows, "pool", split_axis=0, concat_axis=0, tiled=True)

    vmem = pl.BlockSpec(memory_space=pltpu.VMEM)
    rest = pl.pallas_call(
        lambda *refs: rest_kernel(pools, places, last, *refs),
        out_shape=sds((QUARTER, feature), BF16),
        in_specs=[vmem, vmem, hbm],
        compiler_params=PARAMS,
        name="rest",
    )(table, embeddings, meta)
    low_rest, high_rest = shift(rest, 2), shift(rest, -2)
    own0 = to_pools(main.reshape(pools, -1, feature)).reshape(-1, feature)
    sent = pl.pallas_call(
        lambda *refs: join_kernel(pools, *refs),
        out_shape=sds((pools, 3 * QUARTER // pools, feature), BF16),
        compiler_params=PARAMS,
        name="join",
    )(rest, low_rest, high_rest)
    arrived = lax.cond(jnp.any(valid > 0), to_pools, jnp.zeros_like, sent)
    low0, high0 = shift(own0, 2), shift(own0, -2)
    sib0 = swap(own0)

    def tiles(kernel, name, squares, operands, small, out_shape=sds((8, rows_dev), F32), more=()):
        return pl.pallas_call(
            kernel,
            out_shape=out_shape,
            in_specs=[hbm] * len(operands) + [vmem] * len(small),
            scratch_shapes=[
                pltpu.VMEM((2, 3 * QUARTER, QUARTER), F32),
                pltpu.VMEM((4, rows_dev, 128), F32),
                pltpu.VMEM((5, 8, rows_dev), F32),
                *more,
                pltpu.SemaphoreType.DMA((len(operands),)),
                *[pltpu.VMEM(operand.shape, BF16) for operand in operands],
            ],
            compiler_params=PARAMS,
            cost_estimate=cost(squares * QUARTER * QUARTER * feature),
            name=name,
        )(*operands, *small)

    swapped = swap(arrived[:, : 2 * QUARTER // pools])
    early = tiles(early_kernel, "early", 27, (own0, sib0, arrived, swapped), (meta, codes))
    low0 = pl.pallas_call(
        follow_kernel,
        out_shape=sds(low0.shape, BF16),
        in_specs=[hbm] * 3,
        out_specs=hbm,
        input_output_aliases={0: 0},
        compiler_params=PARAMS,
        name="follow",
    )(low0, high0, early)
    lows0 = swap(low0)
    late = tiles(
        late_kernel, "late", 32, (own0, high0, sib0, arrived, swapped, low0), (meta, codes, early)
    )
    best = tiles(
        lambda *refs: last_kernel(pools, group, group * (places - last), group * last, *refs),
        "last", 6, (lows0, high0, arrived), (meta, codes, late),
        out_shape=sds((devices, group * places), F32),
        more=(pltpu.VMEM((8, rows_dev), F32), pltpu.VMEM((group, rows_dev), F32)),
    )
    returned = lax.all_to_all(best, ("pool", "grp"), split_axis=0, concat_axis=0, tiled=True)
    scores = pl.pallas_call(
        lambda *refs: score_kernel(pools, group, places, *refs),
        out_shape=sds((1, rows_dev), F32),
        compiler_params=PARAMS,
        name="score",
    )(table, returned)
    return scores.reshape(rows_dev)


def cost(products):
    return pl.CostEstimate(flops=2 * products, bytes_accessed=0, transcendentals=0)


def solution(mesh):
    in_specs = (P(("pool", "grp"), None), P(), P(), P())
    out_specs = P(("pool", "grp"))
    return jax.shard_map(body, mesh=mesh, in_specs=in_specs, out_specs=out_specs, check_vma=False)
```

```python
import functools

import jax
import jax.numpy as jnp
from jax import lax
from jax.experimental import pallas as pl
from jax.experimental.pallas import tpu as pltpu
from jax.sharding import PartitionSpec as P

EPS = 1e-06
F32 = jnp.float32
BF16 = jnp.bfloat16
I32 = jnp.int32
QUARTER = 256
CODE = 8192
NT = (((1,), (1,)), ((), ()))
PARAMS = pltpu.CompilerParams(vmem_limit_bytes=24 * 1024 * 1024)
TABLE_PARAMS = pltpu.CompilerParams(vmem_limit_bytes=62 * 1024 * 1024)


def iota(shape, dim):
    return lax.broadcasted_iota(I32, shape, dim)


def normal_rows(rows):
    return (rows * lax.rsqrt(jnp.sum(rows * rows, axis=1, keepdims=True) + EPS)).astype(BF16)


def picked_rows(table, emb, first, count, pools):
    width = emb.shape[0]
    wanted = []
    for k in range(first, first + count):
        hit = table[:, k : k + 1] == iota((table.shape[0], width), 1)
        wanted.append(jnp.where(hit, 1.0, 0.0).reshape(pools, -1, width))
    choice = jnp.concatenate(wanted, axis=1).reshape(-1, width).astype(BF16)
    return normal_rows(jnp.dot(choice, emb, preferred_element_type=F32))


def table_kernel(
    pools, group, places, last, members_hbm, valid_hbm, emb_hbm, table_ref, main_ref,
    members_ref, valid_ref, emb_ref, found_ref, sems,
):
    copies = []
    for n, (source, target) in enumerate(
        ((members_hbm, members_ref), (valid_hbm, valid_ref), (emb_hbm, emb_ref))
    ):
        copies.append(pltpu.make_async_copy(source, target, sems.at[n]))
        copies[-1].start()
    rows_dev = emb_ref.shape[0]
    device = lax.axis_index("pool") * group + lax.axis_index("grp")
    blocks, block_len = members_ref.shape
    devices = blocks // 2
    before = jnp.where(
        iota((block_len, block_len), 0) < iota((block_len, block_len), 1), 1.0, 0.0
    ).astype(BF16)
    at = iota((blocks, blocks), 1) == iota((blocks, blocks), 0)
    copies[0].wait()
    copies[1].wait()
    live = jnp.sum(jnp.where(at, valid_ref[...], 0), axis=1, keepdims=True)
    local = members_ref[...] - device * rows_dev
    mine = (local >= 0) & (local < rows_dev) & (iota((blocks, block_len), 1) < live)
    ones = jnp.where(mine, 1.0, 0.0)
    counts = jnp.broadcast_to(jnp.sum(ones, axis=1, keepdims=True), (blocks, 128))
    counts = jnp.where(iota((blocks, 128), 0) % 2 == 1, pltpu.roll(counts, 1, 0), 0.0)
    rank = jnp.dot(ones.astype(BF16), before, preferred_element_type=F32) + counts[:, :1]
    rank = jnp.where(mine, rank, -1.0)
    value = (local + 1).astype(F32)
    lane = iota((blocks, 128), 1)
    found = jnp.zeros((blocks, 128), F32)
    for k in range(places):
        entry = jnp.sum(jnp.where(rank == k, value, 0.0), axis=1, keepdims=True)
        found = jnp.where(lane == k, entry, found)
    found_ref[...] = found
    pair = found_ref[pl.ds(0, devices, stride=2), :] + found_ref[pl.ds(1, devices, stride=2), :]
    table = pair.astype(I32) - 1
    table_ref[...] = table
    copies[2].wait()
    main_ref[...] = picked_rows(table, emb_ref[...], 0, places - last, pools)


def rest_kernel(pools, places, last, table_ref, emb_ref, after, out):
    del after
    out[...] = picked_rows(table_ref[...], emb_ref[...], places - last, last, pools)


def relatives():
    group = lax.axis_size("grp")
    index = lax.axis_index("grp")
    flip = 1 - 2 * (index % 2)
    below = (index + group - 2) % group
    return index, index + flip, below, below + flip, (index + 2) % group


def meta_kernel(
    group, places, last, members_hbm, valid_hbm, cluster_hbm, out_ref, codes_ref,
    members_ref, valid_ref, cluster_ref, packed_ref, sems,
):
    blocks = valid_ref.shape[1]
    block_len = members_ref.shape[1]
    pool = lax.axis_index("pool")
    first_block = pl.multiple_of(pool * 2 * group, 2 * group)
    copies = []
    for n, (source, target) in enumerate(
        (
            (members_hbm.at[pl.ds(first_block, 2 * group), :], members_ref),
            (valid_hbm, valid_ref),
            (cluster_hbm, cluster_ref),
        )
    ):
        copies.append(pltpu.make_async_copy(source, target, sems.at[n]))
        copies[-1].start()
    sources = blocks // 2
    slots = 2 * block_len
    width = group * places
    before = jnp.where(iota((slots, slots), 0) < iota((slots, slots), 1), 1.0, 0.0).astype(BF16)
    slot = iota((1, slots), 1)
    kind = iota((2 * width, slots), 0)
    kind_place = kind % width // group
    kind_owner = kind % group
    kind_value = jnp.where(kind < width, slot // 32, slot % 32 + 1)
    found = jnp.zeros((sources, 2 * width), F32)
    block_lane = iota((1, blocks), 1)
    lane = iota((1, width), 1)
    first_cluster = jnp.zeros((1, width), I32)
    second_cluster = jnp.zeros((1, width), I32)
    for copy in copies:
        copy.wait()
    for owner in range(group):
        halves, lives = [], []
        for half in range(2):
            halves.append(members_ref[2 * owner + half : 2 * owner + half + 1, :])
            at = block_lane == first_block + 2 * owner + half
            lives.append(jnp.sum(jnp.where(at, valid_ref[...], 0), axis=1, keepdims=True))
            cluster = jnp.sum(jnp.where(at, cluster_ref[...], 0), axis=1, keepdims=True)
            if half == 0:
                first_cluster = jnp.where(lane % group == owner, cluster, first_cluster)
            else:
                second_cluster = jnp.where(lane % group == owner, cluster, second_cluster)
        rows = jnp.concatenate(halves, axis=1)
        end = jnp.where(slot < block_len, lives[0], block_len + lives[1])
        origin = jnp.where(slot < end, rows // slots, -1)
        match = iota((sources, slots), 0) == origin
        ones = jnp.where(match, 1.0, 0.0).astype(BF16)
        ranks = jnp.dot(ones, before, preferred_element_type=F32)
        rank = jnp.sum(jnp.where(match, ranks, 0.0), axis=0, keepdims=True).astype(I32)
        weight = jnp.where((kind_owner == owner) & (kind_place == rank), kind_value, 0)
        found = found + lax.dot_general(
            ones, weight.astype(F32).astype(BF16), NT, preferred_element_type=F32
        )
    found = found.astype(I32)
    place = found[:, :width] * 32 + found[:, width:] - 1
    filled = found[:, width:] > 0
    position = jnp.where(filled, place + lane % group * slots, -1)
    cluster = jnp.where(filled, jnp.where(place < block_len, first_cluster, second_cluster), -1)
    main = (places - last) * group
    rest = last * group
    pools = sources // group
    for n, values in enumerate((position, cluster)):
        for p in range(pools):
            own = values[p * group : (p + 1) * group, :]
            out_ref[n, :, p * main : (p + 1) * main] = own[:, :main]
            at = pools * main + p * rest
            out_ref[n, :, at : at + rest] = own[:, main:]
    packed_ref[...] = jnp.zeros(packed_ref.shape, I32)
    for n, cls in enumerate(relatives()[:4]):
        pos = out_ref[0, pl.ds(cls, 1), :]
        cluster = out_ref[1, pl.ds(cls, 1), :]
        packed_ref[n : n + 1, :] = jnp.where(cluster < 0, -2 * CODE, cluster * CODE + pos)
    codes_ref[...] = jnp.transpose(packed_ref[...])


def run(pieces, sims_ref, tiles=None):
    for n in range(len(pieces) + 1):
        if n == 1 and tiles is not None:
            tiles.start_rest()
        if n < len(pieces):
            piece = pieces[n]
            sims_ref[n % 2, : piece["count"], :] = lax.dot_general(
                piece["left"](), piece["right"](), NT, preferred_element_type=F32
            )
        if n > 0:
            take_maxima(sims_ref.at[(n - 1) % 2], **pieces[n - 1])


def take_maxima(sims_ref, left, right, count, codes, cls, rows, start, pos_row, cluster_row, col, col_start, same):
    step = 128
    right_pos, right_cluster = pos_row(), cluster_row()
    parts = QUARTER // 128
    best_col = [jnp.zeros((8, 128), F32) for _ in range(parts)]
    for top in range(0, count, step):
        code = codes[start + top : start + top + step, cls : cls + 1]
        code = jnp.broadcast_to(code, (step, 128))
        pos = code & (CODE - 1)
        cluster = code >> 13
        best = rows[start + top : start + top + step, :]
        for part in range(parts):
            lanes = slice(part * 128, part * 128 + 128)
            sims = sims_ref[top : top + step, lanes]
            sims = jnp.where(cluster == right_cluster[:, lanes], sims, 0.0)
            earlier = right_pos[:, lanes] < pos
            best = jnp.maximum(best, jnp.where(earlier, sims, 0.0))
            if top < same:
                later = jnp.where(earlier, 0.0, sims)
                best_col[part] = jnp.maximum(
                    best_col[part], jnp.max(later.reshape(-1, 8, 128), axis=0)
                )
        rows[start + top : start + top + step, :] = best
    if same > 0:
        for part in range(parts):
            lanes = slice(col_start + part * 128, col_start + part * 128 + 128)
            col[:, lanes] = jnp.maximum(col[:, lanes], best_col[part])


def row_result(row_ref):
    return jnp.max(jnp.transpose(row_ref[...]), axis=0, keepdims=True)


def col_result(col_ref):
    return jnp.max(col_ref[...], axis=0, keepdims=True)


OWN, SIB, LOW, LOWS, HIGH = range(5)


class Tiles:
    def __init__(self, moves, first, held, sems, meta, codes, rows, cols, row_classes, col_classes):
        self.held, self.meta, self.codes, self.rows, self.cols = held, meta, codes, rows, cols
        self.row_classes, self.col_classes = row_classes, col_classes
        self.relatives = relatives()
        self.copies = {}
        per = held.shape[1] // 4
        for n, (cls, ref, at) in enumerate(moves):
            if at is None:
                source, target = ref, held.at[cls, pl.ds(0, 3 * per)]
            else:
                source, target = ref.at[:, pl.ds(at, 16), :], held.at[cls, pl.ds(3 * per, per)]
            self.copies[cls, at is not None] = pltpu.make_async_copy(source, target, sems.at[n])
        self.later = list(self.copies.values())[first:]
        for copy in list(self.copies.values())[:first]:
            copy.start()
        for cls in row_classes:
            rows[cls, :, :] = jnp.zeros(rows.shape[1:], F32)
        for cls in col_classes:
            cols[cls, :, :] = jnp.zeros(cols.shape[1:], F32)

    def start_rest(self):
        for copy in self.later:
            copy.start()
        self.later = []

    def wait(self, cls, last):
        copy = self.copies.pop((cls, last), None)
        if copy is not None:
            copy.wait()

    def wait_all(self):
        for cls, last in list(self.copies):
            self.wait(cls, last)

    def load(self, cls, quarter, count=1):
        if quarter < 3:
            self.wait(cls, False)
        if quarter + count > 3:
            self.wait(cls, True)
        per = self.held.shape[1] // 4
        return self.held[cls, quarter * per : (quarter + count) * per].reshape(count * QUARTER, -1)

    def piece(self, left, quarter, count, right, right_quarter, same=None):
        lanes = slice(right_quarter * QUARTER, (right_quarter + 1) * QUARTER)
        place = self.relatives[right]
        return dict(
            left=lambda: self.load(left, quarter, count),
            right=lambda: self.load(right, right_quarter),
            count=count * QUARTER,
            codes=self.codes,
            cls=left,
            rows=self.rows.at[left],
            start=quarter * QUARTER,
            pos_row=lambda: self.meta[0, pl.ds(place, 1), lanes],
            cluster_row=lambda: self.meta[1, pl.ds(place, 1), lanes],
            col=self.cols.at[right],
            col_start=right_quarter * QUARTER,
            same=count * QUARTER if same is None else same,
        )

    def matched(self, flip, left, right, pairs):
        pieces = []
        for b in range(4):
            mine = [a for a in range(4) if (a, b) in pairs and (a // 2 + b // 2) % 2 == flip]
            if mine:
                assert mine == list(range(mine[0], mine[-1] + 1))
                pieces.append(self.piece(left, mine[0], len(mine), right, b))
        return pieces

    def result(self, cls):
        best = []
        if cls in self.row_classes:
            best.append(row_result(self.rows.at[cls]))
        if cls in self.col_classes:
            best.append(col_result(self.cols.at[cls]))
        return functools.reduce(jnp.maximum, best)


def either(flag, work):
    pl.when(flag)(lambda: work(1))
    pl.when(jnp.logical_not(flag))(lambda: work(0))


def second_core():
    return lax.axis_index("grp") % 2 == 1


def outer_chip():
    chip = lax.axis_index("grp") // 2
    return (chip == 0) | (chip == 3)


ALL_PAIRS = [(a, b) for a in range(4) for b in range(4)]


def follow_kernel(rows, after, also_after, out):
    del rows, after, also_after, out


def join_kernel(pools, rest, low_rest, high_rest, out):
    width = QUARTER // pools
    for n, part in enumerate((rest, low_rest, high_rest)):
        out[:, n * width : (n + 1) * width, :] = part[...].reshape(pools, width, -1)


def near_kernel(own0, sib0, meta, codes, out, sims, rows, cols, held, sems):
    moves = [(OWN, own0, None), (SIB, sib0, None)]
    tiles = Tiles(moves, 1, held, sems, meta, codes, rows, cols, (OWN,), (OWN, SIB))
    run([tiles.piece(OWN, 0, b + 1, OWN, b, same=b * QUARTER) for b in range(3)], sims, tiles)
    tiles.wait_all()
    pairs = [(a, b) for a, b in ALL_PAIRS if 3 not in (a, b)]
    either(second_core(), lambda flip: run(tiles.matched(flip, OWN, SIB, pairs), sims))
    out[...] = jnp.zeros(out.shape, F32)
    for cls in (OWN, SIB):
        out[cls : cls + 1, :] = tiles.result(cls)


def main_kernel(
    own0, arrived, high0, sib0, swapped, low0, meta, codes, near, out, sims, rows, cols, held, sems
):
    width = arrived.shape[1] // 3
    moves = [
        (OWN, own0, None), (OWN, arrived, 0), (HIGH, high0, None), (HIGH, arrived, 2 * width),
        (SIB, sib0, None), (SIB, swapped, 0), (LOW, low0, None), (LOW, arrived, width),
    ]
    tiles = Tiles(
        moves, 3, held, sems, meta, codes, rows, cols, (OWN, SIB, LOW), (OWN, SIB, HIGH)
    )
    pieces = [tiles.piece(OWN, 0, 4, OWN, 3, same=3 * QUARTER)]
    pieces += [tiles.piece(cls, 0, 4, HIGH, b) for cls in (OWN, SIB) for b in range(4)]
    run(pieces, sims, tiles)
    tiles.wait_all()
    pairs = [(a, b) for a, b in ALL_PAIRS if 3 in (a, b)]
    either(second_core(), lambda flip: run(tiles.matched(flip, OWN, SIB, pairs), sims))
    either(outer_chip(), lambda flip: run(tiles.matched(flip, LOW, HIGH, ALL_PAIRS), sims))
    for cls in (OWN, SIB, LOW, HIGH):
        out[cls : cls + 1, :] = jnp.maximum(near[cls : cls + 1, :], tiles.result(cls))


def last_kernel(
    pools, group, main, rest, lows0, high0, swapped, arrived, meta, codes, before, out,
    sims, rows, cols, held, sems, every,
):
    width = arrived.shape[1] // 3
    moves = [
        (LOWS, lows0, None), (HIGH, high0, None),
        (LOWS, swapped, width), (HIGH, arrived, 2 * width),
    ]
    tiles = Tiles(moves, 4, held, sems, meta, codes, rows, cols, (LOWS,), (HIGH,))
    tiles.wait_all()
    either(outer_chip(), lambda flip: run(tiles.matched(flip, LOWS, HIGH, ALL_PAIRS), sims))
    every[...] = jnp.zeros(every.shape, F32)
    for cls, place in enumerate(tiles.relatives):
        best = [] if cls == LOWS else [before[cls : cls + 1, :]]
        if cls in (LOWS, HIGH):
            best.append(tiles.result(cls))
        every[pl.ds(place, 1), :] = functools.reduce(jnp.maximum, best)
    for p in range(pools):
        rows_out = slice(p * group, (p + 1) * group)
        out[rows_out, :main] = every[:, p * main : (p + 1) * main]
        at = pools * main + p * rest
        out[rows_out, main:] = every[:, at : at + rest]


def score_kernel(pools, group, places, table_ref, returned_ref, out_ref):
    rows_dev = out_ref.shape[1]
    arrived = jnp.transpose(
        jnp.concatenate([returned_ref[...], jnp.zeros_like(returned_ref)], axis=1)
    )
    table = table_ref[...]
    row = iota((8, rows_dev), 1)
    total = jnp.zeros((8, rows_dev), F32)
    for p in range(pools):
        for k in range(places):
            value = jnp.max(
                arrived[k * group : (k + 1) * group, p * group : (p + 1) * group],
                axis=1,
                keepdims=True,
            )
            entry = table[p * group : (p + 1) * group, k : k + 1]
            total = jnp.where(entry == row, value, total)
    out_ref[...] = jnp.sum(total, axis=0, keepdims=True)


def body(embeddings, members, valid, block_cluster):
    rows_dev, feature = embeddings.shape
    pools = lax.axis_size("pool")
    group = lax.axis_size("grp")
    devices = pools * group
    places = rows_dev // devices
    last = places // 4
    sds = jax.ShapeDtypeStruct
    hbm = pl.BlockSpec(memory_space=pltpu.HBM)
    valid_row = valid.reshape(1, -1)
    cluster_row = block_cluster.reshape(1, -1)
    blocks, block_len = members.shape

    some = jnp.any(valid > 0)
    table, main = pl.pallas_call(
        lambda *refs: table_kernel(pools, group, places, last, *refs),
        out_shape=(
            sds((devices, 128), I32),
            sds((3 * QUARTER, feature), BF16),
        ),
        in_specs=[hbm] * 3,
        scratch_shapes=[
            pltpu.VMEM((blocks, block_len), I32),
            pltpu.VMEM((1, blocks), I32),
            pltpu.VMEM((rows_dev, feature), BF16),
            pltpu.VMEM((blocks, 128), F32),
            pltpu.SemaphoreType.DMA((3,)),
        ],
        compiler_params=TABLE_PARAMS,
        cost_estimate=cost(rows_dev * rows_dev * feature),
        name="table",
    )(members, valid_row, embeddings)
    meta, codes = pl.pallas_call(
        lambda *refs: meta_kernel(group, places, last, *refs),
        out_shape=(sds((2, group, rows_dev), I32), sds((rows_dev, 128), I32)),
        in_specs=[hbm] * 3,
        scratch_shapes=[
            pltpu.VMEM((2 * group, block_len), I32),
            pltpu.VMEM((1, blocks), I32),
            pltpu.VMEM((1, blocks), I32),
            pltpu.VMEM((128, rows_dev), I32),
            pltpu.SemaphoreType.DMA((3,)),
        ],
        compiler_params=PARAMS,
        cost_estimate=cost(2 * rows_dev**3),
        name="meta",
    )(members, valid_row, cluster_row)

    def shift(rows, by):
        return lax.ppermute(rows, "grp", [(g, (g + by) % group) for g in range(group)])

    def swap(rows):
        return lax.ppermute(rows, "grp", [(g, g ^ 1) for g in range(group)])

    def to_pools(rows):
        return lax.all_to_all(rows, "pool", split_axis=0, concat_axis=0, tiled=True)

    vmem = pl.BlockSpec(memory_space=pltpu.VMEM)
    rest = pl.pallas_call(
        lambda *refs: rest_kernel(pools, places, last, *refs),
        out_shape=sds((QUARTER, feature), BF16),
        in_specs=[vmem, vmem, hbm],
        compiler_params=PARAMS,
        name="rest",
    )(table, embeddings, meta)
    low_rest, high_rest = shift(rest, 2), shift(rest, -2)
    own0 = to_pools(main.reshape(pools, -1, feature)).reshape(-1, feature)
    sent = pl.pallas_call(
        lambda *refs: join_kernel(pools, *refs),
        out_shape=sds((pools, 3 * QUARTER // pools, feature), BF16),
        compiler_params=PARAMS,
        name="join",
    )(rest, low_rest, high_rest)
    own0 = pl.pallas_call(
        follow_kernel,
        out_shape=sds(own0.shape, BF16),
        in_specs=[hbm] * 3,
        out_specs=hbm,
        input_output_aliases={0: 0},
        compiler_params=PARAMS,
        name="follow",
    )(own0, sent, some.astype(I32).reshape(1, 1))
    low0, high0 = shift(own0, 2), shift(own0, -2)
    sib0 = swap(own0)

    def tiles(kernel, name, squares, moves, operands, small, out_shape=(8, rows_dev), more=()):
        return pl.pallas_call(
            kernel,
            out_shape=sds(out_shape, F32),
            in_specs=[hbm] * len(operands) + [vmem] * len(small),
            scratch_shapes=[
                pltpu.VMEM((2, rows_dev, QUARTER), F32),
                pltpu.VMEM((4, rows_dev, 128), F32),
                pltpu.VMEM((5, 8, rows_dev), F32),
                pltpu.VMEM((5, rows_dev // 16, 16, feature), BF16),
                pltpu.SemaphoreType.DMA((moves,)),
                *more,
            ],
            compiler_params=PARAMS,
            cost_estimate=cost(squares * QUARTER * QUARTER * feature),
            name=name,
        )(*[operand.reshape(-1, *operand.shape[-2:]) if operand.ndim == 3 else
            operand.reshape(-1, 16, feature) for operand in operands], *small)

    def bring(sent, own0, sib0, meta, codes):
        near = tiles(near_kernel, "near", 11, 2, (own0, sib0), (meta, codes))
        return to_pools(sent), near

    def bring_nothing(sent, own0, sib0, meta, codes):
        return jnp.zeros_like(sent), jnp.zeros((8, rows_dev), F32)

    arrived, near = lax.cond(
        some, bring, bring_nothing, sent, own0, sib0, meta, codes
    )
    swapped = swap(arrived)
    best = tiles(
        main_kernel, "main", 49, 8, (own0, arrived, high0, sib0, swapped, low0), (meta, codes, near)
    )
    best = tiles(
        lambda *refs: last_kernel(pools, group, group * (places - last), group * last, *refs),
        "last", 8, 4, (swap(low0), high0, swapped, arrived), (meta, codes, best),
        out_shape=(devices, group * places),
        more=(pltpu.VMEM((group, rows_dev), F32),),
    )
    returned = lax.all_to_all(best, ("pool", "grp"), split_axis=0, concat_axis=0, tiled=True)
    scores = pl.pallas_call(
        lambda *refs: score_kernel(pools, group, places, *refs),
        out_shape=sds((1, rows_dev), F32),
        compiler_params=PARAMS,
        name="score",
    )(table, returned)
    return scores.reshape(rows_dev)


def cost(products):
    return pl.CostEstimate(flops=2 * products, bytes_accessed=0, transcendentals=0)


def solution(mesh):
    in_specs = (P(("pool", "grp"), None), P(), P(), P())
    out_specs = P(("pool", "grp"))
    return jax.shard_map(body, mesh=mesh, in_specs=in_specs, out_specs=out_specs, check_vma=False)
```

```python
import functools

import jax
import jax.numpy as jnp
from jax import lax
from jax.experimental import pallas as pl
from jax.experimental.pallas import tpu as pltpu
from jax.sharding import PartitionSpec as P

EPS = 1e-06
F32 = jnp.float32
BF16 = jnp.bfloat16
I32 = jnp.int32
QUARTER = 256
CODE = 8192
NT = (((1,), (1,)), ((), ()))
PARAMS = pltpu.CompilerParams(vmem_limit_bytes=24 * 1024 * 1024)
TABLE_PARAMS = pltpu.CompilerParams(vmem_limit_bytes=62 * 1024 * 1024)


def iota(shape, dim):
    return lax.broadcasted_iota(I32, shape, dim)


def normal_rows(rows):
    return (rows * lax.rsqrt(jnp.sum(rows * rows, axis=1, keepdims=True) + EPS)).astype(BF16)


def picked_rows(table, emb, first, count, pools):
    width = emb.shape[0]
    wanted = []
    for k in range(first, first + count):
        hit = table[:, k : k + 1] == iota((table.shape[0], width), 1)
        wanted.append(jnp.where(hit, 1.0, 0.0).reshape(pools, -1, width))
    choice = jnp.concatenate(wanted, axis=1).reshape(-1, width).astype(BF16)
    return normal_rows(jnp.dot(choice, emb, preferred_element_type=F32))


def table_kernel(
    pools, group, places, last, members_hbm, valid_hbm, emb_hbm, table_ref, main_ref,
    members_ref, valid_ref, emb_ref, found_ref, sems,
):
    copies = []
    for n, (source, target) in enumerate(
        ((members_hbm, members_ref), (valid_hbm, valid_ref), (emb_hbm, emb_ref))
    ):
        copies.append(pltpu.make_async_copy(source, target, sems.at[n]))
        copies[-1].start()
    rows_dev = emb_ref.shape[0]
    device = lax.axis_index("pool") * group + lax.axis_index("grp")
    blocks, block_len = members_ref.shape
    devices = blocks // 2
    before = jnp.where(
        iota((block_len, block_len), 0) < iota((block_len, block_len), 1), 1.0, 0.0
    ).astype(BF16)
    at = iota((blocks, blocks), 1) == iota((blocks, blocks), 0)
    copies[0].wait()
    copies[1].wait()
    live = jnp.sum(jnp.where(at, valid_ref[...], 0), axis=1, keepdims=True)
    local = members_ref[...] - device * rows_dev
    mine = (local >= 0) & (local < rows_dev) & (iota((blocks, block_len), 1) < live)
    ones = jnp.where(mine, 1.0, 0.0)
    counts = jnp.broadcast_to(jnp.sum(ones, axis=1, keepdims=True), (blocks, 128))
    counts = jnp.where(iota((blocks, 128), 0) % 2 == 1, pltpu.roll(counts, 1, 0), 0.0)
    rank = jnp.dot(ones.astype(BF16), before, preferred_element_type=F32) + counts[:, :1]
    rank = jnp.where(mine, rank, -1.0)
    value = (local + 1).astype(F32)
    lane = iota((blocks, 128), 1)
    found = jnp.zeros((blocks, 128), F32)
    for k in range(places):
        entry = jnp.sum(jnp.where(rank == k, value, 0.0), axis=1, keepdims=True)
        found = jnp.where(lane == k, entry, found)
    found_ref[...] = found
    pair = found_ref[pl.ds(0, devices, stride=2), :] + found_ref[pl.ds(1, devices, stride=2), :]
    table = pair.astype(I32) - 1
    table_ref[...] = table
    copies[2].wait()
    main_ref[...] = picked_rows(table, emb_ref[...], 0, places - last, pools)


def rest_kernel(pools, places, last, table_ref, emb_ref, after, out):
    del after
    out[...] = picked_rows(table_ref[...], emb_ref[...], places - last, last, pools)


def relatives():
    group = lax.axis_size("grp")
    index = lax.axis_index("grp")
    flip = 1 - 2 * (index % 2)
    below = (index + group - 2) % group
    return index, index + flip, below, below + flip, (index + 2) % group


def meta_kernel(
    group, places, last, members_hbm, valid_hbm, cluster_hbm, out_ref, codes_ref,
    members_ref, valid_ref, cluster_ref, packed_ref, sems,
):
    blocks = valid_ref.shape[1]
    block_len = members_ref.shape[1]
    pool = lax.axis_index("pool")
    first_block = pl.multiple_of(pool * 2 * group, 2 * group)
    copies = []
    for n, (source, target) in enumerate(
        (
            (members_hbm.at[pl.ds(first_block, 2 * group), :], members_ref),
            (valid_hbm, valid_ref),
            (cluster_hbm, cluster_ref),
        )
    ):
        copies.append(pltpu.make_async_copy(source, target, sems.at[n]))
        copies[-1].start()
    sources = blocks // 2
    slots = 2 * block_len
    width = group * places
    before = jnp.where(iota((slots, slots), 0) < iota((slots, slots), 1), 1.0, 0.0).astype(BF16)
    slot = iota((1, slots), 1)
    kind = iota((2 * width, slots), 0)
    kind_place = kind % width // group
    kind_owner = kind % group
    kind_value = jnp.where(kind < width, slot // 32, slot % 32 + 1)
    found = jnp.zeros((sources, 2 * width), F32)
    block_lane = iota((1, blocks), 1)
    lane = iota((1, width), 1)
    first_cluster = jnp.zeros((1, width), I32)
    second_cluster = jnp.zeros((1, width), I32)
    for copy in copies:
        copy.wait()
    for owner in range(group):
        halves, lives = [], []
        for half in range(2):
            halves.append(members_ref[2 * owner + half : 2 * owner + half + 1, :])
            at = block_lane == first_block + 2 * owner + half
            lives.append(jnp.sum(jnp.where(at, valid_ref[...], 0), axis=1, keepdims=True))
            cluster = jnp.sum(jnp.where(at, cluster_ref[...], 0), axis=1, keepdims=True)
            if half == 0:
                first_cluster = jnp.where(lane % group == owner, cluster, first_cluster)
            else:
                second_cluster = jnp.where(lane % group == owner, cluster, second_cluster)
        rows = jnp.concatenate(halves, axis=1)
        end = jnp.where(slot < block_len, lives[0], block_len + lives[1])
        origin = jnp.where(slot < end, rows // slots, -1)
        match = iota((sources, slots), 0) == origin
        ones = jnp.where(match, 1.0, 0.0).astype(BF16)
        ranks = jnp.dot(ones, before, preferred_element_type=F32)
        rank = jnp.sum(jnp.where(match, ranks, 0.0), axis=0, keepdims=True).astype(I32)
        weight = jnp.where((kind_owner == owner) & (kind_place == rank), kind_value, 0)
        found = found + lax.dot_general(
            ones, weight.astype(F32).astype(BF16), NT, preferred_element_type=F32
        )
    found = found.astype(I32)
    place = found[:, :width] * 32 + found[:, width:] - 1
    filled = found[:, width:] > 0
    position = jnp.where(filled, place + lane % group * slots, -1)
    cluster = jnp.where(filled, jnp.where(place < block_len, first_cluster, second_cluster), -1)
    main = (places - last) * group
    rest = last * group
    pools = sources // group
    for n, values in enumerate((position, cluster)):
        for p in range(pools):
            own = values[p * group : (p + 1) * group, :]
            out_ref[n, :, p * main : (p + 1) * main] = own[:, :main]
            at = pools * main + p * rest
            out_ref[n, :, at : at + rest] = own[:, main:]
    packed_ref[...] = jnp.zeros(packed_ref.shape, I32)
    for n, cls in enumerate(relatives()[:4]):
        pos = out_ref[0, pl.ds(cls, 1), :]
        cluster = out_ref[1, pl.ds(cls, 1), :]
        packed_ref[n : n + 1, :] = jnp.where(cluster < 0, -2 * CODE, cluster * CODE + pos)
    codes_ref[...] = jnp.transpose(packed_ref[...])


def run(pieces, sims_ref, tiles=None):
    for n in range(len(pieces) + 1):
        if n == 1 and tiles is not None:
            tiles.start_rest()
        if n < len(pieces):
            piece = pieces[n]
            sims_ref[n % 2, : piece["count"], :] = lax.dot_general(
                piece["left"](), piece["right"](), NT, preferred_element_type=F32
            )
        if n > 0:
            take_maxima(sims_ref.at[(n - 1) % 2], **pieces[n - 1])


def take_maxima(sims_ref, left, right, count, codes, cls, rows, start, pos_row, cluster_row, col, col_start, same):
    step = 128
    right_pos, right_cluster = pos_row(), cluster_row()
    parts = QUARTER // 128
    best_col = [jnp.zeros((8, 128), F32) for _ in range(parts)]
    for top in range(0, count, step):
        code = codes[start + top : start + top + step, cls : cls + 1]
        code = jnp.broadcast_to(code, (step, 128))
        pos = code & (CODE - 1)
        cluster = code >> 13
        best = rows[start + top : start + top + step, :]
        for part in range(parts):
            lanes = slice(part * 128, part * 128 + 128)
            sims = sims_ref[top : top + step, lanes]
            sims = jnp.where(cluster == right_cluster[:, lanes], sims, 0.0)
            earlier = right_pos[:, lanes] < pos
            best = jnp.maximum(best, jnp.where(earlier, sims, 0.0))
            if top < same:
                later = jnp.where(earlier, 0.0, sims)
                best_col[part] = jnp.maximum(
                    best_col[part], jnp.max(later.reshape(-1, 8, 128), axis=0)
                )
        rows[start + top : start + top + step, :] = best
    if same > 0:
        for part in range(parts):
            lanes = slice(col_start + part * 128, col_start + part * 128 + 128)
            col[:, lanes] = jnp.maximum(col[:, lanes], best_col[part])


def row_result(row_ref):
    return jnp.max(jnp.transpose(row_ref[...]), axis=0, keepdims=True)


def col_result(col_ref):
    return jnp.max(col_ref[...], axis=0, keepdims=True)


OWN, SIB, LOW, LOWS, HIGH = range(5)


class Tiles:
    def __init__(self, moves, first, held, sems, meta, codes, rows, cols, row_classes, col_classes):
        self.held, self.meta, self.codes, self.rows, self.cols = held, meta, codes, rows, cols
        self.row_classes, self.col_classes = row_classes, col_classes
        self.relatives = relatives()
        self.copies = {}
        per = held.shape[1] // 4
        started = []
        for n, (cls, ref, at, quarter, count) in enumerate(moves):
            source = ref if at is None else ref.at[:, pl.ds(at, 16), :]
            target = held.at[cls, pl.ds(quarter * per, count * per)]
            started.append(pltpu.make_async_copy(source, target, sems.at[n]))
            for q in range(quarter, quarter + count):
                self.copies[cls, q] = started[-1]
        self.later = started[first:]
        self.waited = []
        for copy in started[:first]:
            copy.start()
        for cls in row_classes:
            rows[cls, :, :] = jnp.zeros(rows.shape[1:], F32)
        for cls in col_classes:
            cols[cls, :, :] = jnp.zeros(cols.shape[1:], F32)

    def start_rest(self):
        for copy in self.later:
            copy.start()
        self.later = []

    def wait(self, cls, quarter):
        copy = self.copies.pop((cls, quarter), None)
        if copy is not None and not any(copy is other for other in self.waited):
            copy.wait()
            self.waited.append(copy)

    def wait_all(self):
        for cls, quarter in list(self.copies):
            self.wait(cls, quarter)

    def load(self, cls, quarter, count=1):
        for q in range(quarter, quarter + count):
            self.wait(cls, q)
        per = self.held.shape[1] // 4
        return self.held[cls, quarter * per : (quarter + count) * per].reshape(count * QUARTER, -1)

    def piece(self, left, quarter, count, right, right_quarter, same=None):
        lanes = slice(right_quarter * QUARTER, (right_quarter + 1) * QUARTER)
        place = self.relatives[right]
        return dict(
            left=lambda: self.load(left, quarter, count),
            right=lambda: self.load(right, right_quarter),
            count=count * QUARTER,
            codes=self.codes,
            cls=left,
            rows=self.rows.at[left],
            start=quarter * QUARTER,
            pos_row=lambda: self.meta[0, pl.ds(place, 1), lanes],
            cluster_row=lambda: self.meta[1, pl.ds(place, 1), lanes],
            col=self.cols.at[right],
            col_start=right_quarter * QUARTER,
            same=count * QUARTER if same is None else same,
        )

    def matched(self, flip, left, right, pairs):
        pieces = []
        for b in range(4):
            mine = [a for a in range(4) if (a, b) in pairs and (a // 2 + b // 2) % 2 == flip]
            if mine:
                assert mine == list(range(mine[0], mine[-1] + 1))
                pieces.append(self.piece(left, mine[0], len(mine), right, b))
        return pieces

    def result(self, cls):
        best = []
        if cls in self.row_classes:
            best.append(row_result(self.rows.at[cls]))
        if cls in self.col_classes:
            best.append(col_result(self.cols.at[cls]))
        return functools.reduce(jnp.maximum, best)


def either(flag, work):
    pl.when(flag)(lambda: work(1))
    pl.when(jnp.logical_not(flag))(lambda: work(0))


def second_core():
    return lax.axis_index("grp") % 2 == 1


def outer_chip():
    chip = lax.axis_index("grp") // 2
    return (chip == 0) | (chip == 3)


ALL_PAIRS = [(a, b) for a in range(4) for b in range(4)]


def follow_kernel(rows, after, also_after, out):
    del rows, after, also_after, out


def join_kernel(pools, rest, low_rest, high_rest, out):
    width = QUARTER // pools
    for n, part in enumerate((rest, low_rest, high_rest)):
        out[:, n * width : (n + 1) * width, :] = part[...].reshape(pools, width, -1)


def near_kernel(own0, sib0, meta, codes, out, sims, rows, cols, held, sems):
    moves = [(OWN, own0, None, 0, 3), (SIB, sib0, None, 0, 3)]
    tiles = Tiles(moves, 1, held, sems, meta, codes, rows, cols, (OWN,), (OWN, SIB))
    run([tiles.piece(OWN, 0, b + 1, OWN, b, same=b * QUARTER) for b in range(3)], sims, tiles)
    tiles.wait_all()
    pairs = [(a, b) for a, b in ALL_PAIRS if 3 not in (a, b)]
    either(second_core(), lambda flip: run(tiles.matched(flip, OWN, SIB, pairs), sims))
    out[...] = jnp.zeros(out.shape, F32)
    for cls in (OWN, SIB):
        out[cls : cls + 1, :] = tiles.result(cls)


def middle_kernel(
    own0, arrived, high01, sib0, meta, codes, near, out, sims, rows, cols, held, sems
):
    width = arrived.shape[1] // 3
    moves = [
        (OWN, own0, None, 0, 3), (OWN, arrived, 0, 3, 1), (HIGH, high01, None, 0, 2),
        (HIGH, arrived, 2 * width, 3, 1), (SIB, sib0, None, 0, 3),
    ]
    tiles = Tiles(moves, 2, held, sems, meta, codes, rows, cols, (OWN, SIB), (OWN, HIGH))
    pieces = [tiles.piece(OWN, 0, 4, OWN, 3, same=3 * QUARTER)]
    pieces += [tiles.piece(OWN, 0, 4, HIGH, b) for b in (0, 1, 3)]
    pieces += [tiles.piece(SIB, 0, 3, HIGH, b) for b in (0, 1, 3)]
    run(pieces, sims, tiles)
    out[...] = near[...]
    for cls in (OWN, SIB, HIGH):
        out[cls : cls + 1, :] = jnp.maximum(near[cls : cls + 1, :], tiles.result(cls))


def main_kernel(
    own0, arrived, high2, sib0, swapped, low0, high01, meta, codes, before, out,
    sims, rows, cols, held, sems,
):
    width = arrived.shape[1] // 3
    moves = [
        (HIGH, high2, None, 2, 1), (OWN, own0, None, 0, 3), (OWN, arrived, 0, 3, 1),
        (SIB, sib0, None, 0, 3), (SIB, swapped, 0, 3, 1), (HIGH, high01, None, 0, 2),
        (HIGH, arrived, 2 * width, 3, 1), (LOW, low0, None, 0, 3), (LOW, arrived, width, 3, 1),
    ]
    tiles = Tiles(
        moves, 3, held, sems, meta, codes, rows, cols, (OWN, SIB, LOW), (SIB, HIGH)
    )
    pieces = [tiles.piece(OWN, 0, 4, HIGH, 2), tiles.piece(SIB, 0, 4, HIGH, 2)]
    pieces += [tiles.piece(SIB, 3, 1, HIGH, b) for b in (0, 1, 3)]
    run(pieces, sims, tiles)
    pairs = [(a, b) for a, b in ALL_PAIRS if 3 in (a, b)]
    either(second_core(), lambda flip: run(tiles.matched(flip, OWN, SIB, pairs), sims))
    tiles.wait_all()
    either(outer_chip(), lambda flip: run(tiles.matched(flip, LOW, HIGH, ALL_PAIRS), sims))
    for cls in (OWN, SIB, LOW, HIGH):
        out[cls : cls + 1, :] = jnp.maximum(before[cls : cls + 1, :], tiles.result(cls))


def last_kernel(
    pools, group, main, rest, lows0, high01, high2, swapped, arrived, meta, codes, before, out,
    sims, rows, cols, held, sems, every,
):
    width = arrived.shape[1] // 3
    moves = [
        (LOWS, lows0, None, 0, 3), (LOWS, swapped, width, 3, 1), (HIGH, high01, None, 0, 2),
        (HIGH, high2, None, 2, 1), (HIGH, arrived, 2 * width, 3, 1),
    ]
    tiles = Tiles(moves, 5, held, sems, meta, codes, rows, cols, (LOWS,), (HIGH,))
    tiles.wait_all()
    either(outer_chip(), lambda flip: run(tiles.matched(flip, LOWS, HIGH, ALL_PAIRS), sims))
    every[...] = jnp.zeros(every.shape, F32)
    for cls, place in enumerate(tiles.relatives):
        best = [] if cls == LOWS else [before[cls : cls + 1, :]]
        if cls in (LOWS, HIGH):
            best.append(tiles.result(cls))
        every[pl.ds(place, 1), :] = functools.reduce(jnp.maximum, best)
    for p in range(pools):
        rows_out = slice(p * group, (p + 1) * group)
        out[rows_out, :main] = every[:, p * main : (p + 1) * main]
        at = pools * main + p * rest
        out[rows_out, main:] = every[:, at : at + rest]


def score_kernel(pools, group, places, table_ref, returned_ref, out_ref):
    rows_dev = out_ref.shape[1]
    arrived = jnp.transpose(
        jnp.concatenate([returned_ref[...], jnp.zeros_like(returned_ref)], axis=1)
    )
    table = table_ref[...]
    row = iota((8, rows_dev), 1)
    total = jnp.zeros((8, rows_dev), F32)
    for p in range(pools):
        for k in range(places):
            value = jnp.max(
                arrived[k * group : (k + 1) * group, p * group : (p + 1) * group],
                axis=1,
                keepdims=True,
            )
            entry = table[p * group : (p + 1) * group, k : k + 1]
            total = jnp.where(entry == row, value, total)
    out_ref[...] = jnp.sum(total, axis=0, keepdims=True)


def body(embeddings, members, valid, block_cluster):
    rows_dev, feature = embeddings.shape
    pools = lax.axis_size("pool")
    group = lax.axis_size("grp")
    devices = pools * group
    places = rows_dev // devices
    last = places // 4
    sds = jax.ShapeDtypeStruct
    hbm = pl.BlockSpec(memory_space=pltpu.HBM)
    valid_row = valid.reshape(1, -1)
    cluster_row = block_cluster.reshape(1, -1)
    blocks, block_len = members.shape

    some = jnp.any(valid > 0)
    table, main = pl.pallas_call(
        lambda *refs: table_kernel(pools, group, places, last, *refs),
        out_shape=(
            sds((devices, 128), I32),
            sds((3 * QUARTER, feature), BF16),
        ),
        in_specs=[hbm] * 3,
        scratch_shapes=[
            pltpu.VMEM((blocks, block_len), I32),
            pltpu.VMEM((1, blocks), I32),
            pltpu.VMEM((rows_dev, feature), BF16),
            pltpu.VMEM((blocks, 128), F32),
            pltpu.SemaphoreType.DMA((3,)),
        ],
        compiler_params=TABLE_PARAMS,
        cost_estimate=cost(rows_dev * rows_dev * feature),
        name="table",
    )(members, valid_row, embeddings)
    meta, codes = pl.pallas_call(
        lambda *refs: meta_kernel(group, places, last, *refs),
        out_shape=(sds((2, group, rows_dev), I32), sds((rows_dev, 128), I32)),
        in_specs=[hbm] * 3,
        scratch_shapes=[
            pltpu.VMEM((2 * group, block_len), I32),
            pltpu.VMEM((1, blocks), I32),
            pltpu.VMEM((1, blocks), I32),
            pltpu.VMEM((128, rows_dev), I32),
            pltpu.SemaphoreType.DMA((3,)),
        ],
        compiler_params=PARAMS,
        cost_estimate=cost(2 * rows_dev**3),
        name="meta",
    )(members, valid_row, cluster_row)

    def shift(rows, by):
        return lax.ppermute(rows, "grp", [(g, (g + by) % group) for g in range(group)])

    def swap(rows):
        return lax.ppermute(rows, "grp", [(g, g ^ 1) for g in range(group)])

    def follow(rows, after, also_after):
        return pl.pallas_call(
            follow_kernel,
            out_shape=sds(rows.shape, BF16),
            in_specs=[hbm] * 3,
            out_specs=hbm,
            input_output_aliases={0: 0},
            compiler_params=PARAMS,
            name="follow",
        )(rows, after, also_after)

    def to_pools(rows):
        return lax.all_to_all(rows, "pool", split_axis=0, concat_axis=0, tiled=True)

    vmem = pl.BlockSpec(memory_space=pltpu.VMEM)
    rest = pl.pallas_call(
        lambda *refs: rest_kernel(pools, places, last, *refs),
        out_shape=sds((QUARTER, feature), BF16),
        in_specs=[vmem, vmem, hbm],
        compiler_params=PARAMS,
        name="rest",
    )(table, embeddings, meta)
    low_rest, high_rest = shift(rest, 2), shift(rest, -2)
    own0 = to_pools(main.reshape(pools, -1, feature)).reshape(-1, feature)
    sent = pl.pallas_call(
        lambda *refs: join_kernel(pools, *refs),
        out_shape=sds((pools, 3 * QUARTER // pools, feature), BF16),
        compiler_params=PARAMS,
        name="join",
    )(rest, low_rest, high_rest)
    own0 = follow(own0, sent, some.astype(I32).reshape(1, 1))
    low0, high01 = shift(own0, 2), shift(own0[: 2 * QUARTER], -2)
    high2 = shift(own0[2 * QUARTER :], -2)
    sib0 = swap(own0)

    def tiles(kernel, name, squares, moves, operands, small, out_shape=(8, rows_dev), more=()):
        return pl.pallas_call(
            kernel,
            out_shape=sds(out_shape, F32),
            in_specs=[hbm] * len(operands) + [vmem] * len(small),
            scratch_shapes=[
                pltpu.VMEM((2, rows_dev, QUARTER), F32),
                pltpu.VMEM((4, rows_dev, 128), F32),
                pltpu.VMEM((5, 8, rows_dev), F32),
                pltpu.VMEM((5, rows_dev // 16, 16, feature), BF16),
                pltpu.SemaphoreType.DMA((moves,)),
                *more,
            ],
            compiler_params=PARAMS,
            cost_estimate=cost(squares * QUARTER * QUARTER * feature),
            name=name,
        )(*[operand.reshape(-1, *operand.shape[-2:]) if operand.ndim == 3 else
            operand.reshape(-1, 16, feature) for operand in operands], *small)

    def bring(sent, own0, sib0, meta, codes):
        near = tiles(near_kernel, "near", 11, 2, (own0, sib0), (meta, codes))
        return to_pools(sent), near

    def bring_nothing(sent, own0, sib0, meta, codes):
        return jnp.zeros_like(sent), jnp.zeros((8, rows_dev), F32)

    arrived, near = lax.cond(
        some, bring, bring_nothing, sent, own0, sib0, meta, codes
    )
    swapped = swap(arrived)
    middle = tiles(
        middle_kernel, "middle", 25, 5, (own0, arrived, high01, sib0), (meta, codes, near)
    )
    low0 = follow(low0, middle, high2)
    best = tiles(
        main_kernel, "main", 23, 9, (own0, arrived, high2, sib0, swapped, low0, high01),
        (meta, codes, middle),
    )
    best = tiles(
        lambda *refs: last_kernel(pools, group, group * (places - last), group * last, *refs),
        "last", 8, 5, (swap(low0), high01, high2, swapped, arrived), (meta, codes, best),
        out_shape=(devices, group * places),
        more=(pltpu.VMEM((group, rows_dev), F32),),
    )
    returned = lax.all_to_all(best, ("pool", "grp"), split_axis=0, concat_axis=0, tiled=True)
    scores = pl.pallas_call(
        lambda *refs: score_kernel(pools, group, places, *refs),
        out_shape=sds((1, rows_dev), F32),
        compiler_params=PARAMS,
        name="score",
    )(table, returned)
    return scores.reshape(rows_dev)


def cost(products):
    return pl.CostEstimate(flops=2 * products, bytes_accessed=0, transcendentals=0)


def solution(mesh):
    in_specs = (P(("pool", "grp"), None), P(), P(), P())
    out_specs = P(("pool", "grp"))
    return jax.shard_map(body, mesh=mesh, in_specs=in_specs, out_specs=out_specs, check_vma=False)
```

```python
import functools

import jax
import jax.numpy as jnp
from jax import lax
from jax.experimental import pallas as pl
from jax.experimental.pallas import tpu as pltpu
from jax.sharding import PartitionSpec as P

EPS = 1e-06
F32 = jnp.float32
BF16 = jnp.bfloat16
I32 = jnp.int32
QUARTER = 256
CODE = 8192
NT = (((1,), (1,)), ((), ()))
PARAMS = pltpu.CompilerParams(vmem_limit_bytes=12 * 1024 * 1024)
TABLE_PARAMS = pltpu.CompilerParams(vmem_limit_bytes=62 * 1024 * 1024)


def iota(shape, dim):
    return lax.broadcasted_iota(I32, shape, dim)


def normal_rows(rows):
    return (rows * lax.rsqrt(jnp.sum(rows * rows, axis=1, keepdims=True) + EPS)).astype(BF16)


def picked_rows(table, emb, first, count, pools):
    width = emb.shape[0]
    wanted = []
    for k in range(first, first + count):
        hit = table[:, k : k + 1] == iota((table.shape[0], width), 1)
        wanted.append(jnp.where(hit, 1.0, 0.0).reshape(pools, -1, width))
    choice = jnp.concatenate(wanted, axis=1).reshape(-1, width).astype(BF16)
    return normal_rows(jnp.dot(choice, emb, preferred_element_type=F32))


def table_kernel(
    pools, group, places, last, members_hbm, valid_hbm, emb_hbm, table_ref, main_ref,
    members_ref, valid_ref, emb_ref, found_ref, sems,
):
    copies = []
    for n, (source, target) in enumerate(
        ((members_hbm, members_ref), (valid_hbm, valid_ref), (emb_hbm, emb_ref))
    ):
        copies.append(pltpu.make_async_copy(source, target, sems.at[n]))
        copies[-1].start()
    rows_dev = emb_ref.shape[0]
    device = lax.axis_index("pool") * group + lax.axis_index("grp")
    blocks, block_len = members_ref.shape
    devices = blocks // 2
    before = jnp.where(
        iota((block_len, block_len), 0) < iota((block_len, block_len), 1), 1.0, 0.0
    ).astype(BF16)
    at = iota((blocks, blocks), 1) == iota((blocks, blocks), 0)
    copies[0].wait()
    copies[1].wait()
    live = jnp.sum(jnp.where(at, valid_ref[...], 0), axis=1, keepdims=True)
    local = members_ref[...] - device * rows_dev
    mine = (local >= 0) & (local < rows_dev) & (iota((blocks, block_len), 1) < live)
    ones = jnp.where(mine, 1.0, 0.0)
    counts = jnp.broadcast_to(jnp.sum(ones, axis=1, keepdims=True), (blocks, 128))
    counts = jnp.where(iota((blocks, 128), 0) % 2 == 1, pltpu.roll(counts, 1, 0), 0.0)
    rank = jnp.dot(ones.astype(BF16), before, preferred_element_type=F32) + counts[:, :1]
    rank = jnp.where(mine, rank, -1.0)
    value = (local + 1).astype(F32)
    lane = iota((blocks, 128), 1)
    found = jnp.zeros((blocks, 128), F32)
    for k in range(places):
        entry = jnp.sum(jnp.where(rank == k, value, 0.0), axis=1, keepdims=True)
        found = jnp.where(lane == k, entry, found)
    found_ref[...] = found
    pair = found_ref[pl.ds(0, devices, stride=2), :] + found_ref[pl.ds(1, devices, stride=2), :]
    table = pair.astype(I32) - 1
    table_ref[...] = table
    copies[2].wait()
    main_ref[...] = picked_rows(table, emb_ref[...], 0, places - last, pools)


def rest_kernel(pools, places, last, table_ref, emb_ref, after, out):
    del after
    out[...] = picked_rows(table_ref[...], emb_ref[...], places - last, last, pools)


def relatives():
    group = lax.axis_size("grp")
    index = lax.axis_index("grp")
    flip = 1 - 2 * (index % 2)
    below = (index + group - 2) % group
    return index, index + flip, below, below + flip, (index + 2) % group


def meta_kernel(
    group, places, last, members_hbm, valid_hbm, cluster_hbm, out_ref, codes_ref,
    members_ref, valid_ref, cluster_ref, packed_ref, sems,
):
    blocks = valid_ref.shape[1]
    block_len = members_ref.shape[1]
    pool = lax.axis_index("pool")
    first_block = pl.multiple_of(pool * 2 * group, 2 * group)
    copies = []
    for n, (source, target) in enumerate(
        (
            (members_hbm.at[pl.ds(first_block, 2 * group), :], members_ref),
            (valid_hbm, valid_ref),
            (cluster_hbm, cluster_ref),
        )
    ):
        copies.append(pltpu.make_async_copy(source, target, sems.at[n]))
        copies[-1].start()
    sources = blocks // 2
    slots = 2 * block_len
    width = group * places
    before = jnp.where(iota((slots, slots), 0) < iota((slots, slots), 1), 1.0, 0.0).astype(BF16)
    slot = iota((1, slots), 1)
    kind = iota((2 * width, slots), 0)
    kind_place = kind % width // group
    kind_owner = kind % group
    kind_value = jnp.where(kind < width, slot // 32, slot % 32 + 1)
    found = jnp.zeros((sources, 2 * width), F32)
    block_lane = iota((1, blocks), 1)
    lane = iota((1, width), 1)
    first_cluster = jnp.zeros((1, width), I32)
    second_cluster = jnp.zeros((1, width), I32)
    for copy in copies:
        copy.wait()
    for owner in range(group):
        halves, lives = [], []
        for half in range(2):
            halves.append(members_ref[2 * owner + half : 2 * owner + half + 1, :])
            at = block_lane == first_block + 2 * owner + half
            lives.append(jnp.sum(jnp.where(at, valid_ref[...], 0), axis=1, keepdims=True))
            cluster = jnp.sum(jnp.where(at, cluster_ref[...], 0), axis=1, keepdims=True)
            if half == 0:
                first_cluster = jnp.where(lane % group == owner, cluster, first_cluster)
            else:
                second_cluster = jnp.where(lane % group == owner, cluster, second_cluster)
        rows = jnp.concatenate(halves, axis=1)
        end = jnp.where(slot < block_len, lives[0], block_len + lives[1])
        origin = jnp.where(slot < end, rows // slots, -1)
        match = iota((sources, slots), 0) == origin
        ones = jnp.where(match, 1.0, 0.0).astype(BF16)
        ranks = jnp.dot(ones, before, preferred_element_type=F32)
        rank = jnp.sum(jnp.where(match, ranks, 0.0), axis=0, keepdims=True).astype(I32)
        weight = jnp.where((kind_owner == owner) & (kind_place == rank), kind_value, 0)
        found = found + lax.dot_general(
            ones, weight.astype(F32).astype(BF16), NT, preferred_element_type=F32
        )
    found = found.astype(I32)
    place = found[:, :width] * 32 + found[:, width:] - 1
    filled = found[:, width:] > 0
    position = jnp.where(filled, place + lane % group * slots, -1)
    cluster = jnp.where(filled, jnp.where(place < block_len, first_cluster, second_cluster), -1)
    main = (places - last) * group
    rest = last * group
    pools = sources // group
    for n, values in enumerate((position, cluster)):
        for p in range(pools):
            own = values[p * group : (p + 1) * group, :]
            out_ref[n, :, p * main : (p + 1) * main] = own[:, :main]
            at = pools * main + p * rest
            out_ref[n, :, at : at + rest] = own[:, main:]
    packed_ref[...] = jnp.zeros(packed_ref.shape, I32)
    for n, cls in enumerate(relatives()[:4]):
        pos = out_ref[0, pl.ds(cls, 1), :]
        cluster = out_ref[1, pl.ds(cls, 1), :]
        packed_ref[n : n + 1, :] = jnp.where(cluster < 0, -2 * CODE, cluster * CODE + pos)
    codes_ref[...] = jnp.transpose(packed_ref[...])


def run(pieces, sims_ref):
    for n in range(len(pieces) + 1):
        if n < len(pieces):
            piece = pieces[n]
            sims_ref[n % 2, : piece["count"], :] = lax.dot_general(
                piece["left"](), piece["right"](), NT, preferred_element_type=F32
            )
        if n > 0:
            take_maxima(sims_ref.at[(n - 1) % 2], **pieces[n - 1])


def take_maxima(sims_ref, left, right, count, codes, cls, rows, start, pos_row, cluster_row, col, col_start, same):
    step = 128
    right_pos, right_cluster = pos_row(), cluster_row()
    parts = QUARTER // 128
    best_col = [jnp.zeros((8, 128), F32) for _ in range(parts)]
    for top in range(0, count, step):
        code = codes[start + top : start + top + step, cls : cls + 1]
        code = jnp.broadcast_to(code, (step, 128))
        pos = code & (CODE - 1)
        cluster = code >> 13
        best = rows[start + top : start + top + step, :]
        for part in range(parts):
            lanes = slice(part * 128, part * 128 + 128)
            sims = sims_ref[top : top + step, lanes]
            sims = jnp.where(cluster == right_cluster[:, lanes], sims, 0.0)
            earlier = right_pos[:, lanes] < pos
            best = jnp.maximum(best, jnp.where(earlier, sims, 0.0))
            if top < same:
                later = jnp.where(earlier, 0.0, sims)
                best_col[part] = jnp.maximum(
                    best_col[part], jnp.max(later.reshape(-1, 8, 128), axis=0)
                )
        rows[start + top : start + top + step, :] = best
    if same > 0:
        for part in range(parts):
            lanes = slice(col_start + part * 128, col_start + part * 128 + 128)
            col[:, lanes] = jnp.maximum(col[:, lanes], best_col[part])


def row_result(row_ref):
    return jnp.max(jnp.transpose(row_ref[...]), axis=0, keepdims=True)


def col_result(col_ref):
    return jnp.max(col_ref[...], axis=0, keepdims=True)


OWN, SIB, LOW, LOWS, HIGH = range(5)


class Tiles:
    def __init__(self, parts, meta, codes, rows, cols, row_classes, col_classes):
        self.meta, self.codes, self.rows, self.cols = meta, codes, rows, cols
        self.row_classes, self.col_classes = row_classes, col_classes
        self.relatives = relatives()
        self.parts = {}
        for cls, ref, at, quarter, count in parts:
            for q in range(quarter, quarter + count):
                self.parts[cls, q] = (ref, at if len(ref.shape) == 3 else (q - quarter) * QUARTER)
        for cls in row_classes:
            rows[cls, :, :] = jnp.zeros(rows.shape[1:], F32)
        for cls in col_classes:
            cols[cls, :, :] = jnp.zeros(cols.shape[1:], F32)

    def load(self, cls, quarter, count=1):
        ref, at = self.parts[cls, quarter]
        if len(ref.shape) == 3:
            return ref[:, at : at + QUARTER // ref.shape[0], :].reshape(QUARTER, -1)
        return ref[at : at + count * QUARTER, :]

    def piece(self, left, quarter, count, right, right_quarter, same=None):
        lanes = slice(right_quarter * QUARTER, (right_quarter + 1) * QUARTER)
        place = self.relatives[right]
        return dict(
            left=lambda: self.load(left, quarter, count),
            right=lambda: self.load(right, right_quarter),
            count=count * QUARTER,
            codes=self.codes,
            cls=left,
            rows=self.rows.at[left],
            start=quarter * QUARTER,
            pos_row=lambda: self.meta[0, pl.ds(place, 1), lanes],
            cluster_row=lambda: self.meta[1, pl.ds(place, 1), lanes],
            col=self.cols.at[right],
            col_start=right_quarter * QUARTER,
            same=count * QUARTER if same is None else same,
        )

    def matched(self, flip, left, right, pairs):
        pieces = []
        for b in range(4):
            mine = [a for a in range(4) if (a, b) in pairs and (a // 2 + b // 2) % 2 == flip]
            if mine == [0, 1] and self.parts[left, 0][0] is self.parts[left, 1][0]:
                pieces.append(self.piece(left, 0, 2, right, b))
            else:
                pieces += [self.piece(left, a, 1, right, b) for a in mine]
        return pieces

    def result(self, cls):
        best = []
        if cls in self.row_classes:
            best.append(row_result(self.rows.at[cls]))
        if cls in self.col_classes:
            best.append(col_result(self.cols.at[cls]))
        return functools.reduce(jnp.maximum, best)


def either(flag, work):
    pl.when(flag)(lambda: work(1))
    pl.when(jnp.logical_not(flag))(lambda: work(0))


def second_core():
    return lax.axis_index("grp") % 2 == 1


def outer_chip():
    chip = lax.axis_index("grp") // 2
    return (chip == 0) | (chip == 3)


ALL_PAIRS = [(a, b) for a in range(4) for b in range(4)]


def follow_kernel(rows, after, also_after, out):
    del rows, after, also_after, out


def split_kernel(rows, after, also_after, out, first, third, sems):
    del after, also_after, out
    parts = ((first, 0, 2), (third, 2, 1))
    copies = [
        pltpu.make_async_copy(rows.at[pl.ds(at * QUARTER, n * QUARTER), :], part, sems.at[i])
        for i, (part, at, n) in enumerate(parts)
    ]
    for copy in copies:
        copy.start()
    for copy in copies:
        copy.wait()


def join_kernel(pools, rest, low_rest, high_rest, out):
    width = QUARTER // pools
    for n, part in enumerate((rest, low_rest, high_rest)):
        out[:, n * width : (n + 1) * width, :] = part[...].reshape(pools, width, -1)


def near_kernel(own0, sib0, meta, codes, out, sims, rows, cols):
    moves = [(OWN, own0, None, 0, 3), (SIB, sib0, None, 0, 3)]
    tiles = Tiles(
        moves, meta, codes, rows, cols, (OWN,), (OWN, SIB))
    run([tiles.piece(OWN, 0, b + 1, OWN, b, same=b * QUARTER) for b in range(3)], sims)
    pairs = [(a, b) for a, b in ALL_PAIRS if 3 not in (a, b)]
    either(second_core(), lambda flip: run(tiles.matched(flip, OWN, SIB, pairs), sims))
    out[...] = jnp.zeros(out.shape, F32)
    for cls in (OWN, SIB):
        out[cls : cls + 1, :] = tiles.result(cls)


def middle_kernel(
    own0, arrived, high01, sib0, meta, codes, near, out, sims, rows, cols
):
    width = arrived.shape[1] // 3
    moves = [
        (OWN, own0, None, 0, 3), (OWN, arrived, 0, 3, 1), (HIGH, high01, None, 0, 2),
        (HIGH, arrived, 2 * width, 3, 1), (SIB, sib0, None, 0, 3),
    ]
    tiles = Tiles(
        moves, meta, codes, rows, cols, (OWN, SIB), (OWN, HIGH))
    pieces = [tiles.piece(OWN, 0, 3, OWN, 3), tiles.piece(OWN, 3, 1, OWN, 3, same=0)]
    for b in (0, 1, 3):
        pieces += [tiles.piece(OWN, 0, 3, HIGH, b), tiles.piece(OWN, 3, 1, HIGH, b)]
    pieces += [tiles.piece(SIB, 0, 3, HIGH, b) for b in (0, 1, 3)]
    run(pieces, sims)
    out[...] = near[...]
    for cls in (OWN, SIB, HIGH):
        out[cls : cls + 1, :] = jnp.maximum(near[cls : cls + 1, :], tiles.result(cls))


def main_kernel(
    own0, arrived, high2, sib0, swapped, low0, high01, meta, codes, before, out,
    sims, rows, cols,
):
    width = arrived.shape[1] // 3
    moves = [
        (HIGH, high2, None, 2, 1), (OWN, own0, None, 0, 3), (OWN, arrived, 0, 3, 1),
        (SIB, sib0, None, 0, 3), (SIB, swapped, 0, 3, 1), (HIGH, high01, None, 0, 2),
        (HIGH, arrived, 2 * width, 3, 1), (LOW, low0, None, 0, 3), (LOW, arrived, width, 3, 1),
    ]
    tiles = Tiles(
        moves, meta, codes, rows, cols, (OWN, SIB, LOW), (SIB, HIGH)
    )
    pieces = [tiles.piece(cls, 0, 3, HIGH, 2) for cls in (OWN, SIB)]
    pieces += [tiles.piece(OWN, 3, 1, HIGH, 2)]
    pieces += [tiles.piece(SIB, 3, 1, HIGH, b) for b in range(4)]
    run(pieces, sims)
    pairs = [(a, b) for a, b in ALL_PAIRS if 3 in (a, b)]
    either(second_core(), lambda flip: run(tiles.matched(flip, OWN, SIB, pairs), sims))
    either(outer_chip(), lambda flip: run(tiles.matched(flip, LOW, HIGH, ALL_PAIRS), sims))
    for cls in (OWN, SIB, LOW, HIGH):
        out[cls : cls + 1, :] = jnp.maximum(before[cls : cls + 1, :], tiles.result(cls))


def last_kernel(
    pools, group, main, rest, lows0, high01, high2, swapped, arrived, meta, codes, before, out,
    sims, rows, cols, every,
):
    width = arrived.shape[1] // 3
    moves = [
        (LOWS, lows0, None, 0, 3), (LOWS, swapped, width, 3, 1), (HIGH, high01, None, 0, 2),
        (HIGH, high2, None, 2, 1), (HIGH, arrived, 2 * width, 3, 1),
    ]
    tiles = Tiles(
        moves, meta, codes, rows, cols, (LOWS,), (HIGH,))
    either(outer_chip(), lambda flip: run(tiles.matched(flip, LOWS, HIGH, ALL_PAIRS), sims))
    every[...] = jnp.zeros(every.shape, F32)
    for cls, place in enumerate(tiles.relatives):
        best = [] if cls == LOWS else [before[cls : cls + 1, :]]
        if cls in (LOWS, HIGH):
            best.append(tiles.result(cls))
        every[pl.ds(place, 1), :] = functools.reduce(jnp.maximum, best)
    for p in range(pools):
        rows_out = slice(p * group, (p + 1) * group)
        out[rows_out, :main] = every[:, p * main : (p + 1) * main]
        at = pools * main + p * rest
        out[rows_out, main:] = every[:, at : at + rest]


def score_kernel(pools, group, places, table_ref, returned_ref, out_ref):
    rows_dev = out_ref.shape[1]
    arrived = jnp.transpose(
        jnp.concatenate([returned_ref[...], jnp.zeros_like(returned_ref)], axis=1)
    )
    table = table_ref[...]
    row = iota((8, rows_dev), 1)
    total = jnp.zeros((8, rows_dev), F32)
    for p in range(pools):
        for k in range(places):
            value = jnp.max(
                arrived[k * group : (k + 1) * group, p * group : (p + 1) * group],
                axis=1,
                keepdims=True,
            )
            entry = table[p * group : (p + 1) * group, k : k + 1]
            total = jnp.where(entry == row, value, total)
    out_ref[...] = jnp.sum(total, axis=0, keepdims=True)


def body(embeddings, members, valid, block_cluster):
    rows_dev, feature = embeddings.shape
    pools = lax.axis_size("pool")
    group = lax.axis_size("grp")
    devices = pools * group
    places = rows_dev // devices
    last = places // 4
    sds = jax.ShapeDtypeStruct
    hbm = pl.BlockSpec(memory_space=pltpu.HBM)
    valid_row = valid.reshape(1, -1)
    cluster_row = block_cluster.reshape(1, -1)
    blocks, block_len = members.shape

    some = jnp.any(valid > 0)
    table, main = pl.pallas_call(
        lambda *refs: table_kernel(pools, group, places, last, *refs),
        out_shape=(
            sds((devices, 128), I32),
            sds((3 * QUARTER, feature), BF16),
        ),
        in_specs=[hbm] * 3,
        scratch_shapes=[
            pltpu.VMEM((blocks, block_len), I32),
            pltpu.VMEM((1, blocks), I32),
            pltpu.VMEM((rows_dev, feature), BF16),
            pltpu.VMEM((blocks, 128), F32),
            pltpu.SemaphoreType.DMA((3,)),
        ],
        compiler_params=TABLE_PARAMS,
        cost_estimate=cost(rows_dev * rows_dev * feature),
        name="table",
    )(members, valid_row, embeddings)
    meta, codes = pl.pallas_call(
        lambda *refs: meta_kernel(group, places, last, *refs),
        out_shape=(sds((2, group, rows_dev), I32), sds((rows_dev, 128), I32)),
        in_specs=[hbm] * 3,
        scratch_shapes=[
            pltpu.VMEM((2 * group, block_len), I32),
            pltpu.VMEM((1, blocks), I32),
            pltpu.VMEM((1, blocks), I32),
            pltpu.VMEM((128, rows_dev), I32),
            pltpu.SemaphoreType.DMA((3,)),
        ],
        compiler_params=PARAMS,
        cost_estimate=cost(2 * rows_dev**3),
        name="meta",
    )(members, valid_row, cluster_row)

    def shift(rows, by):
        return lax.ppermute(rows, "grp", [(g, (g + by) % group) for g in range(group)])

    def swap(rows):
        return lax.ppermute(rows, "grp", [(g, g ^ 1) for g in range(group)])

    def follow(rows, after, also_after):
        return pl.pallas_call(
            follow_kernel,
            out_shape=sds(rows.shape, BF16),
            in_specs=[hbm] * 3,
            out_specs=hbm,
            input_output_aliases={0: 0},
            compiler_params=PARAMS,
            name="follow",
        )(rows, after, also_after)

    def to_pools(rows):
        return lax.all_to_all(rows, "pool", split_axis=0, concat_axis=0, tiled=True)

    vmem = pl.BlockSpec(memory_space=pltpu.VMEM)
    rest = pl.pallas_call(
        lambda *refs: rest_kernel(pools, places, last, *refs),
        out_shape=sds((QUARTER, feature), BF16),
        in_specs=[vmem, vmem, hbm],
        compiler_params=PARAMS,
        name="rest",
    )(table, embeddings, meta)
    low_rest, high_rest = shift(rest, 2), shift(rest, -2)
    own0 = to_pools(main.reshape(pools, -1, feature)).reshape(-1, feature)
    sent = pl.pallas_call(
        lambda *refs: join_kernel(pools, *refs),
        out_shape=sds((pools, 3 * QUARTER // pools, feature), BF16),
        compiler_params=PARAMS,
        name="join",
    )(rest, low_rest, high_rest)
    own0, own01, own2 = pl.pallas_call(
        split_kernel,
        out_shape=tuple(sds((n * QUARTER, feature), BF16) for n in (3, 2, 1)),
        in_specs=[hbm] * 3,
        out_specs=(hbm, hbm, hbm),
        input_output_aliases={0: 0},
        scratch_shapes=[pltpu.SemaphoreType.DMA((2,))],
        compiler_params=PARAMS,
        name="split",
    )(own0, sent, some.astype(I32).reshape(1, 1))
    low0, high01, high2 = shift(own0, 2), shift(own01, -2), shift(own2, -2)
    sib0 = swap(own0)

    def tiles(kernel, name, squares, operands, small, out_shape=(8, rows_dev), more=()):
        return pl.pallas_call(
            kernel,
            out_shape=sds(out_shape, F32),
            scratch_shapes=[
                pltpu.VMEM((2, 3 * QUARTER, QUARTER), F32),
                pltpu.VMEM((4, rows_dev, 128), F32),
                pltpu.VMEM((5, 8, rows_dev), F32),
                *more,
            ],
            compiler_params=PARAMS,
            cost_estimate=cost(squares * QUARTER * QUARTER * feature),
            name=name,
        )(*operands, *small)

    def bring(sent, own0, sib0, meta, codes):
        near = tiles(near_kernel, "near", 11, (own0, sib0), (meta, codes))
        return to_pools(sent), near

    def bring_nothing(sent, own0, sib0, meta, codes):
        return jnp.zeros_like(sent), jnp.zeros((8, rows_dev), F32)

    arrived, near = lax.cond(
        some, bring, bring_nothing, sent, own0, sib0, meta, codes
    )
    swapped = swap(arrived)
    middle = tiles(
        middle_kernel, "middle", 25, (own0, arrived, high01, sib0), (meta, codes, near)
    )
    low0 = follow(low0, middle, high2)
    best = tiles(
        main_kernel, "main", 23, (own0, arrived, high2, sib0, swapped, low0, high01),
        (meta, codes, middle),
    )
    best = tiles(
        lambda *refs: last_kernel(pools, group, group * (places - last), group * last, *refs),
        "last", 8, (swap(low0), high01, high2, swapped, arrived), (meta, codes, best),
        out_shape=(devices, group * places),
        more=(pltpu.VMEM((group, rows_dev), F32),),
    )
    returned = lax.all_to_all(best, ("pool", "grp"), split_axis=0, concat_axis=0, tiled=True)
    scores = pl.pallas_call(
        lambda *refs: score_kernel(pools, group, places, *refs),
        out_shape=sds((1, rows_dev), F32),
        compiler_params=PARAMS,
        name="score",
    )(table, returned)
    return scores.reshape(rows_dev)


def cost(products):
    return pl.CostEstimate(flops=2 * products, bytes_accessed=0, transcendentals=0)


def solution(mesh):
    in_specs = (P(("pool", "grp"), None), P(), P(), P())
    out_specs = P(("pool", "grp"))
    return jax.shard_map(body, mesh=mesh, in_specs=in_specs, out_specs=out_specs, check_vma=False)
```

```python
import functools

import jax
import jax.numpy as jnp
from jax import lax
from jax.experimental import pallas as pl
from jax.experimental.pallas import tpu as pltpu
from jax.sharding import PartitionSpec as P

EPS = 1e-06
F32 = jnp.float32
BF16 = jnp.bfloat16
I32 = jnp.int32
QUARTER = 256
CODE = 8192
NT = (((1,), (1,)), ((), ()))
PARAMS = pltpu.CompilerParams(vmem_limit_bytes=12 * 1024 * 1024)
TABLE_PARAMS = pltpu.CompilerParams(vmem_limit_bytes=62 * 1024 * 1024)


def iota(shape, dim):
    return lax.broadcasted_iota(I32, shape, dim)


def normal_rows(rows):
    return (rows * lax.rsqrt(jnp.sum(rows * rows, axis=1, keepdims=True) + EPS)).astype(BF16)


def picked_rows(table, emb, first, count, pools):
    width = emb.shape[0]
    wanted = []
    for k in range(first, first + count):
        hit = table[:, k : k + 1] == iota((table.shape[0], width), 1)
        wanted.append(jnp.where(hit, 1.0, 0.0).reshape(pools, -1, width))
    choice = jnp.concatenate(wanted, axis=1).reshape(-1, width).astype(BF16)
    return normal_rows(jnp.dot(choice, emb, preferred_element_type=F32))


def table_kernel(
    pools, group, places, last, members_hbm, valid_hbm, emb_hbm, table_ref, main_ref,
    members_ref, valid_ref, emb_ref, found_ref, sems,
):
    copies = []
    for n, (source, target) in enumerate(
        ((members_hbm, members_ref), (valid_hbm, valid_ref), (emb_hbm, emb_ref))
    ):
        copies.append(pltpu.make_async_copy(source, target, sems.at[n]))
        copies[-1].start()
    rows_dev = emb_ref.shape[0]
    device = lax.axis_index("pool") * group + lax.axis_index("grp")
    blocks, block_len = members_ref.shape
    devices = blocks // 2
    before = jnp.where(
        iota((block_len, block_len), 0) < iota((block_len, block_len), 1), 1.0, 0.0
    ).astype(BF16)
    at = iota((blocks, blocks), 1) == iota((blocks, blocks), 0)
    copies[0].wait()
    copies[1].wait()
    live = jnp.sum(jnp.where(at, valid_ref[...], 0), axis=1, keepdims=True)
    local = members_ref[...] - device * rows_dev
    mine = (local >= 0) & (local < rows_dev) & (iota((blocks, block_len), 1) < live)
    ones = jnp.where(mine, 1.0, 0.0)
    counts = jnp.broadcast_to(jnp.sum(ones, axis=1, keepdims=True), (blocks, 128))
    counts = jnp.where(iota((blocks, 128), 0) % 2 == 1, pltpu.roll(counts, 1, 0), 0.0)
    rank = jnp.dot(ones.astype(BF16), before, preferred_element_type=F32) + counts[:, :1]
    rank = jnp.where(mine, rank, -1.0)
    value = (local + 1).astype(F32)
    lane = iota((blocks, 128), 1)
    found = jnp.zeros((blocks, 128), F32)
    for k in range(places):
        entry = jnp.sum(jnp.where(rank == k, value, 0.0), axis=1, keepdims=True)
        found = jnp.where(lane == k, entry, found)
    found_ref[...] = found
    pair = found_ref[pl.ds(0, devices, stride=2), :] + found_ref[pl.ds(1, devices, stride=2), :]
    table = pair.astype(I32) - 1
    table_ref[...] = table
    copies[2].wait()
    main_ref[...] = picked_rows(table, emb_ref[...], 0, places - last, pools)


def rest_kernel(pools, places, last, table_ref, emb_ref, after, out):
    del after
    out[...] = picked_rows(table_ref[...], emb_ref[...], places - last, last, pools)


def relatives():
    group = lax.axis_size("grp")
    index = lax.axis_index("grp")
    flip = 1 - 2 * (index % 2)
    below = (index + group - 2) % group
    return index, index + flip, below, below + flip, (index + 2) % group


def meta_kernel(
    group, places, last, members_hbm, valid_hbm, cluster_hbm, out_ref, codes_ref,
    members_ref, valid_ref, cluster_ref, packed_ref, sems,
):
    blocks = valid_ref.shape[1]
    block_len = members_ref.shape[1]
    pool = lax.axis_index("pool")
    first_block = pl.multiple_of(pool * 2 * group, 2 * group)
    copies = []
    for n, (source, target) in enumerate(
        (
            (members_hbm.at[pl.ds(first_block, 2 * group), :], members_ref),
            (valid_hbm, valid_ref),
            (cluster_hbm, cluster_ref),
        )
    ):
        copies.append(pltpu.make_async_copy(source, target, sems.at[n]))
        copies[-1].start()
    sources = blocks // 2
    slots = 2 * block_len
    width = group * places
    before = jnp.where(iota((slots, slots), 0) < iota((slots, slots), 1), 1.0, 0.0).astype(BF16)
    slot = iota((1, slots), 1)
    kind = iota((2 * width, slots), 0)
    kind_place = kind % width // group
    kind_owner = kind % group
    kind_value = jnp.where(kind < width, slot // 32, slot % 32 + 1)
    found = jnp.zeros((sources, 2 * width), F32)
    block_lane = iota((1, blocks), 1)
    lane = iota((1, width), 1)
    first_cluster = jnp.zeros((1, width), I32)
    second_cluster = jnp.zeros((1, width), I32)
    for copy in copies:
        copy.wait()
    for owner in range(group):
        halves, lives = [], []
        for half in range(2):
            halves.append(members_ref[2 * owner + half : 2 * owner + half + 1, :])
            at = block_lane == first_block + 2 * owner + half
            lives.append(jnp.sum(jnp.where(at, valid_ref[...], 0), axis=1, keepdims=True))
            cluster = jnp.sum(jnp.where(at, cluster_ref[...], 0), axis=1, keepdims=True)
            if half == 0:
                first_cluster = jnp.where(lane % group == owner, cluster, first_cluster)
            else:
                second_cluster = jnp.where(lane % group == owner, cluster, second_cluster)
        rows = jnp.concatenate(halves, axis=1)
        end = jnp.where(slot < block_len, lives[0], block_len + lives[1])
        origin = jnp.where(slot < end, rows // slots, -1)
        match = iota((sources, slots), 0) == origin
        ones = jnp.where(match, 1.0, 0.0).astype(BF16)
        ranks = jnp.dot(ones, before, preferred_element_type=F32)
        rank = jnp.sum(jnp.where(match, ranks, 0.0), axis=0, keepdims=True).astype(I32)
        weight = jnp.where((kind_owner == owner) & (kind_place == rank), kind_value, 0)
        found = found + lax.dot_general(
            ones, weight.astype(F32).astype(BF16), NT, preferred_element_type=F32
        )
    found = found.astype(I32)
    place = found[:, :width] * 32 + found[:, width:] - 1
    filled = found[:, width:] > 0
    position = jnp.where(filled, place + lane % group * slots, -1)
    cluster = jnp.where(filled, jnp.where(place < block_len, first_cluster, second_cluster), -1)
    main = (places - last) * group
    rest = last * group
    pools = sources // group
    for n, values in enumerate((position, cluster)):
        for p in range(pools):
            own = values[p * group : (p + 1) * group, :]
            out_ref[n, :, p * main : (p + 1) * main] = own[:, :main]
            at = pools * main + p * rest
            out_ref[n, :, at : at + rest] = own[:, main:]
    packed_ref[...] = jnp.zeros(packed_ref.shape, I32)
    for n, cls in enumerate(relatives()[:4]):
        pos = out_ref[0, pl.ds(cls, 1), :]
        cluster = out_ref[1, pl.ds(cls, 1), :]
        packed_ref[n : n + 1, :] = jnp.where(cluster < 0, -2 * CODE, cluster * CODE + pos)
    codes_ref[...] = jnp.transpose(packed_ref[...])


def run(pieces, sims_ref):
    for n in range(len(pieces) + 1):
        if n < len(pieces):
            piece = pieces[n]
            sims_ref[n % 2, : piece["count"], :] = lax.dot_general(
                piece["left"](), piece["right"](), NT, preferred_element_type=F32
            )
        if n > 0:
            take_maxima(sims_ref.at[(n - 1) % 2], **pieces[n - 1])


def take_maxima(sims_ref, left, right, count, codes, cls, rows, start, pos_row, cluster_row, col, col_start, same):
    step = 128
    right_pos, right_cluster = pos_row(), cluster_row()
    parts = QUARTER // 128
    best_col = [jnp.zeros((8, 128), F32) for _ in range(parts)]
    for top in range(0, count, step):
        code = codes[start + top : start + top + step, cls : cls + 1]
        code = jnp.broadcast_to(code, (step, 128))
        pos = code & (CODE - 1)
        cluster = code >> 13
        best = rows[start + top : start + top + step, :]
        for part in range(parts):
            lanes = slice(part * 128, part * 128 + 128)
            sims = sims_ref[top : top + step, lanes]
            sims = jnp.where(cluster == right_cluster[:, lanes], sims, 0.0)
            earlier = right_pos[:, lanes] < pos
            best = jnp.maximum(best, jnp.where(earlier, sims, 0.0))
            if top < same:
                later = jnp.where(earlier, 0.0, sims)
                best_col[part] = jnp.maximum(
                    best_col[part], jnp.max(later.reshape(-1, 8, 128), axis=0)
                )
        rows[start + top : start + top + step, :] = best
    if same > 0:
        for part in range(parts):
            lanes = slice(col_start + part * 128, col_start + part * 128 + 128)
            col[:, lanes] = jnp.maximum(col[:, lanes], best_col[part])


def row_result(row_ref):
    return jnp.max(jnp.transpose(row_ref[...]), axis=0, keepdims=True)


def col_result(col_ref):
    return jnp.max(col_ref[...], axis=0, keepdims=True)


OWN, SIB, LOW, LOWS, HIGH = range(5)


class Tiles:
    def __init__(self, parts, meta, codes, rows, cols, row_classes, col_classes):
        self.meta, self.codes, self.rows, self.cols = meta, codes, rows, cols
        self.row_classes, self.col_classes = row_classes, col_classes
        self.relatives = relatives()
        self.parts = {}
        for cls, ref, at, quarter, count in parts:
            for q in range(quarter, quarter + count):
                self.parts[cls, q] = (ref, at if len(ref.shape) == 3 else (q - quarter) * QUARTER)
        for cls in row_classes:
            rows[cls, :, :] = jnp.zeros(rows.shape[1:], F32)
        for cls in col_classes:
            cols[cls, :, :] = jnp.zeros(cols.shape[1:], F32)

    def load(self, cls, quarter, count=1):
        ref, at = self.parts[cls, quarter]
        if len(ref.shape) == 3:
            return ref[:, at : at + QUARTER // ref.shape[0], :].reshape(QUARTER, -1)
        return ref[at : at + count * QUARTER, :]

    def piece(self, left, quarter, count, right, right_quarter, same=None):
        lanes = slice(right_quarter * QUARTER, (right_quarter + 1) * QUARTER)
        place = self.relatives[right]
        return dict(
            left=lambda: self.load(left, quarter, count),
            right=lambda: self.load(right, right_quarter),
            count=count * QUARTER,
            codes=self.codes,
            cls=left,
            rows=self.rows.at[left],
            start=quarter * QUARTER,
            pos_row=lambda: self.meta[0, pl.ds(place, 1), lanes],
            cluster_row=lambda: self.meta[1, pl.ds(place, 1), lanes],
            col=self.cols.at[right],
            col_start=right_quarter * QUARTER,
            same=count * QUARTER if same is None else same,
        )

    def matched(self, flip, left, right, pairs):
        pieces = []
        for b in range(4):
            mine = [a for a in range(4) if (a, b) in pairs and (a // 2 + b // 2) % 2 == flip]
            if mine == [0, 1] and self.parts[left, 0][0] is self.parts[left, 1][0]:
                pieces.append(self.piece(left, 0, 2, right, b))
            else:
                pieces += [self.piece(left, a, 1, right, b) for a in mine]
        return pieces

    def result(self, cls):
        best = []
        if cls in self.row_classes:
            best.append(row_result(self.rows.at[cls]))
        if cls in self.col_classes:
            best.append(col_result(self.cols.at[cls]))
        return functools.reduce(jnp.maximum, best)


def either(flag, work):
    pl.when(flag)(lambda: work(1))
    pl.when(jnp.logical_not(flag))(lambda: work(0))


def second_core():
    return lax.axis_index("grp") % 2 == 1


def outer_chip():
    chip = lax.axis_index("grp") // 2
    return (chip == 0) | (chip == 3)


ALL_PAIRS = [(a, b) for a in range(4) for b in range(4)]


def follow_kernel(rows, after, also_after, out):
    del rows, after, also_after, out


def split_kernel(rows, after, also_after, out, first, third, sems):
    del after, also_after, out
    parts = ((first, 0, 2), (third, 2, 1))
    copies = [
        pltpu.make_async_copy(rows.at[pl.ds(at * QUARTER, n * QUARTER), :], part, sems.at[i])
        for i, (part, at, n) in enumerate(parts)
    ]
    for copy in copies:
        copy.start()
    for copy in copies:
        copy.wait()


def join_kernel(pools, rest, low_rest, high_rest, out):
    width = QUARTER // pools
    for n, part in enumerate((rest, low_rest, high_rest)):
        out[:, n * width : (n + 1) * width, :] = part[...].reshape(pools, width, -1)


def near_kernel(own0, sib0, meta, codes, out, sims, rows, cols):
    moves = [(OWN, own0, None, 0, 3), (SIB, sib0, None, 0, 3)]
    tiles = Tiles(
        moves, meta, codes, rows, cols, (OWN,), (OWN, SIB))
    run([tiles.piece(OWN, 0, b + 1, OWN, b, same=b * QUARTER) for b in range(3)], sims)
    pairs = [(a, b) for a, b in ALL_PAIRS if 3 not in (a, b)]
    either(second_core(), lambda flip: run(tiles.matched(flip, OWN, SIB, pairs), sims))
    out[...] = jnp.zeros(out.shape, F32)
    for cls in (OWN, SIB):
        out[cls : cls + 1, :] = tiles.result(cls)


def middle_kernel(
    own0, arrived, high01, sib0, meta, codes, near, out, sims, rows, cols
):
    width = arrived.shape[1] // 3
    moves = [
        (OWN, own0, None, 0, 3), (OWN, arrived, 0, 3, 1), (HIGH, high01, None, 0, 2),
        (HIGH, arrived, 2 * width, 3, 1), (SIB, sib0, None, 0, 3),
    ]
    tiles = Tiles(
        moves, meta, codes, rows, cols, (OWN, SIB), (OWN, HIGH))
    pieces = [tiles.piece(OWN, 0, 3, OWN, 3), tiles.piece(OWN, 3, 1, OWN, 3, same=0)]
    for b in (0, 1, 3):
        pieces += [tiles.piece(OWN, 0, 3, HIGH, b), tiles.piece(OWN, 3, 1, HIGH, b)]
    pieces += [tiles.piece(SIB, 0, 3, HIGH, b) for b in (0, 1, 3)]
    run(pieces, sims)
    out[...] = near[...]
    for cls in (OWN, SIB, HIGH):
        out[cls : cls + 1, :] = jnp.maximum(near[cls : cls + 1, :], tiles.result(cls))


def main_kernel(
    own0, arrived, high2, sib0, swapped, low0, high01, meta, codes, before, out,
    sims, rows, cols,
):
    width = arrived.shape[1] // 3
    moves = [
        (HIGH, high2, None, 2, 1), (OWN, own0, None, 0, 3), (OWN, arrived, 0, 3, 1),
        (SIB, sib0, None, 0, 3), (SIB, swapped, 0, 3, 1), (HIGH, high01, None, 0, 2),
        (HIGH, arrived, 2 * width, 3, 1), (LOW, low0, None, 0, 3), (LOW, arrived, width, 3, 1),
    ]
    tiles = Tiles(
        moves, meta, codes, rows, cols, (OWN, SIB, LOW), (SIB, HIGH)
    )
    pieces = [tiles.piece(cls, 0, 3, HIGH, 2) for cls in (OWN, SIB)]
    pieces += [tiles.piece(OWN, 3, 1, HIGH, 2)]
    pieces += [tiles.piece(SIB, 3, 1, HIGH, b) for b in range(4)]
    run(pieces, sims)
    pairs = [(a, b) for a, b in ALL_PAIRS if 3 in (a, b)]
    either(second_core(), lambda flip: run(tiles.matched(flip, OWN, SIB, pairs), sims))
    either(outer_chip(), lambda flip: run(tiles.matched(flip, LOW, HIGH, ALL_PAIRS), sims))
    for cls in (OWN, SIB, LOW, HIGH):
        out[cls : cls + 1, :] = jnp.maximum(before[cls : cls + 1, :], tiles.result(cls))


def last_kernel(
    pools, group, main, rest, lows0, high01, high2, swapped, arrived, meta, codes, before, out,
    sims, rows, cols, every, upper, sem,
):
    width = swapped.shape[1] // 3
    copy = pltpu.make_async_copy(arrived.at[:, pl.ds(2 * width, width), :], upper, sem)
    copy.start()
    moves = [
        (LOWS, lows0, None, 0, 3), (LOWS, swapped, width, 3, 1), (HIGH, high01, None, 0, 2),
        (HIGH, high2, None, 2, 1), (HIGH, upper, 0, 3, 1),
    ]
    tiles = Tiles(
        moves, meta, codes, rows, cols, (LOWS,), (HIGH,))
    copy.wait()
    either(outer_chip(), lambda flip: run(tiles.matched(flip, LOWS, HIGH, ALL_PAIRS), sims))
    every[...] = jnp.zeros(every.shape, F32)
    for cls, place in enumerate(tiles.relatives):
        best = [] if cls == LOWS else [before[cls : cls + 1, :]]
        if cls in (LOWS, HIGH):
            best.append(tiles.result(cls))
        every[pl.ds(place, 1), :] = functools.reduce(jnp.maximum, best)
    for p in range(pools):
        rows_out = slice(p * group, (p + 1) * group)
        out[rows_out, :main] = every[:, p * main : (p + 1) * main]
        at = pools * main + p * rest
        out[rows_out, main:] = every[:, at : at + rest]


def score_kernel(pools, group, places, table_ref, returned_ref, out_ref):
    rows_dev = out_ref.shape[1]
    arrived = jnp.transpose(
        jnp.concatenate([returned_ref[...], jnp.zeros_like(returned_ref)], axis=1)
    )
    table = table_ref[...]
    row = iota((8, rows_dev), 1)
    total = jnp.zeros((8, rows_dev), F32)
    for p in range(pools):
        for k in range(places):
            value = jnp.max(
                arrived[k * group : (k + 1) * group, p * group : (p + 1) * group],
                axis=1,
                keepdims=True,
            )
            entry = table[p * group : (p + 1) * group, k : k + 1]
            total = jnp.where(entry == row, value, total)
    out_ref[...] = jnp.sum(total, axis=0, keepdims=True)


def body(embeddings, members, valid, block_cluster):
    rows_dev, feature = embeddings.shape
    pools = lax.axis_size("pool")
    group = lax.axis_size("grp")
    devices = pools * group
    places = rows_dev // devices
    last = places // 4
    sds = jax.ShapeDtypeStruct
    hbm = pl.BlockSpec(memory_space=pltpu.HBM)
    valid_row = valid.reshape(1, -1)
    cluster_row = block_cluster.reshape(1, -1)
    blocks, block_len = members.shape

    some = jnp.any(valid > 0)
    table, main = pl.pallas_call(
        lambda *refs: table_kernel(pools, group, places, last, *refs),
        out_shape=(
            sds((devices, 128), I32),
            sds((3 * QUARTER, feature), BF16),
        ),
        in_specs=[hbm] * 3,
        scratch_shapes=[
            pltpu.VMEM((blocks, block_len), I32),
            pltpu.VMEM((1, blocks), I32),
            pltpu.VMEM((rows_dev, feature), BF16),
            pltpu.VMEM((blocks, 128), F32),
            pltpu.SemaphoreType.DMA((3,)),
        ],
        compiler_params=TABLE_PARAMS,
        cost_estimate=cost(rows_dev * rows_dev * feature),
        name="table",
    )(members, valid_row, embeddings)
    meta, codes = pl.pallas_call(
        lambda *refs: meta_kernel(group, places, last, *refs),
        out_shape=(sds((2, group, rows_dev), I32), sds((rows_dev, 128), I32)),
        in_specs=[hbm] * 3,
        scratch_shapes=[
            pltpu.VMEM((2 * group, block_len), I32),
            pltpu.VMEM((1, blocks), I32),
            pltpu.VMEM((1, blocks), I32),
            pltpu.VMEM((128, rows_dev), I32),
            pltpu.SemaphoreType.DMA((3,)),
        ],
        compiler_params=PARAMS,
        cost_estimate=cost(2 * rows_dev**3),
        name="meta",
    )(members, valid_row, cluster_row)

    def shift(rows, by):
        return lax.ppermute(rows, "grp", [(g, (g + by) % group) for g in range(group)])

    def swap(rows):
        return lax.ppermute(rows, "grp", [(g, g ^ 1) for g in range(group)])

    def follow(rows, after, also_after):
        return pl.pallas_call(
            follow_kernel,
            out_shape=sds(rows.shape, BF16),
            in_specs=[hbm] * 3,
            out_specs=hbm,
            input_output_aliases={0: 0},
            compiler_params=PARAMS,
            name="follow",
        )(rows, after, also_after)

    def to_pools(rows):
        return lax.all_to_all(rows, "pool", split_axis=0, concat_axis=0, tiled=True)

    vmem = pl.BlockSpec(memory_space=pltpu.VMEM)
    rest = pl.pallas_call(
        lambda *refs: rest_kernel(pools, places, last, *refs),
        out_shape=sds((QUARTER, feature), BF16),
        in_specs=[vmem, vmem, hbm],
        compiler_params=PARAMS,
        name="rest",
    )(table, embeddings, meta)
    low_rest, high_rest = shift(rest, 2), shift(rest, -2)
    own0 = to_pools(main.reshape(pools, -1, feature)).reshape(-1, feature)
    sent = pl.pallas_call(
        lambda *refs: join_kernel(pools, *refs),
        out_shape=sds((pools, 3 * QUARTER // pools, feature), BF16),
        compiler_params=PARAMS,
        name="join",
    )(rest, low_rest, high_rest)
    own0, own01, own2 = pl.pallas_call(
        split_kernel,
        out_shape=tuple(sds((n * QUARTER, feature), BF16) for n in (3, 2, 1)),
        in_specs=[hbm] * 3,
        out_specs=(hbm, vmem, vmem),
        input_output_aliases={0: 0},
        scratch_shapes=[pltpu.SemaphoreType.DMA((2,))],
        compiler_params=PARAMS,
        name="split",
    )(own0, sent, some.astype(I32).reshape(1, 1))
    low0, high01, high2 = shift(own0, 2), shift(own01, -2), shift(own2, -2)
    sib0 = swap(own0)

    def tiles(kernel, name, squares, operands, small, out_shape=(8, rows_dev), more=(), specs=None):
        return pl.pallas_call(
            kernel,
            out_shape=sds(out_shape, F32),
            in_specs=specs or [vmem] * (len(operands) + len(small)),
            scratch_shapes=[
                pltpu.VMEM((2, 3 * QUARTER, QUARTER), F32),
                pltpu.VMEM((4, rows_dev, 128), F32),
                pltpu.VMEM((5, 8, rows_dev), F32),
                *more,
            ],
            compiler_params=PARAMS,
            cost_estimate=cost(squares * QUARTER * QUARTER * feature),
            name=name,
        )(*operands, *small)

    def bring(sent, own0, sib0, meta, codes):
        near = tiles(near_kernel, "near", 11, (own0, sib0), (meta, codes))
        return to_pools(sent), near

    def bring_nothing(sent, own0, sib0, meta, codes):
        return jnp.zeros_like(sent), jnp.zeros((8, rows_dev), F32)

    arrived, near = lax.cond(
        some, bring, bring_nothing, sent, own0, sib0, meta, codes
    )
    swapped = swap(arrived)
    middle = tiles(
        middle_kernel, "middle", 25, (own0, arrived, high01, sib0), (meta, codes, near)
    )
    low0 = follow(low0, middle, high2)
    best = tiles(
        main_kernel, "main", 23, (own0, arrived, high2, sib0, swapped, low0, high01),
        (meta, codes, middle),
    )
    best = tiles(
        lambda *refs: last_kernel(pools, group, group * (places - last), group * last, *refs),
        "last", 8, (swap(low0), high01, high2, swapped, arrived), (meta, codes, best),
        out_shape=(devices, group * places),
        more=(
            pltpu.VMEM((group, rows_dev), F32),
            pltpu.VMEM((pools, QUARTER // pools, feature), BF16),
            pltpu.SemaphoreType.DMA,
        ),
        specs=[vmem] * 4 + [hbm] + [vmem] * 3,
    )
    returned = lax.all_to_all(best, ("pool", "grp"), split_axis=0, concat_axis=0, tiled=True)
    scores = pl.pallas_call(
        lambda *refs: score_kernel(pools, group, places, *refs),
        out_shape=sds((1, rows_dev), F32),
        compiler_params=PARAMS,
        name="score",
    )(table, returned)
    return scores.reshape(rows_dev)


def cost(products):
    return pl.CostEstimate(flops=2 * products, bytes_accessed=0, transcendentals=0)


def solution(mesh):
    in_specs = (P(("pool", "grp"), None), P(), P(), P())
    out_specs = P(("pool", "grp"))
    return jax.shard_map(body, mesh=mesh, in_specs=in_specs, out_specs=out_specs, check_vma=False)
```

```python
import functools

import jax
import jax.numpy as jnp
from jax import lax
from jax.experimental import pallas as pl
from jax.experimental.pallas import tpu as pltpu
from jax.sharding import PartitionSpec as P

EPS = 1e-06
F32 = jnp.float32
BF16 = jnp.bfloat16
I32 = jnp.int32
QUARTER = 256
CODE = 8192
NT = (((1,), (1,)), ((), ()))
PARAMS = pltpu.CompilerParams(vmem_limit_bytes=12 * 1024 * 1024)
TABLE_PARAMS = pltpu.CompilerParams(vmem_limit_bytes=62 * 1024 * 1024)


def iota(shape, dim):
    return lax.broadcasted_iota(I32, shape, dim)


def normal_rows(rows):
    return (rows * lax.rsqrt(jnp.sum(rows * rows, axis=1, keepdims=True) + EPS)).astype(BF16)


def picked_rows(table, emb, first, count, pools):
    width = emb.shape[0]
    wanted = []
    for k in range(first, first + count):
        hit = table[:, k : k + 1] == iota((table.shape[0], width), 1)
        wanted.append(jnp.where(hit, 1.0, 0.0).reshape(pools, -1, width))
    choice = jnp.concatenate(wanted, axis=1).reshape(-1, width).astype(BF16)
    return normal_rows(jnp.dot(choice, emb, preferred_element_type=F32))


def table_kernel(
    pools, group, places, last, members_hbm, valid_hbm, emb_hbm, table_ref, main_ref,
    members_ref, valid_ref, emb_ref, found_ref, sems,
):
    copies = []
    for n, (source, target) in enumerate(
        ((members_hbm, members_ref), (valid_hbm, valid_ref), (emb_hbm, emb_ref))
    ):
        copies.append(pltpu.make_async_copy(source, target, sems.at[n]))
        copies[-1].start()
    rows_dev = emb_ref.shape[0]
    device = lax.axis_index("pool") * group + lax.axis_index("grp")
    blocks, block_len = members_ref.shape
    devices = blocks // 2
    before = jnp.where(
        iota((block_len, block_len), 0) < iota((block_len, block_len), 1), 1.0, 0.0
    ).astype(BF16)
    at = iota((blocks, blocks), 1) == iota((blocks, blocks), 0)
    copies[0].wait()
    copies[1].wait()
    live = jnp.sum(jnp.where(at, valid_ref[...], 0), axis=1, keepdims=True)
    local = members_ref[...] - device * rows_dev
    mine = (local >= 0) & (local < rows_dev) & (iota((blocks, block_len), 1) < live)
    ones = jnp.where(mine, 1.0, 0.0)
    counts = jnp.broadcast_to(jnp.sum(ones, axis=1, keepdims=True), (blocks, 128))
    counts = jnp.where(iota((blocks, 128), 0) % 2 == 1, pltpu.roll(counts, 1, 0), 0.0)
    rank = jnp.dot(ones.astype(BF16), before, preferred_element_type=F32) + counts[:, :1]
    rank = jnp.where(mine, rank, -1.0)
    value = (local + 1).astype(F32)
    lane = iota((blocks, 128), 1)
    found = jnp.zeros((blocks, 128), F32)
    for k in range(places):
        entry = jnp.sum(jnp.where(rank == k, value, 0.0), axis=1, keepdims=True)
        found = jnp.where(lane == k, entry, found)
    found_ref[...] = found
    pair = found_ref[pl.ds(0, devices, stride=2), :] + found_ref[pl.ds(1, devices, stride=2), :]
    table = pair.astype(I32) - 1
    table_ref[...] = table
    copies[2].wait()
    main_ref[...] = picked_rows(table, emb_ref[...], 0, places - last, pools)


def rest_kernel(pools, places, last, table_ref, emb_ref, after, out):
    del after
    out[...] = picked_rows(table_ref[...], emb_ref[...], places - last, last, pools)


def relatives():
    group = lax.axis_size("grp")
    index = lax.axis_index("grp")
    flip = 1 - 2 * (index % 2)
    below = (index + group - 2) % group
    return index, index + flip, below, below + flip, (index + 2) % group


def meta_kernel(
    group, places, last, members_hbm, valid_hbm, cluster_hbm, out_ref, codes_ref,
    members_ref, valid_ref, cluster_ref, packed_ref, sems,
):
    blocks = valid_ref.shape[1]
    block_len = members_ref.shape[1]
    pool = lax.axis_index("pool")
    first_block = pl.multiple_of(pool * 2 * group, 2 * group)
    copies = []
    for n, (source, target) in enumerate(
        (
            (members_hbm.at[pl.ds(first_block, 2 * group), :], members_ref),
            (valid_hbm, valid_ref),
            (cluster_hbm, cluster_ref),
        )
    ):
        copies.append(pltpu.make_async_copy(source, target, sems.at[n]))
        copies[-1].start()
    sources = blocks // 2
    slots = 2 * block_len
    width = group * places
    before = jnp.where(iota((slots, slots), 0) < iota((slots, slots), 1), 1.0, 0.0).astype(BF16)
    slot = iota((1, slots), 1)
    kind = iota((2 * width, slots), 0)
    kind_place = kind % width // group
    kind_owner = kind % group
    kind_value = jnp.where(kind < width, slot // 32, slot % 32 + 1)
    found = jnp.zeros((sources, 2 * width), F32)
    block_lane = iota((1, blocks), 1)
    lane = iota((1, width), 1)
    first_cluster = jnp.zeros((1, width), I32)
    second_cluster = jnp.zeros((1, width), I32)
    for copy in copies:
        copy.wait()
    for owner in range(group):
        halves, lives = [], []
        for half in range(2):
            halves.append(members_ref[2 * owner + half : 2 * owner + half + 1, :])
            at = block_lane == first_block + 2 * owner + half
            lives.append(jnp.sum(jnp.where(at, valid_ref[...], 0), axis=1, keepdims=True))
            cluster = jnp.sum(jnp.where(at, cluster_ref[...], 0), axis=1, keepdims=True)
            if half == 0:
                first_cluster = jnp.where(lane % group == owner, cluster, first_cluster)
            else:
                second_cluster = jnp.where(lane % group == owner, cluster, second_cluster)
        rows = jnp.concatenate(halves, axis=1)
        end = jnp.where(slot < block_len, lives[0], block_len + lives[1])
        origin = jnp.where(slot < end, rows // slots, -1)
        match = iota((sources, slots), 0) == origin
        ones = jnp.where(match, 1.0, 0.0).astype(BF16)
        ranks = jnp.dot(ones, before, preferred_element_type=F32)
        rank = jnp.sum(jnp.where(match, ranks, 0.0), axis=0, keepdims=True).astype(I32)
        weight = jnp.where((kind_owner == owner) & (kind_place == rank), kind_value, 0)
        found = found + lax.dot_general(
            ones, weight.astype(F32).astype(BF16), NT, preferred_element_type=F32
        )
    found = found.astype(I32)
    place = found[:, :width] * 32 + found[:, width:] - 1
    filled = found[:, width:] > 0
    position = jnp.where(filled, place + lane % group * slots, -1)
    cluster = jnp.where(filled, jnp.where(place < block_len, first_cluster, second_cluster), -1)
    main = (places - last) * group
    rest = last * group
    pools = sources // group
    for n, values in enumerate((position, cluster)):
        for p in range(pools):
            own = values[p * group : (p + 1) * group, :]
            out_ref[n, :, p * main : (p + 1) * main] = own[:, :main]
            at = pools * main + p * rest
            out_ref[n, :, at : at + rest] = own[:, main:]
    packed_ref[...] = jnp.zeros(packed_ref.shape, I32)
    for n, cls in enumerate(relatives()[:4]):
        pos = out_ref[0, pl.ds(cls, 1), :]
        cluster = out_ref[1, pl.ds(cls, 1), :]
        packed_ref[n : n + 1, :] = jnp.where(cluster < 0, -2 * CODE, cluster * CODE + pos)
    codes_ref[...] = jnp.transpose(packed_ref[...])


def run(pieces, sims_ref):
    for n in range(len(pieces) + 1):
        if n < len(pieces):
            piece = pieces[n]
            sims_ref[n % 2, : piece["count"], :] = lax.dot_general(
                piece["left"](), piece["right"](), NT, preferred_element_type=F32
            )
        if n > 0:
            take_maxima(sims_ref.at[(n - 1) % 2], **pieces[n - 1])


def take_maxima(sims_ref, left, right, count, codes, cls, rows, start, pos_row, cluster_row, col, col_start, same):
    step = 128
    right_pos, right_cluster = pos_row(), cluster_row()
    parts = QUARTER // 128
    best_col = [jnp.zeros((8, 128), F32) for _ in range(parts)]
    for top in range(0, count, step):
        code = codes[start + top : start + top + step, cls : cls + 1]
        code = jnp.broadcast_to(code, (step, 128))
        pos = code & (CODE - 1)
        cluster = code >> 13
        best = rows[start + top : start + top + step, :]
        for part in range(parts):
            lanes = slice(part * 128, part * 128 + 128)
            sims = sims_ref[top : top + step, lanes]
            sims = jnp.where(cluster == right_cluster[:, lanes], sims, 0.0)
            earlier = right_pos[:, lanes] < pos
            best = jnp.maximum(best, jnp.where(earlier, sims, 0.0))
            if top < same:
                later = jnp.where(earlier, 0.0, sims)
                best_col[part] = jnp.maximum(
                    best_col[part], jnp.max(later.reshape(-1, 8, 128), axis=0)
                )
        rows[start + top : start + top + step, :] = best
    if same > 0:
        for part in range(parts):
            lanes = slice(col_start + part * 128, col_start + part * 128 + 128)
            col[:, lanes] = jnp.maximum(col[:, lanes], best_col[part])


def row_result(row_ref):
    return jnp.max(jnp.transpose(row_ref[...]), axis=0, keepdims=True)


def col_result(col_ref):
    return jnp.max(col_ref[...], axis=0, keepdims=True)


OWN, SIB, LOW, LOWS, HIGH = range(5)


class Tiles:
    def __init__(self, parts, meta, codes, rows, cols, row_classes, col_classes):
        self.meta, self.codes, self.rows, self.cols = meta, codes, rows, cols
        self.row_classes, self.col_classes = row_classes, col_classes
        self.relatives = relatives()
        self.parts = {}
        for cls, ref, at, quarter, count in parts:
            for q in range(quarter, quarter + count):
                self.parts[cls, q] = (ref, at if len(ref.shape) == 3 else (q - quarter) * QUARTER)
        for cls in row_classes:
            rows[cls, :, :] = jnp.zeros(rows.shape[1:], F32)
        for cls in col_classes:
            cols[cls, :, :] = jnp.zeros(cols.shape[1:], F32)

    def load(self, cls, quarter, count=1):
        ref, at = self.parts[cls, quarter]
        if len(ref.shape) == 3:
            return ref[:, at : at + QUARTER // ref.shape[0], :].reshape(QUARTER, -1)
        return ref[at : at + count * QUARTER, :]

    def piece(self, left, quarter, count, right, right_quarter, same=None):
        lanes = slice(right_quarter * QUARTER, (right_quarter + 1) * QUARTER)
        place = self.relatives[right]
        return dict(
            left=lambda: self.load(left, quarter, count),
            right=lambda: self.load(right, right_quarter),
            count=count * QUARTER,
            codes=self.codes,
            cls=left,
            rows=self.rows.at[left],
            start=quarter * QUARTER,
            pos_row=lambda: self.meta[0, pl.ds(place, 1), lanes],
            cluster_row=lambda: self.meta[1, pl.ds(place, 1), lanes],
            col=self.cols.at[right],
            col_start=right_quarter * QUARTER,
            same=count * QUARTER if same is None else same,
        )

    def matched(self, flip, left, right, pairs):
        pieces = []
        for b in range(4):
            mine = [a for a in range(4) if (a, b) in pairs and (a // 2 + b // 2) % 2 == flip]
            if mine == [0, 1] and self.parts[left, 0][0] is self.parts[left, 1][0]:
                pieces.append(self.piece(left, 0, 2, right, b))
            else:
                pieces += [self.piece(left, a, 1, right, b) for a in mine]
        return pieces

    def result(self, cls):
        best = []
        if cls in self.row_classes:
            best.append(row_result(self.rows.at[cls]))
        if cls in self.col_classes:
            best.append(col_result(self.cols.at[cls]))
        return functools.reduce(jnp.maximum, best)


def either(flag, work):
    pl.when(flag)(lambda: work(1))
    pl.when(jnp.logical_not(flag))(lambda: work(0))


def second_core():
    return lax.axis_index("grp") % 2 == 1


def outer_chip():
    chip = lax.axis_index("grp") // 2
    return (chip == 0) | (chip == 3)


ALL_PAIRS = [(a, b) for a in range(4) for b in range(4)]


def follow_kernel(rows, after, also_after, out):
    del rows, after, also_after, out


def join_kernel(pools, rest, low_rest, high_rest, out):
    width = QUARTER // pools
    for n, part in enumerate((rest, low_rest, high_rest)):
        out[:, n * width : (n + 1) * width, :] = part[...].reshape(pools, width, -1)


def near_kernel(own0, sib0, meta, codes, out, sims, rows, cols):
    moves = [(OWN, own0, None, 0, 3), (SIB, sib0, None, 0, 3)]
    tiles = Tiles(
        moves, meta, codes, rows, cols, (OWN,), (OWN, SIB))
    run([tiles.piece(OWN, 0, b + 1, OWN, b, same=b * QUARTER) for b in range(3)], sims)
    pairs = [(a, b) for a, b in ALL_PAIRS if 3 not in (a, b)]
    either(second_core(), lambda flip: run(tiles.matched(flip, OWN, SIB, pairs), sims))
    out[...] = jnp.zeros(out.shape, F32)
    for cls in (OWN, SIB):
        out[cls : cls + 1, :] = tiles.result(cls)


def middle_kernel(own0, arrived, sib0, meta, codes, near, out, sims, rows, cols):
    width = arrived.shape[1] // 3
    moves = [
        (OWN, own0, None, 0, 3), (OWN, arrived, 0, 3, 1), (HIGH, arrived, 2 * width, 3, 1),
        (SIB, sib0, None, 0, 3),
    ]
    tiles = Tiles(moves, meta, codes, rows, cols, (OWN, SIB), (OWN, HIGH))
    pieces = [tiles.piece(OWN, 0, 3, OWN, 3), tiles.piece(OWN, 3, 1, OWN, 3, same=0)]
    pieces += [tiles.piece(OWN, 0, 3, HIGH, 3), tiles.piece(OWN, 3, 1, HIGH, 3)]
    pieces += [tiles.piece(SIB, 0, 3, HIGH, 3)]
    run(pieces, sims)
    out[...] = near[...]
    for cls in (OWN, SIB, HIGH):
        out[cls : cls + 1, :] = jnp.maximum(near[cls : cls + 1, :], tiles.result(cls))


def main_kernel(
    own0, arrived, high0, sib0, swapped, low0, meta, codes, before, out, sims, rows, cols
):
    width = arrived.shape[1] // 3
    moves = [
        (HIGH, high0, None, 0, 3), (OWN, own0, None, 0, 3), (OWN, arrived, 0, 3, 1),
        (SIB, sib0, None, 0, 3), (SIB, swapped, 0, 3, 1), (HIGH, arrived, 2 * width, 3, 1),
        (LOW, low0, None, 0, 3), (LOW, arrived, width, 3, 1),
    ]
    tiles = Tiles(moves, meta, codes, rows, cols, (OWN, SIB, LOW), (SIB, HIGH))
    pieces = []
    for b in range(3):
        for cls in (OWN, SIB):
            pieces += [tiles.piece(cls, 0, 3, HIGH, b), tiles.piece(cls, 3, 1, HIGH, b)]
    pieces += [tiles.piece(SIB, 3, 1, HIGH, 3)]
    run(pieces, sims)
    pairs = [(a, b) for a, b in ALL_PAIRS if 3 in (a, b)]
    either(second_core(), lambda flip: run(tiles.matched(flip, OWN, SIB, pairs), sims))
    either(outer_chip(), lambda flip: run(tiles.matched(flip, LOW, HIGH, ALL_PAIRS), sims))
    for cls in (OWN, SIB, LOW, HIGH):
        out[cls : cls + 1, :] = jnp.maximum(before[cls : cls + 1, :], tiles.result(cls))


def last_kernel(
    pools, group, main, rest, lows0, high0, swapped, arrived, meta, codes, before, out,
    sims, rows, cols, every, upper, sem,
):
    width = swapped.shape[1] // 3
    copy = pltpu.make_async_copy(arrived.at[:, pl.ds(2 * width, width), :], upper, sem)
    copy.start()
    moves = [
        (LOWS, lows0, None, 0, 3), (LOWS, swapped, width, 3, 1), (HIGH, high0, None, 0, 3),
        (HIGH, upper, 0, 3, 1),
    ]
    tiles = Tiles(
        moves, meta, codes, rows, cols, (LOWS,), (HIGH,))
    copy.wait()
    either(outer_chip(), lambda flip: run(tiles.matched(flip, LOWS, HIGH, ALL_PAIRS), sims))
    every[...] = jnp.zeros(every.shape, F32)
    for cls, place in enumerate(tiles.relatives):
        best = [] if cls == LOWS else [before[cls : cls + 1, :]]
        if cls in (LOWS, HIGH):
            best.append(tiles.result(cls))
        every[pl.ds(place, 1), :] = functools.reduce(jnp.maximum, best)
    for p in range(pools):
        rows_out = slice(p * group, (p + 1) * group)
        out[rows_out, :main] = every[:, p * main : (p + 1) * main]
        at = pools * main + p * rest
        out[rows_out, main:] = every[:, at : at + rest]


def score_kernel(pools, group, places, table_ref, returned_ref, out_ref):
    rows_dev = out_ref.shape[1]
    arrived = jnp.transpose(
        jnp.concatenate([returned_ref[...], jnp.zeros_like(returned_ref)], axis=1)
    )
    table = table_ref[...]
    row = iota((8, rows_dev), 1)
    total = jnp.zeros((8, rows_dev), F32)
    for p in range(pools):
        for k in range(places):
            value = jnp.max(
                arrived[k * group : (k + 1) * group, p * group : (p + 1) * group],
                axis=1,
                keepdims=True,
            )
            entry = table[p * group : (p + 1) * group, k : k + 1]
            total = jnp.where(entry == row, value, total)
    out_ref[...] = jnp.sum(total, axis=0, keepdims=True)


def body(embeddings, members, valid, block_cluster):
    rows_dev, feature = embeddings.shape
    pools = lax.axis_size("pool")
    group = lax.axis_size("grp")
    devices = pools * group
    places = rows_dev // devices
    last = places // 4
    sds = jax.ShapeDtypeStruct
    hbm = pl.BlockSpec(memory_space=pltpu.HBM)
    valid_row = valid.reshape(1, -1)
    cluster_row = block_cluster.reshape(1, -1)
    blocks, block_len = members.shape

    some = jnp.any(valid > 0)
    table, main = pl.pallas_call(
        lambda *refs: table_kernel(pools, group, places, last, *refs),
        out_shape=(
            sds((devices, 128), I32),
            sds((3 * QUARTER, feature), BF16),
        ),
        in_specs=[hbm] * 3,
        scratch_shapes=[
            pltpu.VMEM((blocks, block_len), I32),
            pltpu.VMEM((1, blocks), I32),
            pltpu.VMEM((rows_dev, feature), BF16),
            pltpu.VMEM((blocks, 128), F32),
            pltpu.SemaphoreType.DMA((3,)),
        ],
        compiler_params=TABLE_PARAMS,
        cost_estimate=cost(rows_dev * rows_dev * feature),
        name="table",
    )(members, valid_row, embeddings)
    meta, codes = pl.pallas_call(
        lambda *refs: meta_kernel(group, places, last, *refs),
        out_shape=(sds((2, group, rows_dev), I32), sds((rows_dev, 128), I32)),
        in_specs=[hbm] * 3,
        scratch_shapes=[
            pltpu.VMEM((2 * group, block_len), I32),
            pltpu.VMEM((1, blocks), I32),
            pltpu.VMEM((1, blocks), I32),
            pltpu.VMEM((128, rows_dev), I32),
            pltpu.SemaphoreType.DMA((3,)),
        ],
        compiler_params=PARAMS,
        cost_estimate=cost(2 * rows_dev**3),
        name="meta",
    )(members, valid_row, cluster_row)

    def shift(rows, by):
        return lax.ppermute(rows, "grp", [(g, (g + by) % group) for g in range(group)])

    def swap(rows):
        return lax.ppermute(rows, "grp", [(g, g ^ 1) for g in range(group)])

    def follow(rows, after, also_after):
        return pl.pallas_call(
            follow_kernel,
            out_shape=sds(rows.shape, BF16),
            in_specs=[hbm] * 3,
            out_specs=hbm,
            input_output_aliases={0: 0},
            compiler_params=PARAMS,
            name="follow",
        )(rows, after, also_after)

    def to_pools(rows):
        return lax.all_to_all(rows, "pool", split_axis=0, concat_axis=0, tiled=True)

    vmem = pl.BlockSpec(memory_space=pltpu.VMEM)
    rest = pl.pallas_call(
        lambda *refs: rest_kernel(pools, places, last, *refs),
        out_shape=sds((QUARTER, feature), BF16),
        in_specs=[vmem, vmem, hbm],
        compiler_params=PARAMS,
        name="rest",
    )(table, embeddings, meta)
    low_rest, high_rest = shift(rest, 2), shift(rest, -2)
    own0 = to_pools(main.reshape(pools, -1, feature)).reshape(-1, feature)
    sent = pl.pallas_call(
        lambda *refs: join_kernel(pools, *refs),
        out_shape=sds((pools, 3 * QUARTER // pools, feature), BF16),
        compiler_params=PARAMS,
        name="join",
    )(rest, low_rest, high_rest)
    own0 = follow(own0, sent, some.astype(I32).reshape(1, 1))
    low0, high0 = shift(own0, 2), shift(own0, -2)
    sib0 = swap(own0)

    def tiles(kernel, name, squares, operands, small, out_shape=(8, rows_dev), more=(), specs=None):
        return pl.pallas_call(
            kernel,
            out_shape=sds(out_shape, F32),
            in_specs=specs or [vmem] * (len(operands) + len(small)),
            scratch_shapes=[
                pltpu.VMEM((2, 3 * QUARTER, QUARTER), F32),
                pltpu.VMEM((4, rows_dev, 128), F32),
                pltpu.VMEM((5, 8, rows_dev), F32),
                *more,
            ],
            compiler_params=PARAMS,
            cost_estimate=cost(squares * QUARTER * QUARTER * feature),
            name=name,
        )(*operands, *small)

    def bring(sent, own0, sib0, meta, codes):
        near = tiles(near_kernel, "near", 11, (own0, sib0), (meta, codes))
        return to_pools(sent), near

    def bring_nothing(sent, own0, sib0, meta, codes):
        return jnp.zeros_like(sent), jnp.zeros((8, rows_dev), F32)

    arrived, near = lax.cond(
        some, bring, bring_nothing, sent, own0, sib0, meta, codes
    )
    swapped = swap(arrived)
    middle = tiles(middle_kernel, "middle", 11, (own0, arrived, sib0), (meta, codes, near))
    low0 = follow(low0, middle, high0)
    best = tiles(
        main_kernel, "main", 37, (own0, arrived, high0, sib0, swapped, low0), (meta, codes, middle)
    )
    best = tiles(
        lambda *refs: last_kernel(pools, group, group * (places - last), group * last, *refs),
        "last", 8, (swap(low0), high0, swapped, arrived), (meta, codes, best),
        out_shape=(devices, group * places),
        more=(
            pltpu.VMEM((group, rows_dev), F32),
            pltpu.VMEM((pools, QUARTER // pools, feature), BF16),
            pltpu.SemaphoreType.DMA,
        ),
        specs=[vmem] * 3 + [hbm] + [vmem] * 3,
    )
    returned = lax.all_to_all(best, ("pool", "grp"), split_axis=0, concat_axis=0, tiled=True)
    scores = pl.pallas_call(
        lambda *refs: score_kernel(pools, group, places, *refs),
        out_shape=sds((1, rows_dev), F32),
        compiler_params=PARAMS,
        name="score",
    )(table, returned)
    return scores.reshape(rows_dev)


def cost(products):
    return pl.CostEstimate(flops=2 * products, bytes_accessed=0, transcendentals=0)


def solution(mesh):
    in_specs = (P(("pool", "grp"), None), P(), P(), P())
    out_specs = P(("pool", "grp"))
    return jax.shard_map(body, mesh=mesh, in_specs=in_specs, out_specs=out_specs, check_vma=False)
```

```python
import functools

import jax
import jax.numpy as jnp
from jax import lax
from jax.experimental import pallas as pl
from jax.experimental.pallas import tpu as pltpu
from jax.sharding import PartitionSpec as P

EPS = 1e-06
F32 = jnp.float32
BF16 = jnp.bfloat16
I32 = jnp.int32
QUARTER = 256
CODE = 8192
NT = (((1,), (1,)), ((), ()))
PARAMS = pltpu.CompilerParams(vmem_limit_bytes=12 * 1024 * 1024)
TABLE_PARAMS = pltpu.CompilerParams(vmem_limit_bytes=62 * 1024 * 1024)


def iota(shape, dim):
    return lax.broadcasted_iota(I32, shape, dim)


def normal_rows(rows):
    return (rows * lax.rsqrt(jnp.sum(rows * rows, axis=1, keepdims=True) + EPS)).astype(BF16)


def picked_rows(table, emb, first, count, pools):
    width = emb.shape[0]
    wanted = []
    for k in range(first, first + count):
        hit = table[:, k : k + 1] == iota((table.shape[0], width), 1)
        wanted.append(jnp.where(hit, 1.0, 0.0).reshape(pools, -1, width))
    choice = jnp.concatenate(wanted, axis=1).reshape(-1, width).astype(BF16)
    return normal_rows(jnp.dot(choice, emb, preferred_element_type=F32))


def table_kernel(
    pools, group, places, last, members_hbm, valid_hbm, emb_hbm, table_ref, main_ref,
    members_ref, valid_ref, emb_ref, found_ref, sems,
):
    copies = []
    for n, (source, target) in enumerate(
        ((members_hbm, members_ref), (valid_hbm, valid_ref), (emb_hbm, emb_ref))
    ):
        copies.append(pltpu.make_async_copy(source, target, sems.at[n]))
        copies[-1].start()
    rows_dev = emb_ref.shape[0]
    device = lax.axis_index("pool") * group + lax.axis_index("grp")
    blocks, block_len = members_ref.shape
    devices = blocks // 2
    before = jnp.where(
        iota((block_len, block_len), 0) < iota((block_len, block_len), 1), 1.0, 0.0
    ).astype(BF16)
    at = iota((blocks, blocks), 1) == iota((blocks, blocks), 0)
    copies[0].wait()
    copies[1].wait()
    live = jnp.sum(jnp.where(at, valid_ref[...], 0), axis=1, keepdims=True)
    local = members_ref[...] - device * rows_dev
    mine = (local >= 0) & (local < rows_dev) & (iota((blocks, block_len), 1) < live)
    ones = jnp.where(mine, 1.0, 0.0)
    counts = jnp.broadcast_to(jnp.sum(ones, axis=1, keepdims=True), (blocks, 128))
    counts = jnp.where(iota((blocks, 128), 0) % 2 == 1, pltpu.roll(counts, 1, 0), 0.0)
    rank = jnp.dot(ones.astype(BF16), before, preferred_element_type=F32) + counts[:, :1]
    rank = jnp.where(mine, rank, -1.0)
    value = (local + 1).astype(F32)
    lane = iota((blocks, 128), 1)
    found = jnp.zeros((blocks, 128), F32)
    for k in range(places):
        entry = jnp.sum(jnp.where(rank == k, value, 0.0), axis=1, keepdims=True)
        found = jnp.where(lane == k, entry, found)
    found_ref[...] = found
    pair = found_ref[pl.ds(0, devices, stride=2), :] + found_ref[pl.ds(1, devices, stride=2), :]
    table = pair.astype(I32) - 1
    table_ref[...] = table
    copies[2].wait()
    main_ref[...] = picked_rows(table, emb_ref[...], 0, places - last, pools)


def rest_kernel(pools, places, last, table_ref, emb_ref, after, out):
    del after
    out[...] = picked_rows(table_ref[...], emb_ref[...], places - last, last, pools)


def relatives():
    group = lax.axis_size("grp")
    index = lax.axis_index("grp")
    flip = 1 - 2 * (index % 2)
    below = (index + group - 2) % group
    return index, index + flip, below, below + flip, (index + 2) % group


def meta_kernel(
    group, places, last, members_hbm, valid_hbm, cluster_hbm, out_ref, codes_ref,
    members_ref, valid_ref, cluster_ref, packed_ref, sems,
):
    blocks = valid_ref.shape[1]
    block_len = members_ref.shape[1]
    pool = lax.axis_index("pool")
    first_block = pl.multiple_of(pool * 2 * group, 2 * group)
    copies = []
    for n, (source, target) in enumerate(
        (
            (members_hbm.at[pl.ds(first_block, 2 * group), :], members_ref),
            (valid_hbm, valid_ref),
            (cluster_hbm, cluster_ref),
        )
    ):
        copies.append(pltpu.make_async_copy(source, target, sems.at[n]))
        copies[-1].start()
    sources = blocks // 2
    slots = 2 * block_len
    width = group * places
    before = jnp.where(iota((slots, slots), 0) < iota((slots, slots), 1), 1.0, 0.0).astype(BF16)
    slot = iota((1, slots), 1)
    kind = iota((2 * width, slots), 0)
    kind_place = kind % width // group
    kind_owner = kind % group
    kind_value = jnp.where(kind < width, slot // 32, slot % 32 + 1)
    found = jnp.zeros((sources, 2 * width), F32)
    block_lane = iota((1, blocks), 1)
    lane = iota((1, width), 1)
    first_cluster = jnp.zeros((1, width), I32)
    second_cluster = jnp.zeros((1, width), I32)
    for copy in copies:
        copy.wait()
    for owner in range(group):
        halves, lives = [], []
        for half in range(2):
            halves.append(members_ref[2 * owner + half : 2 * owner + half + 1, :])
            at = block_lane == first_block + 2 * owner + half
            lives.append(jnp.sum(jnp.where(at, valid_ref[...], 0), axis=1, keepdims=True))
            cluster = jnp.sum(jnp.where(at, cluster_ref[...], 0), axis=1, keepdims=True)
            if half == 0:
                first_cluster = jnp.where(lane % group == owner, cluster, first_cluster)
            else:
                second_cluster = jnp.where(lane % group == owner, cluster, second_cluster)
        rows = jnp.concatenate(halves, axis=1)
        end = jnp.where(slot < block_len, lives[0], block_len + lives[1])
        origin = jnp.where(slot < end, rows // slots, -1)
        match = iota((sources, slots), 0) == origin
        ones = jnp.where(match, 1.0, 0.0).astype(BF16)
        ranks = jnp.dot(ones, before, preferred_element_type=F32)
        rank = jnp.sum(jnp.where(match, ranks, 0.0), axis=0, keepdims=True).astype(I32)
        weight = jnp.where((kind_owner == owner) & (kind_place == rank), kind_value, 0)
        found = found + lax.dot_general(
            ones, weight.astype(F32).astype(BF16), NT, preferred_element_type=F32
        )
    found = found.astype(I32)
    place = found[:, :width] * 32 + found[:, width:] - 1
    filled = found[:, width:] > 0
    position = jnp.where(filled, place + lane % group * slots, -1)
    cluster = jnp.where(filled, jnp.where(place < block_len, first_cluster, second_cluster), -1)
    main = (places - last) * group
    rest = last * group
    pools = sources // group
    for n, values in enumerate((position, cluster)):
        for p in range(pools):
            own = values[p * group : (p + 1) * group, :]
            out_ref[n, :, p * main : (p + 1) * main] = own[:, :main]
            at = pools * main + p * rest
            out_ref[n, :, at : at + rest] = own[:, main:]
    packed_ref[...] = jnp.zeros(packed_ref.shape, I32)
    for n, cls in enumerate(relatives()[:4]):
        pos = out_ref[0, pl.ds(cls, 1), :]
        cluster = out_ref[1, pl.ds(cls, 1), :]
        packed_ref[n : n + 1, :] = jnp.where(cluster < 0, -2 * CODE, cluster * CODE + pos)
    codes_ref[...] = jnp.transpose(packed_ref[...])


def run(pieces, sims_ref):
    for n in range(len(pieces) + 1):
        if n < len(pieces):
            piece = pieces[n]
            sims_ref[n % 2, : piece["count"], :] = lax.dot_general(
                piece["left"](), piece["right"](), NT, preferred_element_type=F32
            )
        if n > 0:
            take_maxima(sims_ref.at[(n - 1) % 2], **pieces[n - 1])


def take_maxima(sims_ref, left, right, count, codes, cls, rows, start, pos_row, cluster_row, col, col_start, same):
    step = 128
    right_pos, right_cluster = pos_row(), cluster_row()
    parts = QUARTER // 128
    best_col = [jnp.zeros((8, 128), F32) for _ in range(parts)]
    for top in range(0, count, step):
        code = codes[start + top : start + top + step, cls : cls + 1]
        code = jnp.broadcast_to(code, (step, 128))
        pos = code & (CODE - 1)
        cluster = code >> 13
        best = rows[start + top : start + top + step, :]
        for part in range(parts):
            lanes = slice(part * 128, part * 128 + 128)
            sims = sims_ref[top : top + step, lanes]
            sims = jnp.where(cluster == right_cluster[:, lanes], sims, 0.0)
            earlier = right_pos[:, lanes] < pos
            best = jnp.maximum(best, jnp.where(earlier, sims, 0.0))
            if top < same:
                later = jnp.where(earlier, 0.0, sims)
                best_col[part] = jnp.maximum(
                    best_col[part], jnp.max(later.reshape(-1, 8, 128), axis=0)
                )
        rows[start + top : start + top + step, :] = best
    if same > 0:
        for part in range(parts):
            lanes = slice(col_start + part * 128, col_start + part * 128 + 128)
            col[:, lanes] = jnp.maximum(col[:, lanes], best_col[part])


def row_result(row_ref):
    return jnp.max(jnp.transpose(row_ref[...]), axis=0, keepdims=True)


def col_result(col_ref):
    return jnp.max(col_ref[...], axis=0, keepdims=True)


OWN, SIB, LOW, LOWS, HIGH = range(5)


class Tiles:
    def __init__(self, parts, meta, codes, rows, cols, row_classes, col_classes):
        self.meta, self.codes, self.rows, self.cols = meta, codes, rows, cols
        self.row_classes, self.col_classes = row_classes, col_classes
        self.relatives = relatives()
        self.parts = {}
        for cls, ref, at, quarter, count in parts:
            for q in range(quarter, quarter + count):
                self.parts[cls, q] = (ref, at if len(ref.shape) == 3 else (q - quarter) * QUARTER)
        for cls in row_classes:
            rows[cls, :, :] = jnp.zeros(rows.shape[1:], F32)
        for cls in col_classes:
            cols[cls, :, :] = jnp.zeros(cols.shape[1:], F32)

    def load(self, cls, quarter, count=1):
        ref, at = self.parts[cls, quarter]
        if len(ref.shape) == 3:
            return ref[:, at : at + QUARTER // ref.shape[0], :].reshape(QUARTER, -1)
        return ref[at : at + count * QUARTER, :]

    def piece(self, left, quarter, count, right, right_quarter, same=None):
        lanes = slice(right_quarter * QUARTER, (right_quarter + 1) * QUARTER)
        place = self.relatives[right]
        return dict(
            left=lambda: self.load(left, quarter, count),
            right=lambda: self.load(right, right_quarter),
            count=count * QUARTER,
            codes=self.codes,
            cls=left,
            rows=self.rows.at[left],
            start=quarter * QUARTER,
            pos_row=lambda: self.meta[0, pl.ds(place, 1), lanes],
            cluster_row=lambda: self.meta[1, pl.ds(place, 1), lanes],
            col=self.cols.at[right],
            col_start=right_quarter * QUARTER,
            same=count * QUARTER if same is None else same,
        )

    def matched(self, flip, left, right, pairs):
        pieces = []
        for b in range(4):
            mine = [a for a in range(4) if (a, b) in pairs and (a // 2 + b // 2) % 2 == flip]
            if mine == [0, 1] and self.parts[left, 0][0] is self.parts[left, 1][0]:
                pieces.append(self.piece(left, 0, 2, right, b))
            else:
                pieces += [self.piece(left, a, 1, right, b) for a in mine]
        return pieces

    def result(self, cls):
        best = []
        if cls in self.row_classes:
            best.append(row_result(self.rows.at[cls]))
        if cls in self.col_classes:
            best.append(col_result(self.cols.at[cls]))
        return functools.reduce(jnp.maximum, best)


def either(flag, work):
    pl.when(flag)(lambda: work(1))
    pl.when(jnp.logical_not(flag))(lambda: work(0))


def second_core():
    return lax.axis_index("grp") % 2 == 1


def outer_chip():
    chip = lax.axis_index("grp") // 2
    return (chip == 0) | (chip == 3)


ALL_PAIRS = [(a, b) for a in range(4) for b in range(4)]


def follow_kernel(rows, after, also_after, out):
    del rows, after, also_after, out


def join_kernel(pools, rest, low_rest, high_rest, out):
    width = QUARTER // pools
    for n, part in enumerate((rest, low_rest, high_rest)):
        out[:, n * width : (n + 1) * width, :] = part[...].reshape(pools, width, -1)


def near_kernel(own0, sib0, meta, codes, out, sims, rows, cols):
    moves = [(OWN, own0, None, 0, 3), (SIB, sib0, None, 0, 3)]
    tiles = Tiles(
        moves, meta, codes, rows, cols, (OWN,), (OWN, SIB))
    run([tiles.piece(OWN, 0, b + 1, OWN, b, same=b * QUARTER) for b in range(3)], sims)
    pairs = [(a, b) for a, b in ALL_PAIRS if 3 not in (a, b)]
    either(second_core(), lambda flip: run(tiles.matched(flip, OWN, SIB, pairs), sims))
    out[...] = jnp.zeros(out.shape, F32)
    for cls in (OWN, SIB):
        out[cls : cls + 1, :] = tiles.result(cls)


def middle_kernel(
    own0, arrived, sib0, meta, codes, near, out, own_out, arrived_out, sib_out, sims, rows, cols
):
    width = arrived.shape[1] // 3
    moves = [
        (OWN, own0, None, 0, 3), (OWN, arrived, 0, 3, 1), (HIGH, arrived, 2 * width, 3, 1),
        (SIB, sib0, None, 0, 3),
    ]
    tiles = Tiles(moves, meta, codes, rows, cols, (OWN, SIB), (OWN, HIGH))
    pieces = [tiles.piece(OWN, 0, 3, OWN, 3), tiles.piece(OWN, 3, 1, OWN, 3, same=0)]
    pieces += [tiles.piece(OWN, 0, 3, HIGH, 3), tiles.piece(OWN, 3, 1, HIGH, 3)]
    pieces += [tiles.piece(SIB, 0, 3, HIGH, 3)]
    run(pieces, sims)
    own_out[...] = own0[...]
    arrived_out[...] = arrived[...]
    sib_out[...] = sib0[...]
    out[...] = near[...]
    for cls in (OWN, SIB, HIGH):
        out[cls : cls + 1, :] = jnp.maximum(near[cls : cls + 1, :], tiles.result(cls))


def main_kernel(
    own0, arrived, high0, sib0, swapped, low0, meta, codes, before, out, sims, rows, cols
):
    width = arrived.shape[1] // 3
    moves = [
        (HIGH, high0, None, 0, 3), (OWN, own0, None, 0, 3), (OWN, arrived, 0, 3, 1),
        (SIB, sib0, None, 0, 3), (SIB, swapped, 0, 3, 1), (HIGH, arrived, 2 * width, 3, 1),
        (LOW, low0, None, 0, 3), (LOW, arrived, width, 3, 1),
    ]
    tiles = Tiles(moves, meta, codes, rows, cols, (OWN, SIB, LOW), (SIB, HIGH))
    pieces = []
    for b in range(3):
        for cls in (OWN, SIB):
            pieces += [tiles.piece(cls, 0, 3, HIGH, b), tiles.piece(cls, 3, 1, HIGH, b)]
    pieces += [tiles.piece(SIB, 3, 1, HIGH, 3)]
    run(pieces, sims)
    pairs = [(a, b) for a, b in ALL_PAIRS if 3 in (a, b)]
    either(second_core(), lambda flip: run(tiles.matched(flip, OWN, SIB, pairs), sims))
    either(outer_chip(), lambda flip: run(tiles.matched(flip, LOW, HIGH, ALL_PAIRS), sims))
    for cls in (OWN, SIB, LOW, HIGH):
        out[cls : cls + 1, :] = jnp.maximum(before[cls : cls + 1, :], tiles.result(cls))


def last_kernel(
    pools, group, main, rest, lows0, high0, swapped, arrived, meta, codes, before, out,
    sims, rows, cols, every, upper, sem,
):
    width = swapped.shape[1] // 3
    copy = pltpu.make_async_copy(arrived.at[:, pl.ds(2 * width, width), :], upper, sem)
    copy.start()
    moves = [
        (LOWS, lows0, None, 0, 3), (LOWS, swapped, width, 3, 1), (HIGH, high0, None, 0, 3),
        (HIGH, upper, 0, 3, 1),
    ]
    tiles = Tiles(
        moves, meta, codes, rows, cols, (LOWS,), (HIGH,))
    copy.wait()
    either(outer_chip(), lambda flip: run(tiles.matched(flip, LOWS, HIGH, ALL_PAIRS), sims))
    every[...] = jnp.zeros(every.shape, F32)
    for cls, place in enumerate(tiles.relatives):
        best = [] if cls == LOWS else [before[cls : cls + 1, :]]
        if cls in (LOWS, HIGH):
            best.append(tiles.result(cls))
        every[pl.ds(place, 1), :] = functools.reduce(jnp.maximum, best)
    for p in range(pools):
        rows_out = slice(p * group, (p + 1) * group)
        out[rows_out, :main] = every[:, p * main : (p + 1) * main]
        at = pools * main + p * rest
        out[rows_out, main:] = every[:, at : at + rest]


def score_kernel(pools, group, places, table_ref, returned_ref, out_ref):
    rows_dev = out_ref.shape[1]
    arrived = jnp.transpose(
        jnp.concatenate([returned_ref[...], jnp.zeros_like(returned_ref)], axis=1)
    )
    table = table_ref[...]
    row = iota((8, rows_dev), 1)
    total = jnp.zeros((8, rows_dev), F32)
    for p in range(pools):
        for k in range(places):
            value = jnp.max(
                arrived[k * group : (k + 1) * group, p * group : (p + 1) * group],
                axis=1,
                keepdims=True,
            )
            entry = table[p * group : (p + 1) * group, k : k + 1]
            total = jnp.where(entry == row, value, total)
    out_ref[...] = jnp.sum(total, axis=0, keepdims=True)


def body(embeddings, members, valid, block_cluster):
    rows_dev, feature = embeddings.shape
    pools = lax.axis_size("pool")
    group = lax.axis_size("grp")
    devices = pools * group
    places = rows_dev // devices
    last = places // 4
    sds = jax.ShapeDtypeStruct
    hbm = pl.BlockSpec(memory_space=pltpu.HBM)
    valid_row = valid.reshape(1, -1)
    cluster_row = block_cluster.reshape(1, -1)
    blocks, block_len = members.shape

    some = jnp.any(valid > 0)
    table, main = pl.pallas_call(
        lambda *refs: table_kernel(pools, group, places, last, *refs),
        out_shape=(
            sds((devices, 128), I32),
            sds((3 * QUARTER, feature), BF16),
        ),
        in_specs=[hbm] * 3,
        scratch_shapes=[
            pltpu.VMEM((blocks, block_len), I32),
            pltpu.VMEM((1, blocks), I32),
            pltpu.VMEM((rows_dev, feature), BF16),
            pltpu.VMEM((blocks, 128), F32),
            pltpu.SemaphoreType.DMA((3,)),
        ],
        compiler_params=TABLE_PARAMS,
        cost_estimate=cost(rows_dev * rows_dev * feature),
        name="table",
    )(members, valid_row, embeddings)
    meta, codes = pl.pallas_call(
        lambda *refs: meta_kernel(group, places, last, *refs),
        out_shape=(sds((2, group, rows_dev), I32), sds((rows_dev, 128), I32)),
        in_specs=[hbm] * 3,
        scratch_shapes=[
            pltpu.VMEM((2 * group, block_len), I32),
            pltpu.VMEM((1, blocks), I32),
            pltpu.VMEM((1, blocks), I32),
            pltpu.VMEM((128, rows_dev), I32),
            pltpu.SemaphoreType.DMA((3,)),
        ],
        compiler_params=PARAMS,
        cost_estimate=cost(2 * rows_dev**3),
        name="meta",
    )(members, valid_row, cluster_row)

    def shift(rows, by):
        return lax.ppermute(rows, "grp", [(g, (g + by) % group) for g in range(group)])

    def swap(rows):
        return lax.ppermute(rows, "grp", [(g, g ^ 1) for g in range(group)])

    def follow(rows, after, also_after):
        return pl.pallas_call(
            follow_kernel,
            out_shape=sds(rows.shape, BF16),
            in_specs=[hbm] * 3,
            out_specs=hbm,
            input_output_aliases={0: 0},
            compiler_params=PARAMS,
            name="follow",
        )(rows, after, also_after)

    def to_pools(rows):
        return lax.all_to_all(rows, "pool", split_axis=0, concat_axis=0, tiled=True)

    vmem = pl.BlockSpec(memory_space=pltpu.VMEM)
    rest = pl.pallas_call(
        lambda *refs: rest_kernel(pools, places, last, *refs),
        out_shape=sds((QUARTER, feature), BF16),
        in_specs=[vmem, vmem, hbm],
        compiler_params=PARAMS,
        name="rest",
    )(table, embeddings, meta)
    low_rest, high_rest = shift(rest, 2), shift(rest, -2)
    own0 = to_pools(main.reshape(pools, -1, feature)).reshape(-1, feature)
    sent = pl.pallas_call(
        lambda *refs: join_kernel(pools, *refs),
        out_shape=sds((pools, 3 * QUARTER // pools, feature), BF16),
        compiler_params=PARAMS,
        name="join",
    )(rest, low_rest, high_rest)
    own0 = follow(own0, sent, some.astype(I32).reshape(1, 1))
    low0, high0 = shift(own0, 2), shift(own0, -2)
    sib0 = swap(own0)

    def tiles(kernel, name, squares, operands, small, out_shape=(8, rows_dev), more=(), specs=None, kept=()):
        return pl.pallas_call(
            kernel,
            out_shape=(sds(out_shape, F32), *kept) if kept else sds(out_shape, F32),
            in_specs=specs or [vmem] * (len(operands) + len(small)),
            scratch_shapes=[
                pltpu.VMEM((2, 3 * QUARTER, QUARTER), F32),
                pltpu.VMEM((4, rows_dev, 128), F32),
                pltpu.VMEM((5, 8, rows_dev), F32),
                *more,
            ],
            compiler_params=PARAMS,
            cost_estimate=cost(squares * QUARTER * QUARTER * feature),
            name=name,
        )(*operands, *small)

    def bring(sent, own0, sib0, meta, codes):
        near = tiles(near_kernel, "near", 11, (own0, sib0), (meta, codes))
        return to_pools(sent), near

    def bring_nothing(sent, own0, sib0, meta, codes):
        return jnp.zeros_like(sent), jnp.zeros((8, rows_dev), F32)

    arrived, near = lax.cond(
        some, bring, bring_nothing, sent, own0, sib0, meta, codes
    )
    swapped = swap(arrived)
    middle, own0, arrived, sib0 = tiles(
        middle_kernel, "middle", 11, (own0, arrived, sib0), (meta, codes, near),
        kept=[sds(kept.shape, BF16) for kept in (own0, arrived, sib0)],
    )
    low0 = follow(low0, middle, high0)
    best = tiles(
        main_kernel, "main", 37, (own0, arrived, high0, sib0, swapped, low0), (meta, codes, middle)
    )
    best = tiles(
        lambda *refs: last_kernel(pools, group, group * (places - last), group * last, *refs),
        "last", 8, (swap(low0), high0, swapped, arrived), (meta, codes, best),
        out_shape=(devices, group * places),
        more=(
            pltpu.VMEM((group, rows_dev), F32),
            pltpu.VMEM((pools, QUARTER // pools, feature), BF16),
            pltpu.SemaphoreType.DMA,
        ),
        specs=[vmem] * 3 + [hbm] + [vmem] * 3,
    )
    returned = lax.all_to_all(best, ("pool", "grp"), split_axis=0, concat_axis=0, tiled=True)
    scores = pl.pallas_call(
        lambda *refs: score_kernel(pools, group, places, *refs),
        out_shape=sds((1, rows_dev), F32),
        compiler_params=PARAMS,
        name="score",
    )(table, returned)
    return scores.reshape(rows_dev)


def cost(products):
    return pl.CostEstimate(flops=2 * products, bytes_accessed=0, transcendentals=0)


def solution(mesh):
    in_specs = (P(("pool", "grp"), None), P(), P(), P())
    out_specs = P(("pool", "grp"))
    return jax.shard_map(body, mesh=mesh, in_specs=in_specs, out_specs=out_specs, check_vma=False)
```

```python
import functools

import jax
import jax.numpy as jnp
from jax import lax
from jax.experimental import pallas as pl
from jax.experimental.pallas import tpu as pltpu
from jax.sharding import PartitionSpec as P

EPS = 1e-06
F32 = jnp.float32
BF16 = jnp.bfloat16
I32 = jnp.int32
QUARTER = 256
CODE = 8192
NT = (((1,), (1,)), ((), ()))
PARAMS = pltpu.CompilerParams(vmem_limit_bytes=12 * 1024 * 1024)
TABLE_PARAMS = pltpu.CompilerParams(vmem_limit_bytes=62 * 1024 * 1024)


def iota(shape, dim):
    return lax.broadcasted_iota(I32, shape, dim)


def normal_rows(rows):
    return (rows * lax.rsqrt(jnp.sum(rows * rows, axis=1, keepdims=True) + EPS)).astype(BF16)


def picked_rows(table, emb, first, count, pools):
    width = emb.shape[0]
    wanted = []
    for k in range(first, first + count):
        hit = table[:, k : k + 1] == iota((table.shape[0], width), 1)
        wanted.append(jnp.where(hit, 1.0, 0.0).reshape(pools, -1, width))
    choice = jnp.concatenate(wanted, axis=1).reshape(-1, width).astype(BF16)
    return normal_rows(jnp.dot(choice, emb, preferred_element_type=F32))


def table_kernel(
    pools, group, places, last, members_hbm, valid_hbm, emb_hbm, table_ref, main_ref,
    members_ref, valid_ref, emb_ref, found_ref, sems,
):
    copies = []
    for n, (source, target) in enumerate(
        ((members_hbm, members_ref), (valid_hbm, valid_ref), (emb_hbm, emb_ref))
    ):
        copies.append(pltpu.make_async_copy(source, target, sems.at[n]))
        copies[-1].start()
    rows_dev = emb_ref.shape[0]
    device = lax.axis_index("pool") * group + lax.axis_index("grp")
    blocks, block_len = members_ref.shape
    devices = blocks // 2
    before = jnp.where(
        iota((block_len, block_len), 0) < iota((block_len, block_len), 1), 1.0, 0.0
    ).astype(BF16)
    at = iota((blocks, blocks), 1) == iota((blocks, blocks), 0)
    copies[0].wait()
    copies[1].wait()
    live = jnp.sum(jnp.where(at, valid_ref[...], 0), axis=1, keepdims=True)
    local = members_ref[...] - device * rows_dev
    mine = (local >= 0) & (local < rows_dev) & (iota((blocks, block_len), 1) < live)
    ones = jnp.where(mine, 1.0, 0.0)
    counts = jnp.broadcast_to(jnp.sum(ones, axis=1, keepdims=True), (blocks, 128))
    counts = jnp.where(iota((blocks, 128), 0) % 2 == 1, pltpu.roll(counts, 1, 0), 0.0)
    rank = jnp.dot(ones.astype(BF16), before, preferred_element_type=F32) + counts[:, :1]
    rank = jnp.where(mine, rank, -1.0)
    value = (local + 1).astype(F32)
    lane = iota((blocks, 128), 1)
    found = jnp.zeros((blocks, 128), F32)
    for k in range(places):
        entry = jnp.sum(jnp.where(rank == k, value, 0.0), axis=1, keepdims=True)
        found = jnp.where(lane == k, entry, found)
    found_ref[...] = found
    pair = found_ref[pl.ds(0, devices, stride=2), :] + found_ref[pl.ds(1, devices, stride=2), :]
    table = pair.astype(I32) - 1
    table_ref[...] = table
    copies[2].wait()
    for first in range(0, places - last, last):
        part = picked_rows(table, emb_ref[...], first, last, pools)
        part = part.reshape(pools, last * group, -1)
        main_ref[:, first * group : (first + last) * group, :] = part


def rest_kernel(pools, places, last, table_ref, emb_ref, after, out):
    del after
    out[...] = picked_rows(table_ref[...], emb_ref[...], places - last, last, pools)


def relatives():
    group = lax.axis_size("grp")
    index = lax.axis_index("grp")
    flip = 1 - 2 * (index % 2)
    below = (index + group - 2) % group
    return index, index + flip, below, below + flip, (index + 2) % group


def meta_kernel(
    group, places, last, members_hbm, valid_hbm, cluster_hbm, out_ref, codes_ref,
    members_ref, valid_ref, cluster_ref, packed_ref, sems,
):
    blocks = valid_ref.shape[1]
    block_len = members_ref.shape[1]
    pool = lax.axis_index("pool")
    first_block = pl.multiple_of(pool * 2 * group, 2 * group)
    copies = []
    for n, (source, target) in enumerate(
        (
            (members_hbm.at[pl.ds(first_block, 2 * group), :], members_ref),
            (valid_hbm, valid_ref),
            (cluster_hbm, cluster_ref),
        )
    ):
        copies.append(pltpu.make_async_copy(source, target, sems.at[n]))
        copies[-1].start()
    sources = blocks // 2
    slots = 2 * block_len
    width = group * places
    before = jnp.where(iota((slots, slots), 0) < iota((slots, slots), 1), 1.0, 0.0).astype(BF16)
    slot = iota((1, slots), 1)
    kind = iota((2 * width, slots), 0)
    kind_place = kind % width // group
    kind_owner = kind % group
    kind_value = jnp.where(kind < width, slot // 32, slot % 32 + 1)
    found = jnp.zeros((sources, 2 * width), F32)
    block_lane = iota((1, blocks), 1)
    lane = iota((1, width), 1)
    first_cluster = jnp.zeros((1, width), I32)
    second_cluster = jnp.zeros((1, width), I32)
    for copy in copies:
        copy.wait()
    for owner in range(group):
        halves, lives = [], []
        for half in range(2):
            halves.append(members_ref[2 * owner + half : 2 * owner + half + 1, :])
            at = block_lane == first_block + 2 * owner + half
            lives.append(jnp.sum(jnp.where(at, valid_ref[...], 0), axis=1, keepdims=True))
            cluster = jnp.sum(jnp.where(at, cluster_ref[...], 0), axis=1, keepdims=True)
            if half == 0:
                first_cluster = jnp.where(lane % group == owner, cluster, first_cluster)
            else:
                second_cluster = jnp.where(lane % group == owner, cluster, second_cluster)
        rows = jnp.concatenate(halves, axis=1)
        end = jnp.where(slot < block_len, lives[0], block_len + lives[1])
        origin = jnp.where(slot < end, rows // slots, -1)
        match = iota((sources, slots), 0) == origin
        ones = jnp.where(match, 1.0, 0.0).astype(BF16)
        ranks = jnp.dot(ones, before, preferred_element_type=F32)
        rank = jnp.sum(jnp.where(match, ranks, 0.0), axis=0, keepdims=True).astype(I32)
        weight = jnp.where((kind_owner == owner) & (kind_place == rank), kind_value, 0)
        found = found + lax.dot_general(
            ones, weight.astype(F32).astype(BF16), NT, preferred_element_type=F32
        )
    found = found.astype(I32)
    place = found[:, :width] * 32 + found[:, width:] - 1
    filled = found[:, width:] > 0
    position = jnp.where(filled, place + lane % group * slots, -1)
    cluster = jnp.where(filled, jnp.where(place < block_len, first_cluster, second_cluster), -1)
    main = (places - last) * group
    rest = last * group
    pools = sources // group
    for n, values in enumerate((position, cluster)):
        for p in range(pools):
            own = values[p * group : (p + 1) * group, :]
            out_ref[n, :, p * main : (p + 1) * main] = own[:, :main]
            at = pools * main + p * rest
            out_ref[n, :, at : at + rest] = own[:, main:]
    packed_ref[...] = jnp.zeros(packed_ref.shape, I32)
    for n, cls in enumerate(relatives()[:4]):
        pos = out_ref[0, pl.ds(cls, 1), :]
        cluster = out_ref[1, pl.ds(cls, 1), :]
        packed_ref[n : n + 1, :] = jnp.where(cluster < 0, -2 * CODE, cluster * CODE + pos)
    codes_ref[...] = jnp.transpose(packed_ref[...])


def run(pieces, sims_ref):
    for n in range(len(pieces) + 1):
        if n < len(pieces):
            piece = pieces[n]
            sims_ref[n % 2, : piece["count"], :] = lax.dot_general(
                piece["left"](), piece["right"](), NT, preferred_element_type=F32
            )
        if n > 0:
            take_maxima(sims_ref.at[(n - 1) % 2], **pieces[n - 1])


def take_maxima(sims_ref, left, right, count, codes, cls, rows, start, pos_row, cluster_row, col, col_start, same):
    step = 128
    right_pos, right_cluster = pos_row(), cluster_row()
    parts = QUARTER // 128
    best_col = [jnp.zeros((8, 128), F32) for _ in range(parts)]
    for top in range(0, count, step):
        code = codes[start + top : start + top + step, cls : cls + 1]
        code = jnp.broadcast_to(code, (step, 128))
        pos = code & (CODE - 1)
        cluster = code >> 13
        best = rows[start + top : start + top + step, :]
        for part in range(parts):
            lanes = slice(part * 128, part * 128 + 128)
            sims = sims_ref[top : top + step, lanes]
            sims = jnp.where(cluster == right_cluster[:, lanes], sims, 0.0)
            earlier = right_pos[:, lanes] < pos
            best = jnp.maximum(best, jnp.where(earlier, sims, 0.0))
            if top < same:
                later = jnp.where(earlier, 0.0, sims)
                best_col[part] = jnp.maximum(
                    best_col[part], jnp.max(later.reshape(-1, 8, 128), axis=0)
                )
        rows[start + top : start + top + step, :] = best
    if same > 0:
        for part in range(parts):
            lanes = slice(col_start + part * 128, col_start + part * 128 + 128)
            col[:, lanes] = jnp.maximum(col[:, lanes], best_col[part])


def row_result(row_ref):
    return jnp.max(jnp.transpose(row_ref[...]), axis=0, keepdims=True)


def col_result(col_ref):
    return jnp.max(col_ref[...], axis=0, keepdims=True)


OWN, SIB, LOW, LOWS, HIGH = range(5)


class Tiles:
    def __init__(self, parts, meta, codes, rows, cols, row_classes, col_classes):
        self.meta, self.codes, self.rows, self.cols = meta, codes, rows, cols
        self.row_classes, self.col_classes = row_classes, col_classes
        self.relatives = relatives()
        self.parts = {}
        for cls, ref, at, quarter, count in parts:
            for q in range(quarter, quarter + count):
                self.parts[cls, q] = (ref, at if len(ref.shape) == 3 else (q - quarter) * QUARTER)
        for cls in row_classes:
            rows[cls, :, :] = jnp.zeros(rows.shape[1:], F32)
        for cls in col_classes:
            cols[cls, :, :] = jnp.zeros(cols.shape[1:], F32)

    def load(self, cls, quarter, count=1):
        ref, at = self.parts[cls, quarter]
        if len(ref.shape) == 3:
            return ref[:, at : at + QUARTER // ref.shape[0], :].reshape(QUARTER, -1)
        return ref[at : at + count * QUARTER, :]

    def piece(self, left, quarter, count, right, right_quarter, same=None):
        lanes = slice(right_quarter * QUARTER, (right_quarter + 1) * QUARTER)
        place = self.relatives[right]
        return dict(
            left=lambda: self.load(left, quarter, count),
            right=lambda: self.load(right, right_quarter),
            count=count * QUARTER,
            codes=self.codes,
            cls=left,
            rows=self.rows.at[left],
            start=quarter * QUARTER,
            pos_row=lambda: self.meta[0, pl.ds(place, 1), lanes],
            cluster_row=lambda: self.meta[1, pl.ds(place, 1), lanes],
            col=self.cols.at[right],
            col_start=right_quarter * QUARTER,
            same=count * QUARTER if same is None else same,
        )

    def matched(self, flip, left, right, pairs):
        pieces = []
        for b in range(4):
            mine = [a for a in range(4) if (a, b) in pairs and (a // 2 + b // 2) % 2 == flip]
            if mine == [0, 1] and self.parts[left, 0][0] is self.parts[left, 1][0]:
                pieces.append(self.piece(left, 0, 2, right, b))
            else:
                pieces += [self.piece(left, a, 1, right, b) for a in mine]
        return pieces

    def result(self, cls):
        best = []
        if cls in self.row_classes:
            best.append(row_result(self.rows.at[cls]))
        if cls in self.col_classes:
            best.append(col_result(self.cols.at[cls]))
        return functools.reduce(jnp.maximum, best)


def either(flag, work):
    pl.when(flag)(lambda: work(1))
    pl.when(jnp.logical_not(flag))(lambda: work(0))


def second_core():
    return lax.axis_index("grp") % 2 == 1


def outer_chip():
    chip = lax.axis_index("grp") // 2
    return (chip == 0) | (chip == 3)


ALL_PAIRS = [(a, b) for a in range(4) for b in range(4)]


def follow_kernel(rows, after, also_after, out):
    del rows, after, also_after, out


def join_kernel(pools, rest, low_rest, high_rest, out):
    width = QUARTER // pools
    for n, part in enumerate((rest, low_rest, high_rest)):
        out[:, n * width : (n + 1) * width, :] = part[...].reshape(pools, width, -1)


def near_kernel(own0, sib0, meta, codes, out, sims, rows, cols):
    moves = [(OWN, own0, None, 0, 3), (SIB, sib0, None, 0, 3)]
    tiles = Tiles(
        moves, meta, codes, rows, cols, (OWN,), (OWN, SIB))
    run([tiles.piece(OWN, 0, b + 1, OWN, b, same=b * QUARTER) for b in range(3)], sims)
    pairs = [(a, b) for a, b in ALL_PAIRS if 3 not in (a, b)]
    either(second_core(), lambda flip: run(tiles.matched(flip, OWN, SIB, pairs), sims))
    out[...] = jnp.zeros(out.shape, F32)
    for cls in (OWN, SIB):
        out[cls : cls + 1, :] = tiles.result(cls)


def middle_kernel(
    own0, arrived, sib0, meta, codes, near, out, own_out, arrived_out, sib_out, codes_out,
    sims, rows, cols
):
    width = arrived.shape[1] // 3
    moves = [
        (OWN, own0, None, 0, 3), (OWN, arrived, 0, 3, 1), (HIGH, arrived, 2 * width, 3, 1),
        (SIB, sib0, None, 0, 3),
    ]
    tiles = Tiles(moves, meta, codes, rows, cols, (OWN, SIB), (OWN, HIGH))
    pieces = [tiles.piece(OWN, 0, 3, OWN, 3), tiles.piece(OWN, 3, 1, OWN, 3, same=0)]
    pieces += [tiles.piece(OWN, 0, 3, HIGH, 3), tiles.piece(OWN, 3, 1, HIGH, 3)]
    pieces += [tiles.piece(SIB, 0, 3, HIGH, 3)]
    run(pieces, sims)
    own_out[...] = own0[...]
    arrived_out[...] = arrived[...]
    sib_out[...] = sib0[...]
    codes_out[...] = codes[...]
    out[...] = near[...]
    for cls in (OWN, SIB, HIGH):
        out[cls : cls + 1, :] = jnp.maximum(near[cls : cls + 1, :], tiles.result(cls))


def main_kernel(
    own0, arrived, high0, sib0, swapped, low0, meta, codes, before, out, sims, rows, cols
):
    width = arrived.shape[1] // 3
    moves = [
        (HIGH, high0, None, 0, 3), (OWN, own0, None, 0, 3), (OWN, arrived, 0, 3, 1),
        (SIB, sib0, None, 0, 3), (SIB, swapped, 0, 3, 1), (HIGH, arrived, 2 * width, 3, 1),
        (LOW, low0, None, 0, 3), (LOW, arrived, width, 3, 1),
    ]
    tiles = Tiles(moves, meta, codes, rows, cols, (OWN, SIB, LOW), (SIB, HIGH))
    pieces = []
    for b in range(3):
        for cls in (OWN, SIB):
            pieces += [tiles.piece(cls, 0, 3, HIGH, b), tiles.piece(cls, 3, 1, HIGH, b)]
    pieces += [tiles.piece(SIB, 3, 1, HIGH, 3)]
    run(pieces, sims)
    pairs = [(a, b) for a, b in ALL_PAIRS if 3 in (a, b)]
    either(second_core(), lambda flip: run(tiles.matched(flip, OWN, SIB, pairs), sims))
    either(outer_chip(), lambda flip: run(tiles.matched(flip, LOW, HIGH, ALL_PAIRS), sims))
    for cls in (OWN, SIB, LOW, HIGH):
        out[cls : cls + 1, :] = jnp.maximum(before[cls : cls + 1, :], tiles.result(cls))


def last_kernel(
    pools, group, main, rest, lows0, high0, swapped, arrived, meta, codes, before, out,
    sims, rows, cols, every, upper, sem,
):
    width = swapped.shape[1] // 3
    copy = pltpu.make_async_copy(arrived.at[:, pl.ds(2 * width, width), :], upper, sem)
    copy.start()
    moves = [
        (LOWS, lows0, None, 0, 3), (LOWS, swapped, width, 3, 1), (HIGH, high0, None, 0, 3),
        (HIGH, upper, 0, 3, 1),
    ]
    tiles = Tiles(
        moves, meta, codes, rows, cols, (LOWS,), (HIGH,))
    copy.wait()
    either(outer_chip(), lambda flip: run(tiles.matched(flip, LOWS, HIGH, ALL_PAIRS), sims))
    every[...] = jnp.zeros(every.shape, F32)
    for cls, place in enumerate(tiles.relatives):
        best = [] if cls == LOWS else [before[cls : cls + 1, :]]
        if cls in (LOWS, HIGH):
            best.append(tiles.result(cls))
        every[pl.ds(place, 1), :] = functools.reduce(jnp.maximum, best)
    for p in range(pools):
        rows_out = slice(p * group, (p + 1) * group)
        out[rows_out, :main] = every[:, p * main : (p + 1) * main]
        at = pools * main + p * rest
        out[rows_out, main:] = every[:, at : at + rest]


def score_kernel(pools, group, places, table_ref, returned_ref, out_ref):
    rows_dev = out_ref.shape[1]
    arrived = jnp.transpose(
        jnp.concatenate([returned_ref[...], jnp.zeros_like(returned_ref)], axis=1)
    )
    table = table_ref[...]
    row = iota((8, rows_dev), 1)
    total = jnp.zeros((8, rows_dev), F32)
    for p in range(pools):
        for k in range(places):
            value = jnp.max(
                arrived[k * group : (k + 1) * group, p * group : (p + 1) * group],
                axis=1,
                keepdims=True,
            )
            entry = table[p * group : (p + 1) * group, k : k + 1]
            total = jnp.where(entry == row, value, total)
    out_ref[...] = jnp.sum(total, axis=0, keepdims=True)


def body(embeddings, members, valid, block_cluster):
    rows_dev, feature = embeddings.shape
    pools = lax.axis_size("pool")
    group = lax.axis_size("grp")
    devices = pools * group
    places = rows_dev // devices
    last = places // 4
    sds = jax.ShapeDtypeStruct
    hbm = pl.BlockSpec(memory_space=pltpu.HBM)
    valid_row = valid.reshape(1, -1)
    cluster_row = block_cluster.reshape(1, -1)
    blocks, block_len = members.shape

    some = jnp.any(valid > 0)
    table, main = pl.pallas_call(
        lambda *refs: table_kernel(pools, group, places, last, *refs),
        out_shape=(
            sds((devices, 128), I32),
            sds((pools, 3 * QUARTER // pools, feature), BF16),
        ),
        in_specs=[hbm] * 3,
        scratch_shapes=[
            pltpu.VMEM((blocks, block_len), I32),
            pltpu.VMEM((1, blocks), I32),
            pltpu.VMEM((rows_dev, feature), BF16),
            pltpu.VMEM((blocks, 128), F32),
            pltpu.SemaphoreType.DMA((3,)),
        ],
        compiler_params=TABLE_PARAMS,
        cost_estimate=cost(rows_dev * rows_dev * feature),
        name="table",
    )(members, valid_row, embeddings)
    meta, codes = pl.pallas_call(
        lambda *refs: meta_kernel(group, places, last, *refs),
        out_shape=(sds((2, group, rows_dev), I32), sds((rows_dev, 128), I32)),
        in_specs=[hbm] * 3,
        scratch_shapes=[
            pltpu.VMEM((2 * group, block_len), I32),
            pltpu.VMEM((1, blocks), I32),
            pltpu.VMEM((1, blocks), I32),
            pltpu.VMEM((128, rows_dev), I32),
            pltpu.SemaphoreType.DMA((3,)),
        ],
        compiler_params=PARAMS,
        cost_estimate=cost(2 * rows_dev**3),
        name="meta",
    )(members, valid_row, cluster_row)

    def shift(rows, by):
        return lax.ppermute(rows, "grp", [(g, (g + by) % group) for g in range(group)])

    def swap(rows):
        return lax.ppermute(rows, "grp", [(g, g ^ 1) for g in range(group)])

    def follow(rows, after, also_after):
        return pl.pallas_call(
            follow_kernel,
            out_shape=sds(rows.shape, BF16),
            in_specs=[hbm] * 3,
            out_specs=hbm,
            input_output_aliases={0: 0},
            compiler_params=PARAMS,
            name="follow",
        )(rows, after, also_after)

    def to_pools(rows):
        return lax.all_to_all(rows, "pool", split_axis=0, concat_axis=0, tiled=True)

    vmem = pl.BlockSpec(memory_space=pltpu.VMEM)
    rest = pl.pallas_call(
        lambda *refs: rest_kernel(pools, places, last, *refs),
        out_shape=sds((QUARTER, feature), BF16),
        in_specs=[vmem, vmem, hbm],
        compiler_params=PARAMS,
        name="rest",
    )(table, embeddings, meta)
    low_rest, high_rest = shift(rest, 2), shift(rest, -2)
    own0 = to_pools(main).reshape(-1, feature)
    sent = pl.pallas_call(
        lambda *refs: join_kernel(pools, *refs),
        out_shape=sds((pools, 3 * QUARTER // pools, feature), BF16),
        compiler_params=PARAMS,
        name="join",
    )(rest, low_rest, high_rest)
    own0 = follow(own0, sent, some.astype(I32).reshape(1, 1))
    low0, high0 = shift(own0, 2), shift(own0, -2)
    sib0 = swap(own0)

    def tiles(kernel, name, squares, operands, small, out_shape=(8, rows_dev), more=(), specs=None, kept=()):
        return pl.pallas_call(
            kernel,
            out_shape=(sds(out_shape, F32), *kept) if kept else sds(out_shape, F32),
            in_specs=specs or [vmem] * (len(operands) + len(small)),
            scratch_shapes=[
                pltpu.VMEM((2, 3 * QUARTER, QUARTER), F32),
                pltpu.VMEM((4, rows_dev, 128), F32),
                pltpu.VMEM((5, 8, rows_dev), F32),
                *more,
            ],
            compiler_params=PARAMS,
            cost_estimate=cost(squares * QUARTER * QUARTER * feature),
            name=name,
        )(*operands, *small)

    def bring(sent, own0, sib0, meta, codes):
        near = tiles(near_kernel, "near", 11, (own0, sib0), (meta, codes))
        return to_pools(sent), near

    def bring_nothing(sent, own0, sib0, meta, codes):
        return jnp.zeros_like(sent), jnp.zeros((8, rows_dev), F32)

    arrived, near = lax.cond(
        some, bring, bring_nothing, sent, own0, sib0, meta, codes
    )
    swapped = swap(arrived)
    middle, own0, arrived, sib0, codes = tiles(
        middle_kernel, "middle", 11, (own0, arrived, sib0), (meta, codes, near),
        kept=[sds(kept.shape, kept.dtype) for kept in (own0, arrived, sib0, codes)],
    )
    low0 = follow(low0, middle, high0)
    best = tiles(
        main_kernel, "main", 37, (own0, arrived, high0, sib0, swapped, low0), (meta, codes, middle)
    )
    best = tiles(
        lambda *refs: last_kernel(pools, group, group * (places - last), group * last, *refs),
        "last", 8, (swap(low0), high0, swapped, arrived), (meta, codes, best),
        out_shape=(devices, group * places),
        more=(
            pltpu.VMEM((group, rows_dev), F32),
            pltpu.VMEM((pools, QUARTER // pools, feature), BF16),
            pltpu.SemaphoreType.DMA,
        ),
        specs=[vmem] * 3 + [hbm] + [vmem] * 3,
    )
    returned = lax.all_to_all(best, ("pool", "grp"), split_axis=0, concat_axis=0, tiled=True)
    scores = pl.pallas_call(
        lambda *refs: score_kernel(pools, group, places, *refs),
        out_shape=sds((1, rows_dev), F32),
        compiler_params=PARAMS,
        name="score",
    )(table, returned)
    return scores.reshape(rows_dev)


def cost(products):
    return pl.CostEstimate(flops=2 * products, bytes_accessed=0, transcendentals=0)


def solution(mesh):
    in_specs = (P(("pool", "grp"), None), P(), P(), P())
    out_specs = P(("pool", "grp"))
    return jax.shard_map(body, mesh=mesh, in_specs=in_specs, out_specs=out_specs, check_vma=False)
```

```python
import functools

import jax
import jax.numpy as jnp
from jax import lax
from jax.experimental import pallas as pl
from jax.experimental.pallas import tpu as pltpu
from jax.sharding import PartitionSpec as P

EPS = 1e-06
F32 = jnp.float32
BF16 = jnp.bfloat16
I32 = jnp.int32
QUARTER = 256
CODE = 8192
NT = (((1,), (1,)), ((), ()))
PARAMS = pltpu.CompilerParams(vmem_limit_bytes=12 * 1024 * 1024)
TABLE_PARAMS = pltpu.CompilerParams(vmem_limit_bytes=62 * 1024 * 1024)


def iota(shape, dim):
    return lax.broadcasted_iota(I32, shape, dim)


def normal_rows(rows):
    return (rows * lax.rsqrt(jnp.sum(rows * rows, axis=1, keepdims=True) + EPS)).astype(BF16)


def picked_rows(table, emb, first, count, pools):
    width = emb.shape[0]
    wanted = []
    for k in range(first, first + count):
        hit = table[:, k : k + 1] == iota((table.shape[0], width), 1)
        wanted.append(jnp.where(hit, 1.0, 0.0).reshape(pools, -1, width))
    choice = jnp.concatenate(wanted, axis=1).reshape(-1, width).astype(BF16)
    return normal_rows(jnp.dot(choice, emb, preferred_element_type=F32))


def table_kernel(
    pools, group, places, last, members_hbm, valid_hbm, emb_hbm, table_ref, main_ref,
    members_ref, valid_ref, emb_ref, found_ref, sems,
):
    copies = []
    for n, (source, target) in enumerate(
        ((members_hbm, members_ref), (valid_hbm, valid_ref), (emb_hbm, emb_ref))
    ):
        copies.append(pltpu.make_async_copy(source, target, sems.at[n]))
        copies[-1].start()
    rows_dev = emb_ref.shape[0]
    device = lax.axis_index("pool") * group + lax.axis_index("grp")
    blocks, block_len = members_ref.shape
    devices = blocks // 2
    before = jnp.where(
        iota((block_len, block_len), 0) < iota((block_len, block_len), 1), 1.0, 0.0
    ).astype(BF16)
    at = iota((blocks, blocks), 1) == iota((blocks, blocks), 0)
    copies[0].wait()
    copies[1].wait()
    live = jnp.sum(jnp.where(at, valid_ref[...], 0), axis=1, keepdims=True)
    local = members_ref[...] - device * rows_dev
    mine = (local >= 0) & (local < rows_dev) & (iota((blocks, block_len), 1) < live)
    ones = jnp.where(mine, 1.0, 0.0)
    counts = jnp.broadcast_to(jnp.sum(ones, axis=1, keepdims=True), (blocks, 128))
    counts = jnp.where(iota((blocks, 128), 0) % 2 == 1, pltpu.roll(counts, 1, 0), 0.0)
    rank = jnp.dot(ones.astype(BF16), before, preferred_element_type=F32) + counts[:, :1]
    rank = jnp.where(mine, rank, -1.0)
    value = (local + 1).astype(F32)
    lane = iota((blocks, 128), 1)
    found = jnp.zeros((blocks, 128), F32)
    for k in range(places):
        entry = jnp.sum(jnp.where(rank == k, value, 0.0), axis=1, keepdims=True)
        found = jnp.where(lane == k, entry, found)
    found_ref[...] = found
    pair = found_ref[pl.ds(0, devices, stride=2), :] + found_ref[pl.ds(1, devices, stride=2), :]
    table = pair.astype(I32) - 1
    table_ref[...] = table
    copies[2].wait()
    for first in range(0, places - last, last):
        part = picked_rows(table, emb_ref[...], first, last, pools)
        part = part.reshape(pools, last * group, -1)
        main_ref[:, first * group : (first + last) * group, :] = part


def rest_kernel(pools, places, last, table_ref, emb_ref, out):
    out[...] = picked_rows(table_ref[...], emb_ref[...], places - last, last, pools)


def relatives():
    group = lax.axis_size("grp")
    index = lax.axis_index("grp")
    flip = 1 - 2 * (index % 2)
    below = (index + group - 2) % group
    return index, index + flip, below, below + flip, (index + 2) % group


def meta_kernel(
    group, places, last, members_hbm, valid_hbm, cluster_hbm, out_ref, codes_ref,
    members_ref, valid_ref, cluster_ref, packed_ref, sems,
):
    blocks = valid_ref.shape[1]
    block_len = members_ref.shape[1]
    pool = lax.axis_index("pool")
    first_block = pl.multiple_of(pool * 2 * group, 2 * group)
    copies = []
    for n, (source, target) in enumerate(
        (
            (members_hbm.at[pl.ds(first_block, 2 * group), :], members_ref),
            (valid_hbm, valid_ref),
            (cluster_hbm, cluster_ref),
        )
    ):
        copies.append(pltpu.make_async_copy(source, target, sems.at[n]))
        copies[-1].start()
    sources = blocks // 2
    slots = 2 * block_len
    width = group * places
    before = jnp.where(iota((slots, slots), 0) < iota((slots, slots), 1), 1.0, 0.0).astype(BF16)
    slot = iota((1, slots), 1)
    kind = iota((2 * width, slots), 0)
    kind_place = kind % width // group
    kind_owner = kind % group
    kind_value = jnp.where(kind < width, slot // 32, slot % 32 + 1)
    found = jnp.zeros((sources, 2 * width), F32)
    block_lane = iota((1, blocks), 1)
    lane = iota((1, width), 1)
    first_cluster = jnp.zeros((1, width), I32)
    second_cluster = jnp.zeros((1, width), I32)
    for copy in copies:
        copy.wait()
    for owner in range(group):
        halves, lives = [], []
        for half in range(2):
            halves.append(members_ref[2 * owner + half : 2 * owner + half + 1, :])
            at = block_lane == first_block + 2 * owner + half
            lives.append(jnp.sum(jnp.where(at, valid_ref[...], 0), axis=1, keepdims=True))
            cluster = jnp.sum(jnp.where(at, cluster_ref[...], 0), axis=1, keepdims=True)
            if half == 0:
                first_cluster = jnp.where(lane % group == owner, cluster, first_cluster)
            else:
                second_cluster = jnp.where(lane % group == owner, cluster, second_cluster)
        rows = jnp.concatenate(halves, axis=1)
        end = jnp.where(slot < block_len, lives[0], block_len + lives[1])
        origin = jnp.where(slot < end, rows // slots, -1)
        match = iota((sources, slots), 0) == origin
        ones = jnp.where(match, 1.0, 0.0).astype(BF16)
        ranks = jnp.dot(ones, before, preferred_element_type=F32)
        rank = jnp.sum(jnp.where(match, ranks, 0.0), axis=0, keepdims=True).astype(I32)
        weight = jnp.where((kind_owner == owner) & (kind_place == rank), kind_value, 0)
        found = found + lax.dot_general(
            ones, weight.astype(F32).astype(BF16), NT, preferred_element_type=F32
        )
    found = found.astype(I32)
    place = found[:, :width] * 32 + found[:, width:] - 1
    filled = found[:, width:] > 0
    position = jnp.where(filled, place + lane % group * slots, -1)
    cluster = jnp.where(filled, jnp.where(place < block_len, first_cluster, second_cluster), -1)
    main = (places - last) * group
    rest = last * group
    pools = sources // group
    for n, values in enumerate((position, cluster)):
        for p in range(pools):
            own = values[p * group : (p + 1) * group, :]
            out_ref[n, :, p * main : (p + 1) * main] = own[:, :main]
            at = pools * main + p * rest
            out_ref[n, :, at : at + rest] = own[:, main:]
    packed_ref[...] = jnp.zeros(packed_ref.shape, I32)
    for n, cls in enumerate(relatives()[:4]):
        pos = out_ref[0, pl.ds(cls, 1), :]
        cluster = out_ref[1, pl.ds(cls, 1), :]
        packed_ref[n : n + 1, :] = jnp.where(cluster < 0, -2 * CODE, cluster * CODE + pos)
    codes_ref[...] = jnp.transpose(packed_ref[...])


def run(pieces, sims_ref):
    for n in range(len(pieces) + 1):
        if n < len(pieces):
            piece = pieces[n]
            sims_ref[n % 2, : piece["count"], :] = lax.dot_general(
                piece["left"](), piece["right"](), NT, preferred_element_type=F32
            )
        if n > 0:
            take_maxima(sims_ref.at[(n - 1) % 2], **pieces[n - 1])


def take_maxima(sims_ref, left, right, count, codes, cls, rows, start, pos_row, cluster_row, col, col_start, same):
    step = 128
    right_pos, right_cluster = pos_row(), cluster_row()
    parts = QUARTER // 128
    best_col = [jnp.zeros((8, 128), F32) for _ in range(parts)]
    for top in range(0, count, step):
        code = codes[start + top : start + top + step, cls : cls + 1]
        code = jnp.broadcast_to(code, (step, 128))
        pos = code & (CODE - 1)
        cluster = code >> 13
        best = rows[start + top : start + top + step, :]
        for part in range(parts):
            lanes = slice(part * 128, part * 128 + 128)
            sims = sims_ref[top : top + step, lanes]
            sims = jnp.where(cluster == right_cluster[:, lanes], sims, 0.0)
            earlier = right_pos[:, lanes] < pos
            best = jnp.maximum(best, jnp.where(earlier, sims, 0.0))
            if top < same:
                later = jnp.where(earlier, 0.0, sims)
                best_col[part] = jnp.maximum(
                    best_col[part], jnp.max(later.reshape(-1, 8, 128), axis=0)
                )
        rows[start + top : start + top + step, :] = best
    if same > 0:
        for part in range(parts):
            lanes = slice(col_start + part * 128, col_start + part * 128 + 128)
            col[:, lanes] = jnp.maximum(col[:, lanes], best_col[part])


def row_result(row_ref):
    return jnp.max(jnp.transpose(row_ref[...]), axis=0, keepdims=True)


def col_result(col_ref):
    return jnp.max(col_ref[...], axis=0, keepdims=True)


OWN, SIB, LOW, LOWS, HIGH = range(5)


class Tiles:
    def __init__(self, parts, meta, codes, rows, cols, row_classes, col_classes):
        self.meta, self.codes, self.rows, self.cols = meta, codes, rows, cols
        self.row_classes, self.col_classes = row_classes, col_classes
        self.relatives = relatives()
        self.parts = {}
        for cls, ref, at, quarter, count in parts:
            for q in range(quarter, quarter + count):
                self.parts[cls, q] = (ref, at if len(ref.shape) == 3 else (q - quarter) * QUARTER)
        for cls in row_classes:
            rows[cls, :, :] = jnp.zeros(rows.shape[1:], F32)
        for cls in col_classes:
            cols[cls, :, :] = jnp.zeros(cols.shape[1:], F32)

    def load(self, cls, quarter, count=1):
        ref, at = self.parts[cls, quarter]
        if len(ref.shape) == 3:
            return ref[:, at : at + QUARTER // ref.shape[0], :].reshape(QUARTER, -1)
        return ref[at : at + count * QUARTER, :]

    def piece(self, left, quarter, count, right, right_quarter, same=None):
        lanes = slice(right_quarter * QUARTER, (right_quarter + 1) * QUARTER)
        place = self.relatives[right]
        return dict(
            left=lambda: self.load(left, quarter, count),
            right=lambda: self.load(right, right_quarter),
            count=count * QUARTER,
            codes=self.codes,
            cls=left,
            rows=self.rows.at[left],
            start=quarter * QUARTER,
            pos_row=lambda: self.meta[0, pl.ds(place, 1), lanes],
            cluster_row=lambda: self.meta[1, pl.ds(place, 1), lanes],
            col=self.cols.at[right],
            col_start=right_quarter * QUARTER,
            same=count * QUARTER if same is None else same,
        )

    def matched(self, flip, left, right, pairs):
        pieces = []
        for b in range(4):
            mine = [a for a in range(4) if (a, b) in pairs and (a // 2 + b // 2) % 2 == flip]
            if mine == [0, 1] and self.parts[left, 0][0] is self.parts[left, 1][0]:
                pieces.append(self.piece(left, 0, 2, right, b))
            else:
                pieces += [self.piece(left, a, 1, right, b) for a in mine]
        return pieces

    def result(self, cls):
        best = []
        if cls in self.row_classes:
            best.append(row_result(self.rows.at[cls]))
        if cls in self.col_classes:
            best.append(col_result(self.cols.at[cls]))
        return functools.reduce(jnp.maximum, best)


def either(flag, work):
    pl.when(flag)(lambda: work(1))
    pl.when(jnp.logical_not(flag))(lambda: work(0))


def second_core():
    return lax.axis_index("grp") % 2 == 1


def outer_chip():
    chip = lax.axis_index("grp") // 2
    return (chip == 0) | (chip == 3)


ALL_PAIRS = [(a, b) for a in range(4) for b in range(4)]


def follow_kernel(rows, after, also_after, out):
    del rows, after, also_after, out


def join_kernel(pools, rest, low_rest, high_rest, after, out):
    del after
    width = QUARTER // pools
    for n, part in enumerate((rest, low_rest, high_rest)):
        out[:, n * width : (n + 1) * width, :] = part[...].reshape(pools, width, -1)


def near_kernel(own0, sib0, meta, codes, out, sims, rows, cols):
    moves = [(OWN, own0, None, 0, 3), (SIB, sib0, None, 0, 3)]
    tiles = Tiles(
        moves, meta, codes, rows, cols, (OWN,), (OWN, SIB))
    run([tiles.piece(OWN, 0, b + 1, OWN, b, same=b * QUARTER) for b in range(3)], sims)
    pairs = [(a, b) for a, b in ALL_PAIRS if 3 not in (a, b)]
    either(second_core(), lambda flip: run(tiles.matched(flip, OWN, SIB, pairs), sims))
    out[...] = jnp.zeros(out.shape, F32)
    for cls in (OWN, SIB):
        out[cls : cls + 1, :] = tiles.result(cls)


def middle_kernel(
    own0, arrived, sib0, meta, codes, near, out, own_out, arrived_out, sib_out, codes_out,
    sims, rows, cols
):
    width = arrived.shape[1] // 3
    moves = [
        (OWN, own0, None, 0, 3), (OWN, arrived, 0, 3, 1), (HIGH, arrived, 2 * width, 3, 1),
        (SIB, sib0, None, 0, 3),
    ]
    tiles = Tiles(moves, meta, codes, rows, cols, (OWN, SIB), (OWN, HIGH))
    pieces = [tiles.piece(OWN, 0, 3, OWN, 3), tiles.piece(OWN, 3, 1, OWN, 3, same=0)]
    pieces += [tiles.piece(OWN, 0, 3, HIGH, 3), tiles.piece(OWN, 3, 1, HIGH, 3)]
    pieces += [tiles.piece(SIB, 0, 3, HIGH, 3)]
    run(pieces, sims)
    own_out[...] = own0[...]
    arrived_out[...] = arrived[...]
    sib_out[...] = sib0[...]
    codes_out[...] = codes[...]
    out[...] = near[...]
    for cls in (OWN, SIB, HIGH):
        out[cls : cls + 1, :] = jnp.maximum(near[cls : cls + 1, :], tiles.result(cls))


def main_kernel(
    own0, arrived, high0, sib0, swapped, low0, meta, codes, before, out, sims, rows, cols
):
    width = arrived.shape[1] // 3
    moves = [
        (HIGH, high0, None, 0, 3), (OWN, own0, None, 0, 3), (OWN, arrived, 0, 3, 1),
        (SIB, sib0, None, 0, 3), (SIB, swapped, 0, 3, 1), (HIGH, arrived, 2 * width, 3, 1),
        (LOW, low0, None, 0, 3), (LOW, arrived, width, 3, 1),
    ]
    tiles = Tiles(moves, meta, codes, rows, cols, (OWN, SIB, LOW), (SIB, HIGH))
    pieces = []
    for b in range(3):
        for cls in (OWN, SIB):
            pieces += [tiles.piece(cls, 0, 3, HIGH, b), tiles.piece(cls, 3, 1, HIGH, b)]
    pieces += [tiles.piece(SIB, 3, 1, HIGH, 3)]
    run(pieces, sims)
    pairs = [(a, b) for a, b in ALL_PAIRS if 3 in (a, b)]
    either(second_core(), lambda flip: run(tiles.matched(flip, OWN, SIB, pairs), sims))
    either(outer_chip(), lambda flip: run(tiles.matched(flip, LOW, HIGH, ALL_PAIRS), sims))
    for cls in (OWN, SIB, LOW, HIGH):
        out[cls : cls + 1, :] = jnp.maximum(before[cls : cls + 1, :], tiles.result(cls))


def last_kernel(
    pools, group, main, rest, lows0, high0, swapped, arrived, meta, codes, before, out,
    sims, rows, cols, every, upper, sem,
):
    width = swapped.shape[1] // 3
    copy = pltpu.make_async_copy(arrived.at[:, pl.ds(2 * width, width), :], upper, sem)
    copy.start()
    moves = [
        (LOWS, lows0, None, 0, 3), (LOWS, swapped, width, 3, 1), (HIGH, high0, None, 0, 3),
        (HIGH, upper, 0, 3, 1),
    ]
    tiles = Tiles(
        moves, meta, codes, rows, cols, (LOWS,), (HIGH,))
    copy.wait()
    either(outer_chip(), lambda flip: run(tiles.matched(flip, LOWS, HIGH, ALL_PAIRS), sims))
    every[...] = jnp.zeros(every.shape, F32)
    for cls, place in enumerate(tiles.relatives):
        best = [] if cls == LOWS else [before[cls : cls + 1, :]]
        if cls in (LOWS, HIGH):
            best.append(tiles.result(cls))
        every[pl.ds(place, 1), :] = functools.reduce(jnp.maximum, best)
    for p in range(pools):
        rows_out = slice(p * group, (p + 1) * group)
        out[rows_out, :main] = every[:, p * main : (p + 1) * main]
        at = pools * main + p * rest
        out[rows_out, main:] = every[:, at : at + rest]


def score_kernel(pools, group, places, table_ref, returned_ref, out_ref):
    rows_dev = out_ref.shape[1]
    arrived = jnp.transpose(
        jnp.concatenate([returned_ref[...], jnp.zeros_like(returned_ref)], axis=1)
    )
    table = table_ref[...]
    row = iota((8, rows_dev), 1)
    total = jnp.zeros((8, rows_dev), F32)
    for p in range(pools):
        for k in range(places):
            value = jnp.max(
                arrived[k * group : (k + 1) * group, p * group : (p + 1) * group],
                axis=1,
                keepdims=True,
            )
            entry = table[p * group : (p + 1) * group, k : k + 1]
            total = jnp.where(entry == row, value, total)
    out_ref[...] = jnp.sum(total, axis=0, keepdims=True)


def body(embeddings, members, valid, block_cluster):
    rows_dev, feature = embeddings.shape
    pools = lax.axis_size("pool")
    group = lax.axis_size("grp")
    devices = pools * group
    places = rows_dev // devices
    last = places // 4
    sds = jax.ShapeDtypeStruct
    hbm = pl.BlockSpec(memory_space=pltpu.HBM)
    valid_row = valid.reshape(1, -1)
    cluster_row = block_cluster.reshape(1, -1)
    blocks, block_len = members.shape

    some = jnp.any(valid > 0)
    table, main = pl.pallas_call(
        lambda *refs: table_kernel(pools, group, places, last, *refs),
        out_shape=(
            sds((devices, 128), I32),
            sds((pools, 3 * QUARTER // pools, feature), BF16),
        ),
        in_specs=[hbm] * 3,
        scratch_shapes=[
            pltpu.VMEM((blocks, block_len), I32),
            pltpu.VMEM((1, blocks), I32),
            pltpu.VMEM((rows_dev, feature), BF16),
            pltpu.VMEM((blocks, 128), F32),
            pltpu.SemaphoreType.DMA((3,)),
        ],
        compiler_params=TABLE_PARAMS,
        cost_estimate=cost(rows_dev * rows_dev * feature),
        name="table",
    )(members, valid_row, embeddings)
    meta, codes = pl.pallas_call(
        lambda *refs: meta_kernel(group, places, last, *refs),
        out_shape=(sds((2, group, rows_dev), I32), sds((rows_dev, 128), I32)),
        in_specs=[hbm] * 3,
        scratch_shapes=[
            pltpu.VMEM((2 * group, block_len), I32),
            pltpu.VMEM((1, blocks), I32),
            pltpu.VMEM((1, blocks), I32),
            pltpu.VMEM((128, rows_dev), I32),
            pltpu.SemaphoreType.DMA((3,)),
        ],
        compiler_params=PARAMS,
        cost_estimate=cost(2 * rows_dev**3),
        name="meta",
    )(members, valid_row, cluster_row)

    def shift(rows, by):
        return lax.ppermute(rows, "grp", [(g, (g + by) % group) for g in range(group)])

    def swap(rows):
        return lax.ppermute(rows, "grp", [(g, g ^ 1) for g in range(group)])

    def follow(rows, after, also_after):
        return pl.pallas_call(
            follow_kernel,
            out_shape=sds(rows.shape, BF16),
            in_specs=[hbm] * 3,
            out_specs=hbm,
            input_output_aliases={0: 0},
            compiler_params=PARAMS,
            name="follow",
        )(rows, after, also_after)

    def to_pools(rows):
        return lax.all_to_all(rows, "pool", split_axis=0, concat_axis=0, tiled=True)

    vmem = pl.BlockSpec(memory_space=pltpu.VMEM)
    rest = pl.pallas_call(
        lambda *refs: rest_kernel(pools, places, last, *refs),
        out_shape=sds((QUARTER, feature), BF16),
        compiler_params=PARAMS,
        name="rest",
    )(table, embeddings)
    low_rest, high_rest = shift(rest, 2), shift(rest, -2)
    own0 = to_pools(main).reshape(-1, feature)
    sent = pl.pallas_call(
        lambda *refs: join_kernel(pools, *refs),
        out_shape=sds((pools, 3 * QUARTER // pools, feature), BF16),
        in_specs=[vmem] * 3 + [hbm],
        compiler_params=PARAMS,
        name="join",
    )(rest, low_rest, high_rest, meta)
    own0 = follow(own0, sent, some.astype(I32).reshape(1, 1))
    low0, high0 = shift(own0, 2), shift(own0, -2)
    sib0 = swap(own0)

    def tiles(kernel, name, squares, operands, small, out_shape=(8, rows_dev), more=(), specs=None, kept=()):
        return pl.pallas_call(
            kernel,
            out_shape=(sds(out_shape, F32), *kept) if kept else sds(out_shape, F32),
            in_specs=specs or [vmem] * (len(operands) + len(small)),
            scratch_shapes=[
                pltpu.VMEM((2, 3 * QUARTER, QUARTER), F32),
                pltpu.VMEM((4, rows_dev, 128), F32),
                pltpu.VMEM((5, 8, rows_dev), F32),
                *more,
            ],
            compiler_params=PARAMS,
            cost_estimate=cost(squares * QUARTER * QUARTER * feature),
            name=name,
        )(*operands, *small)

    def bring(sent, own0, sib0, meta, codes):
        near = tiles(near_kernel, "near", 11, (own0, sib0), (meta, codes))
        return to_pools(sent), near

    def bring_nothing(sent, own0, sib0, meta, codes):
        return jnp.zeros_like(sent), jnp.zeros((8, rows_dev), F32)

    arrived, near = lax.cond(
        some, bring, bring_nothing, sent, own0, sib0, meta, codes
    )
    swapped = swap(arrived)
    middle, own0, arrived, sib0, codes = tiles(
        middle_kernel, "middle", 11, (own0, arrived, sib0), (meta, codes, near),
        kept=[sds(kept.shape, kept.dtype) for kept in (own0, arrived, sib0, codes)],
    )
    low0 = follow(low0, middle, high0)
    best = tiles(
        main_kernel, "main", 37, (own0, arrived, high0, sib0, swapped, low0), (meta, codes, middle)
    )
    best = tiles(
        lambda *refs: last_kernel(pools, group, group * (places - last), group * last, *refs),
        "last", 8, (swap(low0), high0, swapped, arrived), (meta, codes, best),
        out_shape=(devices, group * places),
        more=(
            pltpu.VMEM((group, rows_dev), F32),
            pltpu.VMEM((pools, QUARTER // pools, feature), BF16),
            pltpu.SemaphoreType.DMA,
        ),
        specs=[vmem] * 3 + [hbm] + [vmem] * 3,
    )
    returned = lax.all_to_all(best, ("pool", "grp"), split_axis=0, concat_axis=0, tiled=True)
    scores = pl.pallas_call(
        lambda *refs: score_kernel(pools, group, places, *refs),
        out_shape=sds((1, rows_dev), F32),
        compiler_params=PARAMS,
        name="score",
    )(table, returned)
    return scores.reshape(rows_dev)


def cost(products):
    return pl.CostEstimate(flops=2 * products, bytes_accessed=0, transcendentals=0)


def solution(mesh):
    in_specs = (P(("pool", "grp"), None), P(), P(), P())
    out_specs = P(("pool", "grp"))
    return jax.shard_map(body, mesh=mesh, in_specs=in_specs, out_specs=out_specs, check_vma=False)
```

```python
import functools

import jax
import jax.numpy as jnp
from jax import lax
from jax.experimental import pallas as pl
from jax.experimental.pallas import tpu as pltpu
from jax.sharding import PartitionSpec as P

EPS = 1e-06
F32 = jnp.float32
BF16 = jnp.bfloat16
I32 = jnp.int32
QUARTER = 256
CODE = 8192
NT = (((1,), (1,)), ((), ()))
PARAMS = pltpu.CompilerParams(vmem_limit_bytes=12 * 1024 * 1024)
TABLE_PARAMS = pltpu.CompilerParams(vmem_limit_bytes=62 * 1024 * 1024)


def iota(shape, dim):
    return lax.broadcasted_iota(I32, shape, dim)


def normal_rows(rows):
    return (rows * lax.rsqrt(jnp.sum(rows * rows, axis=1, keepdims=True) + EPS)).astype(BF16)


def picked_rows(table, emb, first, count, pools):
    width = emb.shape[0]
    wanted = []
    for k in range(first, first + count):
        hit = table[:, k : k + 1] == iota((table.shape[0], width), 1)
        wanted.append(jnp.where(hit, 1.0, 0.0).reshape(pools, -1, width))
    choice = jnp.concatenate(wanted, axis=1).reshape(-1, width).astype(BF16)
    return normal_rows(jnp.dot(choice, emb, preferred_element_type=F32))


def table_kernel(
    pools, group, places, last, members_hbm, valid_hbm, emb_hbm, table_ref, main_ref,
    members_ref, valid_ref, emb_ref, found_ref, sems,
):
    copies = []
    for n, (source, target) in enumerate(
        ((members_hbm, members_ref), (valid_hbm, valid_ref), (emb_hbm, emb_ref))
    ):
        copies.append(pltpu.make_async_copy(source, target, sems.at[n]))
        copies[-1].start()
    rows_dev = emb_ref.shape[0]
    device = lax.axis_index("pool") * group + lax.axis_index("grp")
    blocks, block_len = members_ref.shape
    devices = blocks // 2
    before = jnp.where(
        iota((block_len, block_len), 0) < iota((block_len, block_len), 1), 1.0, 0.0
    ).astype(BF16)
    at = iota((blocks, blocks), 1) == iota((blocks, blocks), 0)
    copies[0].wait()
    copies[1].wait()
    live = jnp.sum(jnp.where(at, valid_ref[...], 0), axis=1, keepdims=True)
    local = members_ref[...] - device * rows_dev
    mine = (local >= 0) & (local < rows_dev) & (iota((blocks, block_len), 1) < live)
    ones = jnp.where(mine, 1.0, 0.0)
    counts = jnp.broadcast_to(jnp.sum(ones, axis=1, keepdims=True), (blocks, 128))
    counts = jnp.where(iota((blocks, 128), 0) % 2 == 1, pltpu.roll(counts, 1, 0), 0.0)
    rank = jnp.dot(ones.astype(BF16), before, preferred_element_type=F32) + counts[:, :1]
    rank = jnp.where(mine, rank, -1.0)
    value = (local + 1).astype(F32)
    lane = iota((blocks, 128), 1)
    found = jnp.zeros((blocks, 128), F32)
    for k in range(places):
        entry = jnp.sum(jnp.where(rank == k, value, 0.0), axis=1, keepdims=True)
        found = jnp.where(lane == k, entry, found)
    found_ref[...] = found
    pair = found_ref[pl.ds(0, devices, stride=2), :] + found_ref[pl.ds(1, devices, stride=2), :]
    table = pair.astype(I32) - 1
    table_ref[...] = table
    copies[2].wait()
    for first in range(0, places - last, last):
        part = picked_rows(table, emb_ref[...], first, last, pools)
        part = part.reshape(pools, last * group, -1)
        main_ref[:, first * group : (first + last) * group, :] = part


def rest_kernel(pools, places, last, table_ref, emb_ref, out):
    out[...] = picked_rows(table_ref[...], emb_ref[...], places - last, last, pools)


def relatives():
    group = lax.axis_size("grp")
    index = lax.axis_index("grp")
    flip = 1 - 2 * (index % 2)
    below = (index + group - 2) % group
    return index, index + flip, below, below + flip, (index + 2) % group


def meta_kernel(
    group, places, last, members_hbm, valid_hbm, cluster_hbm, out_ref, codes_ref,
    members_ref, valid_ref, cluster_ref, packed_ref, sems,
):
    blocks = valid_ref.shape[1]
    block_len = members_ref.shape[1]
    pool = lax.axis_index("pool")
    first_block = pl.multiple_of(pool * 2 * group, 2 * group)
    copies = []
    for n, (source, target) in enumerate(
        (
            (members_hbm.at[pl.ds(first_block, 2 * group), :], members_ref),
            (valid_hbm, valid_ref),
            (cluster_hbm, cluster_ref),
        )
    ):
        copies.append(pltpu.make_async_copy(source, target, sems.at[n]))
        copies[-1].start()
    sources = blocks // 2
    slots = 2 * block_len
    width = group * places
    before = jnp.where(iota((slots, slots), 0) < iota((slots, slots), 1), 1.0, 0.0).astype(BF16)
    slot = iota((1, slots), 1)
    kind = iota((2 * width, slots), 0)
    kind_place = kind % width // group
    kind_owner = kind % group
    kind_value = jnp.where(kind < width, slot // 32, slot % 32 + 1)
    found = jnp.zeros((sources, 2 * width), F32)
    block_lane = iota((1, blocks), 1)
    lane = iota((1, width), 1)
    first_cluster = jnp.zeros((1, width), I32)
    second_cluster = jnp.zeros((1, width), I32)
    for copy in copies:
        copy.wait()
    for owner in range(group):
        halves, lives = [], []
        for half in range(2):
            halves.append(members_ref[2 * owner + half : 2 * owner + half + 1, :])
            at = block_lane == first_block + 2 * owner + half
            lives.append(jnp.sum(jnp.where(at, valid_ref[...], 0), axis=1, keepdims=True))
            cluster = jnp.sum(jnp.where(at, cluster_ref[...], 0), axis=1, keepdims=True)
            if half == 0:
                first_cluster = jnp.where(lane % group == owner, cluster, first_cluster)
            else:
                second_cluster = jnp.where(lane % group == owner, cluster, second_cluster)
        rows = jnp.concatenate(halves, axis=1)
        end = jnp.where(slot < block_len, lives[0], block_len + lives[1])
        origin = jnp.where(slot < end, rows // slots, -1)
        match = iota((sources, slots), 0) == origin
        ones = jnp.where(match, 1.0, 0.0).astype(BF16)
        ranks = jnp.dot(ones, before, preferred_element_type=F32)
        rank = jnp.sum(jnp.where(match, ranks, 0.0), axis=0, keepdims=True).astype(I32)
        weight = jnp.where((kind_owner == owner) & (kind_place == rank), kind_value, 0)
        found = found + lax.dot_general(
            ones, weight.astype(F32).astype(BF16), NT, preferred_element_type=F32
        )
    found = found.astype(I32)
    place = found[:, :width] * 32 + found[:, width:] - 1
    filled = found[:, width:] > 0
    position = jnp.where(filled, place + lane % group * slots, -1)
    cluster = jnp.where(filled, jnp.where(place < block_len, first_cluster, second_cluster), -1)
    main = (places - last) * group
    rest = last * group
    pools = sources // group
    for n, values in enumerate((position, cluster)):
        for p in range(pools):
            own = values[p * group : (p + 1) * group, :]
            out_ref[n, :, p * main : (p + 1) * main] = own[:, :main]
            at = pools * main + p * rest
            out_ref[n, :, at : at + rest] = own[:, main:]
    packed_ref[...] = jnp.zeros(packed_ref.shape, I32)
    for n, cls in enumerate(relatives()[:4]):
        pos = out_ref[0, pl.ds(cls, 1), :]
        cluster = out_ref[1, pl.ds(cls, 1), :]
        packed_ref[n : n + 1, :] = jnp.where(cluster < 0, -2 * CODE, cluster * CODE + pos)
    codes_ref[...] = jnp.transpose(packed_ref[...])


def run(pieces, sims_ref):
    for n in range(len(pieces) + 1):
        if n < len(pieces):
            piece = pieces[n]
            sims_ref[n % 2, : piece["count"], :] = lax.dot_general(
                piece["left"](), piece["right"](), NT, preferred_element_type=F32
            )
        if n > 0:
            take_maxima(sims_ref.at[(n - 1) % 2], **pieces[n - 1])


def take_maxima(sims_ref, left, right, count, codes, cls, rows, start, pos_row, cluster_row, col, col_start, same):
    step = 128
    right_pos, right_cluster = pos_row(), cluster_row()
    parts = QUARTER // 128
    best_col = [jnp.zeros((8, 128), F32) for _ in range(parts)]
    for top in range(0, count, step):
        code = codes[start + top : start + top + step, cls : cls + 1]
        code = jnp.broadcast_to(code, (step, 128))
        pos = code & (CODE - 1)
        cluster = code >> 13
        best = rows[start + top : start + top + step, :]
        for part in range(parts):
            lanes = slice(part * 128, part * 128 + 128)
            sims = sims_ref[top : top + step, lanes]
            sims = jnp.where(cluster == right_cluster[:, lanes], sims, 0.0)
            earlier = right_pos[:, lanes] < pos
            best = jnp.maximum(best, jnp.where(earlier, sims, 0.0))
            if top < same:
                later = jnp.where(earlier, 0.0, sims)
                best_col[part] = jnp.maximum(
                    best_col[part], jnp.max(later.reshape(-1, 8, 128), axis=0)
                )
        rows[start + top : start + top + step, :] = best
    if same > 0:
        for part in range(parts):
            lanes = slice(col_start + part * 128, col_start + part * 128 + 128)
            col[:, lanes] = jnp.maximum(col[:, lanes], best_col[part])


def row_result(row_ref):
    return jnp.max(jnp.transpose(row_ref[...]), axis=0, keepdims=True)


def col_result(col_ref):
    return jnp.max(col_ref[...], axis=0, keepdims=True)


OWN, SIB, LOW, LOWS, HIGH = range(5)


class Tiles:
    def __init__(self, parts, meta, codes, rows, cols, row_classes, col_classes):
        self.meta, self.codes, self.rows, self.cols = meta, codes, rows, cols
        self.row_classes, self.col_classes = row_classes, col_classes
        self.relatives = relatives()
        self.parts = {}
        for cls, ref, at, quarter, count in parts:
            for q in range(quarter, quarter + count):
                self.parts[cls, q] = (ref, at if len(ref.shape) == 3 else (q - quarter) * QUARTER)
        for cls in row_classes:
            rows[cls, :, :] = jnp.zeros(rows.shape[1:], F32)
        for cls in col_classes:
            cols[cls, :, :] = jnp.zeros(cols.shape[1:], F32)

    def load(self, cls, quarter, count=1):
        ref, at = self.parts[cls, quarter]
        if len(ref.shape) == 3:
            return ref[:, at : at + QUARTER // ref.shape[0], :].reshape(QUARTER, -1)
        return ref[at : at + count * QUARTER, :]

    def piece(self, left, quarter, count, right, right_quarter, same=None):
        lanes = slice(right_quarter * QUARTER, (right_quarter + 1) * QUARTER)
        place = self.relatives[right]
        return dict(
            left=lambda: self.load(left, quarter, count),
            right=lambda: self.load(right, right_quarter),
            count=count * QUARTER,
            codes=self.codes,
            cls=left,
            rows=self.rows.at[left],
            start=quarter * QUARTER,
            pos_row=lambda: self.meta[0, pl.ds(place, 1), lanes],
            cluster_row=lambda: self.meta[1, pl.ds(place, 1), lanes],
            col=self.cols.at[right],
            col_start=right_quarter * QUARTER,
            same=count * QUARTER if same is None else same,
        )

    def matched(self, flip, left, right, pairs):
        pieces = []
        for b in range(4):
            mine = [a for a in range(4) if (a, b) in pairs and (a // 2 + b // 2) % 2 == flip]
            if mine == [0, 1] and self.parts[left, 0][0] is self.parts[left, 1][0]:
                pieces.append(self.piece(left, 0, 2, right, b))
            else:
                pieces += [self.piece(left, a, 1, right, b) for a in mine]
        return pieces

    def result(self, cls):
        best = []
        if cls in self.row_classes:
            best.append(row_result(self.rows.at[cls]))
        if cls in self.col_classes:
            best.append(col_result(self.cols.at[cls]))
        return functools.reduce(jnp.maximum, best)


def either(flag, work):
    pl.when(flag)(lambda: work(1))
    pl.when(jnp.logical_not(flag))(lambda: work(0))


def second_core():
    return lax.axis_index("grp") % 2 == 1


def outer_chip():
    chip = lax.axis_index("grp") // 2
    return (chip == 0) | (chip == 3)


ALL_PAIRS = [(a, b) for a in range(4) for b in range(4)]


def follow_kernel(rows, after, also_after, out):
    del rows, after, also_after, out


def join_kernel(pools, rest, low_rest, high_rest, after, out):
    del after
    width = QUARTER // pools
    for n, part in enumerate((rest, low_rest, high_rest)):
        out[:, n * width : (n + 1) * width, :] = part[...].reshape(pools, width, -1)


def near_kernel(own0, sib0, meta, codes, out, sims, rows, cols):
    moves = [(OWN, own0, None, 0, 3), (SIB, sib0, None, 0, 3)]
    tiles = Tiles(
        moves, meta, codes, rows, cols, (OWN,), (OWN, SIB))
    run([tiles.piece(OWN, 0, b + 1, OWN, b, same=b * QUARTER) for b in range(3)], sims)
    pairs = [(a, b) for a, b in ALL_PAIRS if 3 not in (a, b)]
    either(second_core(), lambda flip: run(tiles.matched(flip, OWN, SIB, pairs), sims))
    out[...] = jnp.zeros(out.shape, F32)
    for cls in (OWN, SIB):
        out[cls : cls + 1, :] = tiles.result(cls)


def middle_kernel(
    own0, arrived, sib0, meta, codes, near, out, own_out, arrived_out, sib_out, codes_out,
    sims, rows, cols
):
    width = arrived.shape[1] // 3
    moves = [
        (OWN, own0, None, 0, 3), (OWN, arrived, 0, 3, 1), (HIGH, arrived, 2 * width, 3, 1),
        (SIB, sib0, None, 0, 3),
    ]
    tiles = Tiles(moves, meta, codes, rows, cols, (OWN, SIB), (OWN, HIGH))
    pieces = [tiles.piece(OWN, 0, 3, OWN, 3), tiles.piece(OWN, 3, 1, OWN, 3, same=0)]
    pieces += [tiles.piece(OWN, 0, 3, HIGH, 3), tiles.piece(OWN, 3, 1, HIGH, 3)]
    pieces += [tiles.piece(SIB, 0, 3, HIGH, 3)]
    run(pieces, sims)
    own_out[...] = own0[...]
    arrived_out[...] = arrived[...]
    sib_out[...] = sib0[...]
    codes_out[...] = codes[...]
    out[...] = near[...]
    for cls in (OWN, SIB, HIGH):
        out[cls : cls + 1, :] = jnp.maximum(near[cls : cls + 1, :], tiles.result(cls))


def main_kernel(
    own0, arrived, high0, sib0, swapped, low0, meta, codes, before, out, sims, rows, cols
):
    width = arrived.shape[1] // 3
    moves = [
        (HIGH, high0, None, 0, 3), (OWN, own0, None, 0, 3), (OWN, arrived, 0, 3, 1),
        (SIB, sib0, None, 0, 3), (SIB, swapped, 0, 3, 1), (HIGH, arrived, 2 * width, 3, 1),
        (LOW, low0, None, 0, 3), (LOW, arrived, width, 3, 1),
    ]
    tiles = Tiles(moves, meta, codes, rows, cols, (OWN, SIB, LOW), (SIB, HIGH))
    pieces = []
    for b in range(3):
        for cls in (OWN, SIB):
            pieces += [tiles.piece(cls, 0, 3, HIGH, b), tiles.piece(cls, 3, 1, HIGH, b)]
    pieces += [tiles.piece(SIB, 3, 1, HIGH, 3)]
    run(pieces, sims)
    pairs = [(a, b) for a, b in ALL_PAIRS if 3 in (a, b)]
    either(second_core(), lambda flip: run(tiles.matched(flip, OWN, SIB, pairs), sims))
    either(outer_chip(), lambda flip: run(tiles.matched(flip, LOW, HIGH, ALL_PAIRS), sims))
    for cls in (OWN, SIB, LOW, HIGH):
        out[cls : cls + 1, :] = jnp.maximum(before[cls : cls + 1, :], tiles.result(cls))


def last_kernel(
    pools, group, main, rest, lows0, high0, swapped, arrived, meta, codes, before, out,
    sims, rows, cols, every, upper, sem,
):
    width = swapped.shape[1] // 3
    copy = pltpu.make_async_copy(arrived.at[:, pl.ds(2 * width, width), :], upper, sem)
    copy.start()
    moves = [
        (LOWS, lows0, None, 0, 3), (LOWS, swapped, width, 3, 1), (HIGH, high0, None, 0, 3),
        (HIGH, upper, 0, 3, 1),
    ]
    tiles = Tiles(
        moves, meta, codes, rows, cols, (LOWS,), (HIGH,))
    copy.wait()
    either(outer_chip(), lambda flip: run(tiles.matched(flip, LOWS, HIGH, ALL_PAIRS), sims))
    every[...] = jnp.zeros(every.shape, F32)
    for cls, place in enumerate(tiles.relatives):
        best = [] if cls == LOWS else [before[cls : cls + 1, :]]
        if cls in (LOWS, HIGH):
            best.append(tiles.result(cls))
        every[pl.ds(place, 1), :] = functools.reduce(jnp.maximum, best)
    for p in range(pools):
        rows_out = slice(p * group, (p + 1) * group)
        out[rows_out, :main] = every[:, p * main : (p + 1) * main]
        at = pools * main + p * rest
        out[rows_out, main:] = every[:, at : at + rest]


def score_kernel(pools, group, places, table_ref, returned_ref, out_ref):
    rows_dev = out_ref.shape[1]
    arrived = jnp.transpose(
        jnp.concatenate([returned_ref[...], jnp.zeros_like(returned_ref)], axis=1)
    )
    table = table_ref[...]
    row = iota((8, rows_dev), 1)
    total = jnp.zeros((8, rows_dev), F32)
    for p in range(pools):
        for k in range(places):
            value = jnp.max(
                arrived[k * group : (k + 1) * group, p * group : (p + 1) * group],
                axis=1,
                keepdims=True,
            )
            entry = table[p * group : (p + 1) * group, k : k + 1]
            total = jnp.where(entry == row, value, total)
    out_ref[...] = jnp.sum(total, axis=0, keepdims=True)


def body(embeddings, members, valid, block_cluster):
    rows_dev, feature = embeddings.shape
    pools = lax.axis_size("pool")
    group = lax.axis_size("grp")
    devices = pools * group
    places = rows_dev // devices
    last = places // 4
    sds = jax.ShapeDtypeStruct
    hbm = pl.BlockSpec(memory_space=pltpu.HBM)
    valid_row = valid.reshape(1, -1)
    cluster_row = block_cluster.reshape(1, -1)
    blocks, block_len = members.shape

    some = jnp.any(valid > 0)
    table, main = pl.pallas_call(
        lambda *refs: table_kernel(pools, group, places, last, *refs),
        out_shape=(
            sds((devices, 128), I32),
            sds((pools, 3 * QUARTER // pools, feature), BF16),
        ),
        in_specs=[hbm] * 3,
        scratch_shapes=[
            pltpu.VMEM((blocks, block_len), I32),
            pltpu.VMEM((1, blocks), I32),
            pltpu.VMEM((rows_dev, feature), BF16),
            pltpu.VMEM((blocks, 128), F32),
            pltpu.SemaphoreType.DMA((3,)),
        ],
        compiler_params=TABLE_PARAMS,
        cost_estimate=cost(rows_dev * rows_dev * feature),
        name="table",
    )(members, valid_row, embeddings)
    meta, codes = pl.pallas_call(
        lambda *refs: meta_kernel(group, places, last, *refs),
        out_shape=(sds((2, group, rows_dev), I32), sds((rows_dev, 128), I32)),
        in_specs=[hbm] * 3,
        scratch_shapes=[
            pltpu.VMEM((2 * group, block_len), I32),
            pltpu.VMEM((1, blocks), I32),
            pltpu.VMEM((1, blocks), I32),
            pltpu.VMEM((128, rows_dev), I32),
            pltpu.SemaphoreType.DMA((3,)),
        ],
        compiler_params=PARAMS,
        cost_estimate=cost(2 * rows_dev**3),
        name="meta",
    )(members, valid_row, cluster_row)

    def shift(rows, by):
        return lax.ppermute(rows, "grp", [(g, (g + by) % group) for g in range(group)])

    def swap(rows):
        return lax.ppermute(rows, "grp", [(g, g ^ 1) for g in range(group)])

    def follow(rows, after, also_after):
        return pl.pallas_call(
            follow_kernel,
            out_shape=sds(rows.shape, BF16),
            in_specs=[hbm] * 3,
            out_specs=hbm,
            input_output_aliases={0: 0},
            compiler_params=PARAMS,
            name="follow",
        )(rows, after, also_after)

    def to_pools(rows):
        return lax.all_to_all(rows, "pool", split_axis=0, concat_axis=0, tiled=True)

    vmem = pl.BlockSpec(memory_space=pltpu.VMEM)
    rest = pl.pallas_call(
        lambda *refs: rest_kernel(pools, places, last, *refs),
        out_shape=sds((QUARTER, feature), BF16),
        compiler_params=PARAMS,
        name="rest",
    )(table, embeddings)
    low_rest, high_rest = shift(rest, 2), shift(rest, -2)
    own0 = to_pools(main).reshape(-1, feature)
    sent = pl.pallas_call(
        lambda *refs: join_kernel(pools, *refs),
        out_shape=sds((pools, 3 * QUARTER // pools, feature), BF16),
        in_specs=[vmem] * 3 + [hbm],
        compiler_params=TABLE_PARAMS,
        name="join",
    )(rest, low_rest, high_rest, meta)
    own0 = follow(own0, sent, some.astype(I32).reshape(1, 1))
    low0, high0 = shift(own0, 2), shift(own0, -2)
    sib0 = swap(own0)

    def tiles(kernel, name, squares, operands, small, out_shape=(8, rows_dev), more=(), specs=None, kept=()):
        return pl.pallas_call(
            kernel,
            out_shape=(sds(out_shape, F32), *kept) if kept else sds(out_shape, F32),
            in_specs=specs or [vmem] * (len(operands) + len(small)),
            scratch_shapes=[
                pltpu.VMEM((2, 3 * QUARTER, QUARTER), F32),
                pltpu.VMEM((4, rows_dev, 128), F32),
                pltpu.VMEM((5, 8, rows_dev), F32),
                *more,
            ],
            compiler_params=PARAMS,
            cost_estimate=cost(squares * QUARTER * QUARTER * feature),
            name=name,
        )(*operands, *small)

    def bring(sent, own0, sib0, meta, codes):
        near = tiles(near_kernel, "near", 11, (own0, sib0), (meta, codes))
        return to_pools(sent), near

    def bring_nothing(sent, own0, sib0, meta, codes):
        return jnp.zeros_like(sent), jnp.zeros((8, rows_dev), F32)

    arrived, near = lax.cond(
        some, bring, bring_nothing, sent, own0, sib0, meta, codes
    )
    swapped = swap(arrived)
    middle, own0, arrived, sib0, codes = tiles(
        middle_kernel, "middle", 11, (own0, arrived, sib0), (meta, codes, near),
        kept=[sds(kept.shape, kept.dtype) for kept in (own0, arrived, sib0, codes)],
    )
    low0 = follow(low0, middle, high0)
    best = tiles(
        main_kernel, "main", 37, (own0, arrived, high0, sib0, swapped, low0), (meta, codes, middle)
    )
    best = tiles(
        lambda *refs: last_kernel(pools, group, group * (places - last), group * last, *refs),
        "last", 8, (swap(low0), high0, swapped, arrived), (meta, codes, best),
        out_shape=(devices, group * places),
        more=(
            pltpu.VMEM((group, rows_dev), F32),
            pltpu.VMEM((pools, QUARTER // pools, feature), BF16),
            pltpu.SemaphoreType.DMA,
        ),
        specs=[vmem] * 3 + [hbm] + [vmem] * 3,
    )
    returned = lax.all_to_all(best, ("pool", "grp"), split_axis=0, concat_axis=0, tiled=True)
    scores = pl.pallas_call(
        lambda *refs: score_kernel(pools, group, places, *refs),
        out_shape=sds((1, rows_dev), F32),
        compiler_params=PARAMS,
        name="score",
    )(table, returned)
    return scores.reshape(rows_dev)


def cost(products):
    return pl.CostEstimate(flops=2 * products, bytes_accessed=0, transcendentals=0)


def solution(mesh):
    in_specs = (P(("pool", "grp"), None), P(), P(), P())
    out_specs = P(("pool", "grp"))
    return jax.shard_map(body, mesh=mesh, in_specs=in_specs, out_specs=out_specs, check_vma=False)
```
